32 devices in a mesh: section: 2 (over z_hi), dp: 8 (over y, x, core), tensor: 2 (over z_lo).
Axes of the slice: x: 2, y: 2, z: 4 (z_hi: 2, z_lo: 2; z = z_hi * 2 + z_lo), core: 2. Of those that a mesh axis runs over, the one named last changes fastest.
Arguments:
- block_input: bfloat16 [2, 1536, 2048], P(None, ('dp', 'tensor')), may hold values from -6 to 6
- segment_ids: int32 [2, 1536], P(None, 'dp'), may hold values from 0 to 2, as said below
- out_cotangent: bfloat16 [2, 1536, 2048], P(None, ('dp', 'tensor')), may hold values from -6 to 6
- attn_norm: float32 [2, 2048], P('section'), may hold values from 0.5 to 1.5
- q_weight: bfloat16 [2, 2048, 2048], P('section', 'dp', 'tensor'), may hold values from -0.125 to 0.125
- k_weight: bfloat16 [2, 2048, 1024], P('section', 'dp', 'tensor'), may hold values from -0.125 to 0.125
- v_weight: bfloat16 [2, 2048, 1024], P('section', 'dp', 'tensor'), may hold values from -0.125 to 0.125
- o_weight: bfloat16 [2, 2048, 2048], P('section', 'tensor', 'dp'), may hold values from -1 to 1
- q_norm: float32 [2, 128], P('section'), may hold values from 0.5 to 1.5
- k_norm: float32 [2, 128], P('section'), may hold values from 0.5 to 1.5
- ffn_norm: float32 [2, 2048], P('section'), may hold values from 0.5 to 1.5
- gate_weight: bfloat16 [2, 2048, 6144], P('section', 'dp', 'tensor'), may hold values from -0.125 to 0.125
- up_weight: bfloat16 [2, 2048, 6144], P('section', 'dp', 'tensor'), may hold values from -0.125 to 0.125
- down_weight: bfloat16 [2, 6144, 2048], P('section', 'tensor', 'dp'), may hold values from -0.078125 to 0.078125
Outputs:
- section_outputs: bfloat16 [2, 2, 1536, 2048], P('section', None, ('dp', 'tensor'))
- section_input_grads: bfloat16 [2, 2, 1536, 2048], P('section', None, ('dp', 'tensor'))
- attn_norm_grad: float32 [2, 2048], P('section')
- q_weight_grad: float32 [2, 2048, 2048], P('section', 'dp', 'tensor')
- k_weight_grad: float32 [2, 2048, 1024], P('section', 'dp', 'tensor')
- v_weight_grad: float32 [2, 2048, 1024], P('section', 'dp', 'tensor')
- o_weight_grad: float32 [2, 2048, 2048], P('section', 'tensor', 'dp')
- q_norm_grad: float32 [2, 128], P('section')
- k_norm_grad: float32 [2, 128], P('section')
- ffn_norm_grad: float32 [2, 2048], P('section')
- gate_weight_grad: float32 [2, 2048, 6144], P('section', 'dp', 'tensor')
- up_weight_grad: float32 [2, 2048, 6144], P('section', 'dp', 'tensor')
- down_weight_grad: float32 [2, 6144, 2048], P('section', 'tensor', 'dp')
The draws below stay inside these ranges and needn't reach their ends.
Inputs may be any that keep to these rules, and one draw needn't show every extreme that they name: `segment_ids`: each sequence of 192 tokens holds three documents numbered 0, 1, 2 in order; document 1 starts at a position from 24 to 47, and document 2 starts at a position from 144 to 167.
All inputs are finite; a program needn't handle non-finite values.
Results may differ from the reference program's by a relative error of at most 0.03.
Values may be sent and summed in bfloat16 or wider, within the bound.
A program may use at most 384 MiB of HBM per device.

```python
import jax
import jax.numpy as jnp
from jax import lax

D = 2048
HEADS = 16
KV_HEADS = 8
HEAD_DIM = 128
FF = 6144
SEQ = 192
MICRO = 2
ROWS = 1536
N_SECTION = 2


def draw_segment_ids(key, part):
    key = jax.random.fold_in(key, 7)
    key_first, key_second = jax.random.split(key)
    sequences = ROWS // SEQ
    first_cut = jax.random.randint(key_first, (MICRO, sequences, 1), SEQ // 8, SEQ // 4)
    second_cut = jax.random.randint(key_second, (MICRO, sequences, 1), 3 * SEQ // 4, 7 * SEQ // 8)
    position = jnp.arange(SEQ).astype(jnp.int32)[None, None, :]
    numbers = (position >= first_cut).astype(jnp.int32) + (position >= second_cut).astype(jnp.int32)
    return numbers.reshape(MICRO, ROWS).astype(jnp.int32)


def strengthened(drawn, own_key, source, target, shards_of, factor):
    def block_of(dim):
        return (jnp.arange(drawn.shape[dim]) // (drawn.shape[dim] // shards_of)).reshape((-1,) + (1,) * (drawn.ndim - 1 - dim))

    one_side = jax.random.permutation(own_key, shards_of)[block_of(target)]
    other_side = (block_of(target) + shards_of // 2) % shards_of
    return jnp.where((block_of(source) == one_side) | (block_of(source) == other_side), factor * drawn, drawn)


def steps_of(stream_key, extent, shards, low, largest):
    loudness, own = 1.0, jax.random.fold_in(stream_key, 6)
    for dim, parts in shards:
        steps = jnp.exp(jax.random.uniform(jax.random.fold_in(own, dim), (parts,), jnp.float32, low / len(shards), largest / len(shards)))
        loudness = loudness * jnp.repeat(steps, extent[dim] // parts).reshape([-1 if axis == dim else 1 for axis in range(len(extent))])
    return loudness


def gaussian(own_key, extent, deviation, bound, cuts=(), held_as=jnp.bfloat16):
    factor_of = steps_of(own_key, extent, cuts, -0.22, 0.18) if cuts else 1.0
    entries = jax.random.normal(own_key, extent, jnp.float32) * deviation * factor_of
    return jnp.minimum(jnp.maximum(entries, -bound), bound).astype(held_as)


def bell_draw_with(stream_key, extent, width, limit, cuts, heavy, kind=jnp.bfloat16):
    values = width * jax.random.normal(stream_key, extent, jnp.float32)
    if cuts:
        values = values * steps_of(stream_key, extent, cuts, -0.22, 0.18)
    return jnp.clip(strengthened(values, jax.random.fold_in(stream_key, 3), *heavy), -limit, limit).astype(kind)


def setup_inputs(seed: int = 0) -> dict:
    keys = jax.random.split(jax.random.key(seed), 15)
    return {
        "block_input": bell_draw_with(keys[0], (MICRO, ROWS, D), 1.0, 6.0, ((1, 16),), (1, 2, 16, 2.0)),
        "segment_ids": draw_segment_ids(jax.random.fold_in(keys[14], 71), 0),
        "out_cotangent": gaussian(keys[2], (MICRO, ROWS, D), 1.0, 6.0, ((1, 16),)),
        "attn_norm": jnp.clip(1.0 + 0.1 * jax.random.normal(keys[3], (N_SECTION, D), jnp.float32), 0.5, 1.5),
        "q_weight": gaussian(keys[4], (N_SECTION, D, HEADS * HEAD_DIM), D ** -0.5, 0.125, ((0, 2), (1, 8), (2, 2))),
        "k_weight": gaussian(keys[5], (N_SECTION, D, KV_HEADS * HEAD_DIM), D ** -0.5, 0.125, ((0, 2), (1, 8), (2, 2))),
        "v_weight": gaussian(keys[6], (N_SECTION, D, KV_HEADS * HEAD_DIM), D ** -0.5, 0.125, ((0, 2), (1, 8), (2, 2))),
        "o_weight": gaussian(keys[7], (N_SECTION, HEADS * HEAD_DIM, D), (HEADS * HEAD_DIM // 64) ** -0.5, 1.0, ((0, 2), (1, 2), (2, 8))),
        "q_norm": jnp.clip(1.0 + 0.1 * jax.random.normal(keys[8], (N_SECTION, HEAD_DIM), jnp.float32), 0.5, 1.5),
        "k_norm": jnp.clip(1.0 + 0.1 * jax.random.normal(keys[9], (N_SECTION, HEAD_DIM), jnp.float32), 0.5, 1.5),
        "ffn_norm": jnp.clip(1.0 + 0.1 * jax.random.normal(keys[10], (N_SECTION, D), jnp.float32), 0.5, 1.5),
        "gate_weight": gaussian(keys[11], (N_SECTION, D, FF), D ** -0.5, 0.125, ((0, 2), (1, 8), (2, 2))),
        "up_weight": gaussian(keys[12], (N_SECTION, D, FF), D ** -0.5, 0.125, ((0, 2), (1, 8), (2, 2))),
        "down_weight": gaussian(keys[13], (N_SECTION, FF, D), FF ** -0.5, 0.078125, ((0, 2), (1, 2), (2, 8))),
    }


norm_eps = 1e-06
rope_base = 1000000.0
masked_score = -1e+30
highest = lax.Precision.HIGHEST

@jax.custom_vjp
def low(v):
    return lax.optimization_barrier(v.astype(jnp.bfloat16)).astype(jnp.float32)

@jax.custom_vjp
def low_back(v):
    return v

def low_keep(v):
    return (low(v), None)

def low_pass(kept, grad):
    return (grad,)

def back_keep(v):
    return (v, None)

def back_low(kept, grad):
    return (low(grad),)
low.defvjp(low_keep, low_pass)
low_back.defvjp(back_keep, back_low)

def matmul(left_side, right_side):
    return jnp.dot(left_side, right_side, precision=highest, preferred_element_type=jnp.float32)

def inverse_rms(values):
    return lax.rsqrt(lax.optimization_barrier(jnp.mean(values * values, axis=-1, keepdims=True)) + norm_eps)

def rope_tables(length, head_width):
    exponent = jnp.arange(0, head_width, 2).astype(jnp.float32) / head_width
    inverse = rope_base ** (-exponent)
    angles = jnp.arange(length).astype(jnp.float32)[:, None] * inverse[None, :]
    cosine = jnp.cos(angles)
    sine_table = jnp.sin(angles)
    return (jnp.concatenate([cosine, cosine], axis=-1), jnp.concatenate([sine_table, sine_table], axis=-1))

def rotate_half(values):
    half_width = values.shape[-1] // 2
    return jnp.concatenate([-values[..., half_width:], values[..., :half_width]], axis=-1)

def apply_rope(values, cosine, sine_table):
    return values * cosine[:, None, :] + rotate_half(values) * sine_table[:, None, :]

def layer(hidden_in, segments, weights):
    attn_gain, w_query, w_key, w_value, w_output, query_gain, key_gain, ffn_gain, w_gate, w_up, w_down = weights
    length = hidden_in.shape[0]
    hidden_in = low_back(hidden_in)
    normed = low(hidden_in * inverse_rms(hidden_in) * attn_gain)
    queries = low_back(matmul(normed, w_query)).reshape(length, HEADS, HEAD_DIM)
    key_raw = low_back(matmul(normed, w_key)).reshape(length, KV_HEADS, HEAD_DIM)
    values = low(low_back(matmul(normed, w_value))).reshape(length, KV_HEADS, HEAD_DIM)
    cosine, sine_table = rope_tables(length, HEAD_DIM)
    query_rot = low(apply_rope(queries * inverse_rms(queries) * query_gain, cosine, sine_table))
    key_rot = low(apply_rope(key_raw * inverse_rms(key_raw) * key_gain, cosine, sine_table))
    group_size = HEADS // KV_HEADS
    key_all = jnp.repeat(key_rot, group_size, axis=1)
    value_all = jnp.repeat(values, group_size, axis=1)
    scores = jnp.einsum('qhd,khd->hqk', query_rot, key_all, precision=highest, preferred_element_type=jnp.float32)
    scores = low_back(scores * HEAD_DIM ** (-0.5))
    position = jnp.arange(length)
    allowed = (position[:, None] >= position[None, :]) & (segments[:, None] == segments[None, :])
    scores = jnp.where(allowed[None], scores, masked_score)
    row_top = lax.optimization_barrier(jnp.max(scores, axis=-1, keepdims=True))
    exponent = jnp.exp(scores - row_top)
    soft_weights = low(exponent / lax.optimization_barrier(jnp.sum(exponent, axis=-1, keepdims=True)))
    attended = jnp.einsum('hqk,khd->qhd', soft_weights, value_all, precision=highest, preferred_element_type=jnp.float32)
    attended = low(low_back(attended.reshape(length, HEADS * HEAD_DIM)))
    mixed_rows = hidden_in + low_back(matmul(attended, w_output))
    normed_ffn = low(mixed_rows * inverse_rms(mixed_rows) * ffn_gain)
    gate_pre = low_back(matmul(normed_ffn, w_gate))
    upward = low_back(matmul(normed_ffn, w_up))
    activated = low(gate_pre * jax.nn.sigmoid(gate_pre) * upward)
    return low(mixed_rows + low_back(matmul(activated, w_down)))

def reference(block_input, segment_ids, out_cotangent, attn_norm, q_weight, k_weight, v_weight, o_weight, q_norm, k_norm, ffn_norm, gate_weight, up_weight, down_weight):
    stacked = (attn_norm, q_weight, k_weight, v_weight, o_weight, q_norm, k_norm, ffn_norm, gate_weight, up_weight, down_weight)
    first_weights = tuple((array[0].astype(jnp.float32) for array in stacked))
    second_weights = tuple((array[1].astype(jnp.float32) for array in stacked))
    inputs = block_input.reshape(-1, SEQ, D).astype(jnp.float32)
    segments_all = segment_ids.reshape(-1, SEQ)
    cotangents = out_cotangent.reshape(-1, SEQ, D).astype(jnp.float32)

    def one_sequence(totals, packed):
        tokens_in, seq_ids, cotangent = packed
        first_out, first_back = jax.vjp(lambda hidden, weights: layer(hidden, seq_ids, weights), tokens_in, first_weights)
        second_out, second_back = jax.vjp(lambda hidden, weights: layer(hidden, seq_ids, weights), first_out, second_weights)
        middle_grad, second_grads = second_back(cotangent)
        input_grad, first_grads = first_back(middle_grad)
        totals = jax.tree.map(lambda running, addend: running + addend, totals, (first_grads, second_grads))
        return (totals, (first_out, second_out, input_grad, middle_grad))
    zeros = jax.tree.map(jnp.zeros_like, (first_weights, second_weights))
    totals, (first_outs, second_outs, input_grads, middle_grads) = lax.scan(one_sequence, zeros, (inputs, segments_all, cotangents))
    outputs = jnp.stack([first_outs, second_outs]).reshape(2, MICRO, ROWS, D).astype(jnp.bfloat16)
    grads_in = jnp.stack([input_grads, middle_grads]).reshape(2, MICRO, ROWS, D).astype(jnp.bfloat16)
    per_weight = [jnp.stack([grad_one, grad_two]) for grad_one, grad_two in zip(totals[0], totals[1])]
    return (outputs, grads_in, per_weight[0], per_weight[1], per_weight[2], per_weight[3], per_weight[4], per_weight[5], per_weight[6], per_weight[7], per_weight[8], per_weight[9], per_weight[10])
```

```python
import functools

import jax
import jax.numpy as jnp
from jax import lax
from jax.experimental import pallas as pl
from jax.experimental.pallas import tpu as pltpu
from jax.sharding import PartitionSpec as P

norm_eps = 1e-06
rope_base = 1000000.0
masked_score = -1e30
f32 = jnp.float32
bf16 = jnp.bfloat16
MIB = 1024 * 1024


def dot_nn(left, right):
    return lax.dot_general(left, right, (((1,), (0,)), ((), ())), preferred_element_type=f32)


def dot_nt(left, right):
    return lax.dot_general(left, right, (((1,), (1,)), ((), ())), preferred_element_type=f32)


def dot_tn(left, right):
    return lax.dot_general(left, right, (((0,), (0,)), ((), ())), preferred_element_type=f32)


def inverse_rms(values):
    return lax.rsqrt(jnp.mean(values * values, axis=-1, keepdims=True) + norm_eps)


def norm_back(grad_out, values, inverse, gain_vec):
    scaled = grad_out * gain_vec
    return inverse * (
        scaled - values * inverse * inverse * jnp.mean(scaled * values, axis=-1, keepdims=True)
    )


def rotated(raw, gain, cosine, signed_sine):
    inverse = inverse_rms(raw)
    scaled = raw * inverse * gain
    turned = scaled * cosine + pltpu.roll(scaled, 64, 1) * signed_sine
    return inverse, turned.astype(bf16)


def softmax_rows(query_rot, key_rot, allowed, scale):
    scores = jnp.where(allowed, dot_nt(query_rot, key_rot) * scale, masked_score)
    exponent = jnp.exp(scores - jnp.max(scores, axis=-1, keepdims=True))
    return exponent / jnp.sum(exponent, axis=-1, keepdims=True)


def attn_forward_kernel(
    group, width, normed, w_q, w_k, w_v, w_o, gains, cosine, signed_sine, mask,
    queries, keys, values, attended, partial, total,
):
    rows = normed[...]
    raw_q = dot_nn(rows, w_q[...])
    raw_k = dot_nn(rows, w_k[...])
    value = dot_nn(rows, w_v[...]).astype(bf16)
    queries[...] = raw_q
    keys[...] = raw_k
    values[...] = value
    cos, sin = cosine[...], signed_sine[...]
    allowed = mask[...] > 0.5
    _, key_rot = rotated(raw_k, gains[1:2, :], cos, sin)
    scale = width ** (-0.5)
    heads = []
    for head in range(group):
        _, query_rot = rotated(raw_q[:, head * width : (head + 1) * width], gains[0:1, :], cos, sin)
        weights = softmax_rows(query_rot, key_rot, allowed, scale)
        heads.append(dot_nn(weights.astype(bf16), value).astype(bf16))
    mixed = jnp.concatenate(heads, axis=1)
    attended[...] = mixed
    product = dot_nt(mixed, w_o[...])
    step = pl.program_id(0)

    @pl.when(step == 0)
    def _():
        total[...] = product

    @pl.when(step > 0)
    def _():
        total[...] += product

    @pl.when(step == pl.num_programs(0) - 1)
    def _():
        partial[...] = total[...].astype(bf16)


def attn_backward_kernel(
    group, width, grad_proj, queries, keys, values, w_q, w_k, w_v, w_o, gains, cosine, signed_sine,
    mask, grads, gain_grads, partial, total,
):
    step = pl.program_id(0)
    cos, sin = cosine[...], signed_sine[...]
    allowed = mask[...] > 0.5
    scale = width ** (-0.5)
    gain_q, gain_k = gains[0:1, :], gains[1:2, :]
    grad_attended = dot_nn(grad_proj[...], w_o[...]).astype(bf16)
    raw_k, value = keys[...], values[...]
    inverse_k, key_rot = rotated(raw_k, gain_k, cos, sin)
    grad_key = jnp.zeros_like(raw_k)
    grad_value = jnp.zeros_like(raw_k)
    gain_q_sum = jnp.zeros((1, width), f32)
    parts = []
    for head in range(group):
        raw_q = queries[:, head * width : (head + 1) * width]
        grad_head = grad_attended[:, head * width : (head + 1) * width]
        inverse_q, query_rot = rotated(raw_q, gain_q, cos, sin)
        weights = softmax_rows(query_rot, key_rot, allowed, scale)
        grad_weights = dot_nt(grad_head, value)
        delta = jnp.sum(weights * grad_weights, axis=-1, keepdims=True)
        grad_scores = (weights * (grad_weights - delta)).astype(bf16)
        grad_value += dot_tn(weights.astype(bf16), grad_head)
        grad_key += dot_tn(grad_scores, query_rot)
        grad_query = dot_nn(grad_scores, key_rot) * scale
        grad_query = grad_query * cos - pltpu.roll(grad_query, 64, 1) * sin
        gain_q_sum += jnp.sum(grad_query * raw_q * inverse_q, axis=0, keepdims=True)
        parts.append(norm_back(grad_query, raw_q, inverse_q, gain_q).astype(bf16))
    grad_key = grad_key * scale
    grad_key = grad_key * cos - pltpu.roll(grad_key, 64, 1) * sin
    gain_k_sum = jnp.sum(grad_key * raw_k * inverse_k, axis=0, keepdims=True)
    grad_q = jnp.concatenate(parts, axis=1)
    grad_k = norm_back(grad_key, raw_k, inverse_k, gain_k).astype(bf16)
    grad_v = grad_value.astype(bf16)
    grads[0, :, :] = jnp.concatenate([grad_q, grad_k, grad_v], axis=1)
    sums = jnp.concatenate([gain_q_sum, gain_k_sum, jnp.zeros((6, width), f32)], axis=0)
    product = dot_nt(grad_q, w_q[...]) + dot_nt(grad_k, w_k[...]) + dot_nt(grad_v, w_v[...])

    @pl.when(step == 0)
    def _():
        total[...] = product
        gain_grads[...] = sums

    @pl.when(step > 0)
    def _():
        total[...] += product
        gain_grads[...] += sums

    @pl.when(step == pl.num_programs(0) - 1)
    def _():
        partial[...] = total[...].astype(bf16)


def ffn_forward_kernel(normed, w_gate, w_up, w_down, gate, upward, activated, partial, total):
    step = pl.program_id(0)
    rows = normed[...]
    gate_block = dot_nn(rows, w_gate[...])
    up_block = dot_nn(rows, w_up[...])
    gate[...] = gate_block
    upward[...] = up_block
    active = (gate_block * jax.nn.sigmoid(gate_block) * up_block).astype(bf16)
    activated[...] = active
    product = dot_nt(active, w_down[...])

    @pl.when(step == 0)
    def _():
        total[...] = product

    @pl.when(step > 0)
    def _():
        total[...] += product

    @pl.when(step == pl.num_programs(0) - 1)
    def _():
        partial[...] = total[...].astype(bf16)


def ffn_backward_kernel(grad_down, gate, upward, w_gate, w_up, w_down, grads, partial, total):
    step = pl.program_id(0)
    grad_act = dot_nn(grad_down[...], w_down[...])
    gate_block, up_block = gate[...], upward[...]
    sig = jax.nn.sigmoid(gate_block)
    grad_gate = (grad_act * up_block * sig * (1.0 + gate_block * (1.0 - sig))).astype(bf16)
    grad_up = (grad_act * gate_block * sig).astype(bf16)
    grads[0, :, :] = grad_gate
    grads[1, :, :] = grad_up
    product = dot_nt(grad_gate, w_gate[...]) + dot_nt(grad_up, w_up[...])

    @pl.when(step == 0)
    def _():
        total[...] = product

    @pl.when(step > 0)
    def _():
        total[...] += product

    @pl.when(step == pl.num_programs(0) - 1)
    def _():
        partial[...] = total[...].astype(bf16)


def weight_grad_kernel(left_t, right, out):
    out[...] = dot_nn(left_t[0], right[0]).astype(bf16)


def whole(shape):
    return pl.BlockSpec(shape, lambda step: (0,) * len(shape))


def columns(rows, width, first):
    return pl.BlockSpec((rows, width), lambda step: (0, first + step))


def params(mib):
    return pltpu.CompilerParams(
        dimension_semantics=("arbitrary",), vmem_limit_bytes=mib * MIB
    )


def cost(flops, size):
    return pl.CostEstimate(flops=int(flops), bytes_accessed=int(size), transcendentals=0)


def attn_forward(normed, pack, gains, tables, mask):
    length, depth = normed.shape
    width = gains.shape[1]
    q_width = pack.shape[1] // 3
    kv_heads = q_width // 2 // width
    group = q_width // width // kv_heads
    blk = group * width
    return pl.pallas_call(
        functools.partial(attn_forward_kernel, group, width),
        grid=(kv_heads,),
        in_specs=[
            whole((length, depth)),
            columns(depth, blk, 0),
            columns(depth, width, q_width // width),
            columns(depth, width, q_width // width + kv_heads),
            columns(depth, blk, 2 * q_width // blk),
            whole(gains.shape),
            whole((length, width)),
            whole((length, width)),
            whole((length, length)),
        ],
        out_specs=[
            columns(length, blk, 0),
            columns(length, width, 0),
            columns(length, width, 0),
            columns(length, blk, 0),
            whole((length, depth)),
        ],
        out_shape=[
            jax.ShapeDtypeStruct((length, q_width), f32),
            jax.ShapeDtypeStruct((length, q_width // 2), f32),
            jax.ShapeDtypeStruct((length, q_width // 2), bf16),
            jax.ShapeDtypeStruct((length, q_width), bf16),
            jax.ShapeDtypeStruct((length, depth), bf16),
        ],
        scratch_shapes=[pltpu.VMEM((length, depth), f32)],
        compiler_params=params(32),
        cost_estimate=cost(2 * length * depth * pack.shape[1], pack.size * 2),
        name="attn_forward",
    )(normed, pack, pack, pack, pack, gains, *tables, mask)


def attn_backward(grad_proj, queries, keys, values, pack, gains, tables, mask):
    length, depth = grad_proj.shape
    width = gains.shape[1]
    q_width = pack.shape[1] // 3
    kv_heads = q_width // 2 // width
    group = q_width // width // kv_heads
    blk = group * width
    return pl.pallas_call(
        functools.partial(attn_backward_kernel, group, width),
        grid=(kv_heads,),
        in_specs=[
            whole((length, depth)),
            columns(length, blk, 0),
            columns(length, width, 0),
            columns(length, width, 0),
            columns(depth, blk, 0),
            columns(depth, width, q_width // width),
            columns(depth, width, q_width // width + kv_heads),
            columns(depth, blk, 2 * q_width // blk),
            whole(gains.shape),
            whole((length, width)),
            whole((length, width)),
            whole((length, length)),
        ],
        out_specs=[
            pl.BlockSpec((1, length, blk + 2 * width), lambda step: (step, 0, 0)),
            whole((8, width)),
            whole((length, depth)),
        ],
        out_shape=[
            jax.ShapeDtypeStruct((kv_heads, length, blk + 2 * width), bf16),
            jax.ShapeDtypeStruct((8, width), f32),
            jax.ShapeDtypeStruct((length, depth), bf16),
        ],
        scratch_shapes=[pltpu.VMEM((length, depth), f32)],
        compiler_params=params(32),
        cost_estimate=cost(2 * length * depth * pack.shape[1], pack.size * 2),
        name="attn_backward",
    )(grad_proj, queries, keys, values, pack, pack, pack, pack, gains, *tables, mask)


def unit_block(units):
    return 512 if units % 512 == 0 else 256


def ffn_forward(normed, pack):
    length, depth = normed.shape
    units = pack.shape[1] // 3
    blk = unit_block(units)
    steps = units // blk
    return pl.pallas_call(
        ffn_forward_kernel,
        grid=(steps,),
        in_specs=[
            whole((length, depth)),
            columns(depth, blk, 0),
            columns(depth, blk, steps),
            columns(depth, blk, 2 * steps),
        ],
        out_specs=[
            columns(length, blk, 0),
            columns(length, blk, 0),
            columns(length, blk, 0),
            whole((length, depth)),
        ],
        out_shape=[
            jax.ShapeDtypeStruct((length, units), f32),
            jax.ShapeDtypeStruct((length, units), f32),
            jax.ShapeDtypeStruct((length, units), bf16),
            jax.ShapeDtypeStruct((length, depth), bf16),
        ],
        scratch_shapes=[pltpu.VMEM((length, depth), f32)],
        compiler_params=params(40),
        cost_estimate=cost(2 * length * depth * pack.shape[1], pack.size * 2),
        name="ffn_forward",
    )(normed, pack, pack, pack)


def ffn_backward(grad_down, gate, upward, pack):
    length, depth = grad_down.shape
    units = pack.shape[1] // 3
    blk = unit_block(units)
    steps = units // blk
    return pl.pallas_call(
        ffn_backward_kernel,
        grid=(steps,),
        in_specs=[
            whole((length, depth)),
            columns(length, blk, 0),
            columns(length, blk, 0),
            columns(depth, blk, 0),
            columns(depth, blk, steps),
            columns(depth, blk, 2 * steps),
        ],
        out_specs=[
            pl.BlockSpec((2, length, blk), lambda step: (0, 0, step)),
            whole((length, depth)),
        ],
        out_shape=[
            jax.ShapeDtypeStruct((2, length, units), bf16),
            jax.ShapeDtypeStruct((length, depth), bf16),
        ],
        scratch_shapes=[pltpu.VMEM((length, depth), f32)],
        compiler_params=params(40),
        cost_estimate=cost(2 * length * depth * pack.shape[1], pack.size * 2),
        name="ffn_backward",
    )(grad_down, gate, upward, pack, pack, pack)


def weight_grad(left_t, right, which):
    _, depth, tokens = left_t.shape
    count, _, width = right.shape
    blk = unit_block(width)
    per = width // blk
    return pl.pallas_call(
        weight_grad_kernel,
        grid=(count * per,),
        in_specs=[
            pl.BlockSpec((1, depth, tokens), lambda step: (which(step // per), 0, 0)),
            pl.BlockSpec((1, tokens, blk), lambda step: (step // per, 0, step % per)),
        ],
        out_specs=pl.BlockSpec((depth, blk), lambda step: (0, step)),
        out_shape=jax.ShapeDtypeStruct((depth, count * width), bf16),
        compiler_params=params(40),
        cost_estimate=cost(
            2 * depth * tokens * count * width, depth * count * width * 2 + right.size * 2
        ),
        name="weight_grad",
    )(left_t, right)


def rope_tables(position, head_width):
    exponent = jnp.arange(0, head_width, 2).astype(f32) / head_width
    inverse = rope_base ** (-exponent)
    angles = position.astype(f32)[:, None] * inverse[None, :]
    cosine, sine = jnp.cos(angles), jnp.sin(angles)
    return (
        jnp.concatenate([cosine, cosine], axis=-1),
        jnp.concatenate([-sine, sine], axis=-1),
    )


def per_device(
    block_input,
    segment_ids,
    out_cotangent,
    attn_norm,
    q_weight,
    k_weight,
    v_weight,
    o_weight,
    q_norm,
    k_norm,
    ffn_norm,
    gate_weight,
    up_weight,
    down_weight,
):
    section = lax.axis_index("section")
    place = lax.axis_index("dp")
    core = place % 2
    half = lax.axis_index("tensor")
    n_dp = lax.axis_size("dp")
    n_chip = n_dp // 2
    micro_count, own_rows, depth = block_input.shape
    quarter = own_rows // 2
    length = 2 * own_rows
    head_width = q_norm.shape[1]
    first_core = core == 0
    swap_core = [(i, i ^ 1) for i in range(n_dp)]
    swap_half = [(0, 1), (1, 0)]
    chip_groups = [[2 * chip + one for chip in range(n_chip)] for one in (0, 1)]

    def to_core(values):
        return lax.ppermute(values, "dp", swap_core)

    def to_half(values):
        return lax.ppermute(values, "tensor", swap_half)

    def split_columns(weight):
        side = weight.shape[1] // 2
        left, right = weight[:, :side], weight[:, side:]
        return jnp.where(first_core, left, right), jnp.where(first_core, right, left)

    def split_rows(weight):
        side = weight.shape[0] // 2
        left, right = weight[:side].T, weight[side:].T
        return jnp.where(first_core, left, right), jnp.where(first_core, right, left)

    def gathered(pairs):
        mine = jnp.concatenate([pair[0] for pair in pairs], axis=1)
        theirs = to_core(jnp.concatenate([pair[1] for pair in pairs], axis=1))
        chip_block = jnp.concatenate(
            [jnp.where(first_core, mine, theirs), jnp.where(first_core, theirs, mine)], axis=0
        )
        return lax.all_gather(
            chip_block, "dp", axis=0, tiled=True, axis_index_groups=chip_groups
        )

    attn_pack = gathered(
        [
            split_columns(q_weight[0]),
            split_columns(k_weight[0]),
            split_columns(v_weight[0]),
            split_rows(o_weight[0]),
        ]
    )
    ffn_pack = gathered(
        [split_columns(gate_weight[0]), split_columns(up_weight[0]), split_rows(down_weight[0])]
    )

    attn_gain, ffn_gain = attn_norm[0], ffn_norm[0]
    head_gains = jnp.concatenate([q_norm, k_norm, jnp.zeros((6, head_width), f32)], axis=0)

    both = jnp.stack([block_input, out_cotangent])
    kept = jnp.where(first_core, both[:, :, :quarter], both[:, :, quarter:])
    received = to_core(jnp.where(first_core, both[:, :, quarter:], both[:, :, :quarter]))
    first_rows = jnp.where(first_core, kept, received)
    second_rows = jnp.where(first_core, received, kept)
    inputs = [[rows[0, micro] for rows in (first_rows, second_rows)] for micro in range(micro_count)]
    cotangents = [
        [rows[1, micro] for rows in (first_rows, second_rows)] for micro in range(micro_count)
    ]

    def arranged(values):
        parts = values.reshape(2, 2, quarter)
        parts = jnp.where(half == 0, parts, parts[::-1])
        parts = jnp.where(first_core, parts, parts[:, ::-1])
        return parts.transpose(1, 0, 2).reshape(length)

    position = arranged(jnp.arange(length, dtype=jnp.int32))
    tables = rope_tables(position, head_width)
    other_ids = to_core(segment_ids)
    masks = []
    for micro in range(micro_count):
        own, other = segment_ids[micro], other_ids[micro]
        pair = []
        for ids in (jnp.where(first_core, own, other), jnp.where(first_core, other, own)):
            ids = arranged(ids)
            allowed = (position[:, None] >= position[None, :]) & (ids[:, None] == ids[None, :])
            pair.append(allowed.astype(f32))
        masks.append(pair)

    def row_gather(rows):
        pair = jnp.concatenate([rows, to_half(rows)], axis=0)
        return jnp.concatenate([pair, to_core(pair)], axis=0)

    def row_scatter(partial):
        side = 2 * quarter
        pair = partial[:side].astype(f32) + to_core(partial[side:]).astype(f32)
        return pair[:quarter] + to_half(pair[quarter:].astype(bf16)).astype(f32)

    def layer_forward(hidden_in, mask):
        hidden = hidden_in.astype(f32)
        inverse_in = inverse_rms(hidden)
        normed = row_gather((hidden * inverse_in * attn_gain).astype(bf16))
        queries, keys, values, attended, partial = attn_forward(
            normed, attn_pack, head_gains, tables, mask
        )
        mixed = hidden + row_scatter(partial)
        inverse_mid = inverse_rms(mixed)
        normed_ffn = row_gather((mixed * inverse_mid * ffn_gain).astype(bf16))
        gate, upward, activated, partial = ffn_forward(normed_ffn, ffn_pack)
        result = (mixed + row_scatter(partial)).astype(bf16)
        back = (hidden_in, queries, keys, values, mixed, gate, upward)
        saved = (normed, attended, normed_ffn, activated)
        return result, back, saved

    def layer_backward(grad_in, back, mask):
        hidden_in, queries, keys, values, mixed, gate, upward = back
        grad_down = row_gather(grad_in)
        ffn_grads, partial = ffn_backward(grad_down, gate, upward, ffn_pack)
        grad_normed_ffn = row_scatter(partial)
        inverse_mid = inverse_rms(mixed)
        ffn_gain_grad = jnp.sum(grad_normed_ffn * mixed * inverse_mid, axis=0)
        grad_mixed = grad_in.astype(f32) + norm_back(
            grad_normed_ffn, mixed, inverse_mid, ffn_gain
        )
        grad_proj = row_gather(grad_mixed.astype(bf16))
        attn_grads, head_gain_grads, partial = attn_backward(
            grad_proj, queries, keys, values, attn_pack, head_gains, tables, mask
        )
        grad_normed = row_scatter(partial)
        hidden = hidden_in.astype(f32)
        inverse_in = inverse_rms(hidden)
        attn_gain_grad = jnp.sum(grad_normed * hidden * inverse_in, axis=0)
        grad_hidden = (grad_mixed + norm_back(grad_normed, hidden, inverse_in, attn_gain)).astype(
            bf16
        )
        saved = (grad_down, ffn_grads, grad_proj, attn_grads)
        gains = (attn_gain_grad, ffn_gain_grad, head_gain_grads)
        return grad_hidden, saved, gains

    at_first = section == 0

    def pick(first, second):
        return jax.tree.map(lambda a, b: jnp.where(at_first, a, b), first, second)

    chunks = range(2)
    forward_route = [(0, 1)]
    backward_route = [(1, 0)]
    zero_rows = jnp.zeros_like(inputs[0][0])
    forward_masks = [masks[0], pick(masks[1], masks[0]), masks[1]]
    results, backs, saves = [], [], []
    for step in range(3):
        step_out = []
        for chunk in chunks:
            own = inputs[step][chunk] if step < 2 else zero_rows
            if step > 0:
                arrived = lax.ppermute(results[step - 1][chunk], "section", forward_route)
                own = jnp.where(at_first, own, arrived)
            step_out.append(layer_forward(own, forward_masks[step][chunk]))
        results.append([out[0] for out in step_out])
        backs.append([out[1] for out in step_out])
        saves.append([out[2] for out in step_out])
    backward_masks = [masks[0], pick(masks[0], masks[1]), masks[1]]
    grads, back_saves, gain_total = [], [], None
    for step in range(3):
        step_out = []
        for chunk in chunks:
            own = cotangents[step][chunk] if step < 2 else zero_rows
            if step > 0:
                arrived = lax.ppermute(grads[step - 1][chunk], "section", backward_route)
            else:
                arrived = zero_rows
            own = jnp.where(at_first, arrived, own)
            back = pick(backs[0][chunk], backs[2][chunk]) if step == 1 else backs[1][chunk]
            step_out.append(layer_backward(own, back, backward_masks[step][chunk]))
            gains = step_out[-1][2]
            gain_total = gains if gain_total is None else jax.tree.map(jnp.add, gain_total, gains)
        grads.append([out[0] for out in step_out])
        back_saves.append([out[1] for out in step_out])

    def micro_rows(table, first_step, second_step):
        return [pick(table[first_step][chunk], table[second_step][chunk]) for chunk in chunks]

    out_rows = jnp.stack(
        [jnp.stack(micro_rows(results, micro, micro + 1)) for micro in range(2)]
        + [jnp.stack(micro_rows(grads, micro + 1, micro)) for micro in range(2)]
    )
    mine = jnp.where(first_core, out_rows[:, 0], out_rows[:, 1])
    theirs = to_core(jnp.where(first_core, out_rows[:, 1], out_rows[:, 0]))
    whole_rows = jnp.concatenate(
        [jnp.where(first_core, mine, theirs), jnp.where(first_core, theirs, mine)], axis=1
    )
    section_outputs, section_input_grads = whole_rows[None, :2], whole_rows[None, 2:]

    saved = [
        pick(saves[micro][chunk], saves[micro + 1][chunk]) for micro in range(2) for chunk in chunks
    ]
    back_saved = [
        pick(back_saves[micro + 1][chunk], back_saves[micro][chunk])
        for micro in range(2)
        for chunk in chunks
    ]

    def stacked(items, axis=0):
        return jnp.concatenate(items, axis=axis)

    normed_t = stacked([item[0] for item in saved]).T
    attended = stacked([item[1] for item in saved])
    normed_ffn_t = stacked([item[2] for item in saved]).T
    activated = stacked([item[3] for item in saved])
    grad_down_t = stacked([item[0] for item in back_saved]).T
    ffn_grads = stacked([item[1] for item in back_saved], axis=1)
    grad_proj_t = stacked([item[2] for item in back_saved]).T
    attn_grads = stacked([item[3] for item in back_saved], axis=1)

    def reduced(partial):
        rows = lax.psum_scatter(
            partial, "dp", scatter_dimension=0, tiled=True, axis_index_groups=chip_groups
        )
        side = rows.shape[0] // 2
        own = jnp.where(first_core, rows[:side], rows[side:])
        other = to_core(jnp.where(first_core, rows[side:], rows[:side]))
        return (
            jnp.where(first_core, own, other).astype(f32),
            jnp.where(first_core, other, own).astype(f32),
        )

    ffn_sides = reduced(
        weight_grad(
            jnp.stack([normed_ffn_t, grad_down_t]),
            jnp.concatenate([ffn_grads, activated[None]], axis=0),
            lambda block: block // 2,
        )
    )
    attn_right = jnp.concatenate([attn_grads, attended[None]], axis=0)
    kv_heads = attn_grads.shape[0]
    attn_sides = reduced(
        weight_grad(
            jnp.stack([normed_t, grad_proj_t]), attn_right, lambda block: block // kv_heads
        )
    )
    units = gate_weight.shape[2] // 2
    q_width = q_weight.shape[2] // 2
    blk = attn_grads.shape[2]
    q_blk = blk - 2 * head_width

    def across(first, last):
        return jnp.concatenate([side[:, first:last] for side in ffn_sides], axis=1)[None]

    def heads_of(first, last):
        return jnp.concatenate(
            [
                side[:, blk * head + first : blk * head + last]
                for side in attn_sides
                for head in range(kv_heads)
            ],
            axis=1,
        )[None]

    down_grad = jnp.concatenate([side[:, 2 * units :].T for side in ffn_sides], axis=0)[None]
    o_grad = jnp.concatenate([side[:, kv_heads * blk :].T for side in attn_sides], axis=0)[None]

    packed = jnp.concatenate(
        [gain_total[0], gain_total[1], gain_total[2][0], gain_total[2][1]]
    ).reshape(-1, head_width)
    packed = packed + to_core(packed)
    packed = packed + to_half(packed)
    reach = 2
    while reach < n_dp:
        packed = packed + lax.ppermute(packed, "dp", [(i, i ^ reach) for i in range(n_dp)])
        reach *= 2
    packed = packed.reshape(-1)
    return (
        section_outputs,
        section_input_grads,
        packed[None, :depth],
        heads_of(0, q_blk),
        heads_of(q_blk, q_blk + head_width),
        heads_of(q_blk + head_width, blk),
        o_grad,
        packed[None, 2 * depth : 2 * depth + head_width],
        packed[None, 2 * depth + head_width :],
        packed[None, depth : 2 * depth],
        across(0, units),
        across(units, 2 * units),
        down_grad,
    )


def solution(mesh):
    rows = P(None, ("dp", "tensor"), None)
    out_rows = P("section", None, ("dp", "tensor"), None)
    gain = P("section", None)
    wide = P("section", "dp", "tensor")
    tall = P("section", "tensor", "dp")
    return jax.shard_map(
        per_device,
        mesh=mesh,
        in_specs=(
            rows, P(None, "dp"), rows, gain, wide, wide, wide, tall, gain, gain, gain, wide, wide, tall,
        ),
        out_specs=(
            out_rows, out_rows, gain, wide, wide, wide, tall, gain, gain, gain, wide, wide, tall,
        ),
        check_vma=False,
    )
```

```python
import functools

import jax
import jax.numpy as jnp
from jax import lax
from jax.experimental import pallas as pl
from jax.experimental.pallas import tpu as pltpu
from jax.sharding import PartitionSpec as P

norm_eps = 1e-06
rope_base = 1000000.0
masked_score = -1e30
row_chunks = 4
f32 = jnp.float32
bf16 = jnp.bfloat16
MIB = 1024 * 1024
MESH = pl.DeviceIdType.MESH


def dot_nn(left, right):
    return lax.dot_general(left, right, (((1,), (0,)), ((), ())), preferred_element_type=f32)


def dot_nt(left, right):
    return lax.dot_general(left, right, (((1,), (1,)), ((), ())), preferred_element_type=f32)


def dot_tn(left, right):
    return lax.dot_general(left, right, (((0,), (0,)), ((), ())), preferred_element_type=f32)


def inverse_rms(values):
    return lax.rsqrt(jnp.mean(values * values, axis=-1, keepdims=True) + norm_eps)


def norm_back(grad_out, values, inverse, gain_vec):
    scaled = grad_out * gain_vec
    return inverse * (
        scaled - values * inverse * inverse * jnp.mean(scaled * values, axis=-1, keepdims=True)
    )


class Exchange:
    def __init__(self, send_sems, recv_sems):
        place = lax.axis_index("dp")
        self.core = {"dp": place + 1 - 2 * (place % 2)}
        self.half = {"tensor": 1 - lax.axis_index("tensor")}
        self.section = {"section": 1 - lax.axis_index("section")}
        self.send_sems, self.recv_sems = send_sems, recv_sems

    def greet(self, with_section):
        barrier = pltpu.get_barrier_semaphore()
        others = [self.core, self.half] + ([self.section] if with_section else [])
        for other in others:
            pl.semaphore_signal(barrier, inc=1, device_id=other, device_id_type=MESH)
        pl.semaphore_wait(barrier, len(others))

    def copy(self, source, target, other, stage, chunk):
        return pltpu.make_async_remote_copy(
            src_ref=source,
            dst_ref=target,
            send_sem=self.send_sems.at[stage, chunk],
            recv_sem=self.recv_sems.at[stage, chunk],
            device_id=other,
            device_id_type=MESH,
        )


def gather_then(exchange, rows, use):
    chunks, total, _ = rows.shape
    own = total // 4
    first = [
        exchange.copy(rows.at[c, pl.ds(0, own)], rows.at[c, pl.ds(own, own)], exchange.half, 0, c)
        for c in range(chunks)
    ]
    second = [
        exchange.copy(
            rows.at[c, pl.ds(0, 2 * own)], rows.at[c, pl.ds(2 * own, 2 * own)], exchange.core, 1, c
        )
        for c in range(chunks)
    ]
    for c in range(chunks):
        first[c].start()
    for c in range(chunks):
        first[c].wait_recv()
        second[c].start()
        if c > 0:
            second[c - 1].wait_recv()
            use(c - 1)
    second[chunks - 1].wait_recv()
    use(chunks - 1)
    return first + second


def scatter_from(exchange, make, finish, keep, send_core, recv_core, send_half, recv_half):
    chunks, pair, _ = keep.shape
    own = pair // 2
    first = [
        exchange.copy(send_core.at[c], recv_core.at[c], exchange.core, 2, c) for c in range(chunks)
    ]
    second = [
        exchange.copy(send_half.at[c], recv_half.at[c], exchange.half, 3, c) for c in range(chunks)
    ]

    def middle(c):
        first[c].wait_recv()
        summed = keep[c] + recv_core[c].astype(f32)
        send_half[c] = summed[own:].astype(bf16)
        second[c].start()
        keep[c, :own] = summed[:own]

    for c in range(chunks):
        product = make(c)
        send_core[c] = product[pair:].astype(bf16)
        first[c].start()
        keep[c] = product[:pair]
        if c > 0:
            middle(c - 1)
    middle(chunks - 1)
    for c in range(chunks):
        second[c].wait_recv()
        finish(c, keep[c, :own] + recv_half[c].astype(f32))
    return first + second


def load_pack(pack, held, sems):
    depth = held.shape[0] // 4
    return [
        pltpu.make_async_copy(
            pack.at[pl.ds(c * depth, depth)], held.at[pl.ds(c * depth, depth)], sems.at[c]
        )
        for c in range(4)
    ]


def row_mean(values):
    size = values.shape[0] * values.shape[2]
    return jnp.sum(jnp.sum(values, axis=0), axis=-1, keepdims=True)[None] * (1.0 / size)


def accumulate(total, left, weights, first_row, first_col, width, start):
    depth = left.shape[1]
    blk = 512 if width % 512 == 0 else 256

    def body(index, _):
        at = pl.multiple_of(index * blk, blk)
        product = dot_nn(left, weights[pl.ds(first_row, depth), pl.ds(first_col + at, blk)])
        if start:
            total[:, pl.ds(at, blk)] = product
        else:
            total[:, pl.ds(at, blk)] += product
        return 0

    lax.fori_loop(0, width // blk, body, 0)


def rotated(raw, gain, cosine, signed_sine):
    inverse = inverse_rms(raw)
    scaled = raw * inverse * gain
    turned = scaled * cosine + pltpu.roll(scaled, 64, 1) * signed_sine
    return inverse, turned.astype(bf16)


def softmax_rows(query_rot, key_rot, allowed, scale):
    scores = jnp.where(allowed, dot_nt(query_rot, key_rot) * scale, masked_score)
    exponent = jnp.exp(scores - jnp.max(scores, axis=-1, keepdims=True))
    return exponent / jnp.sum(exponent, axis=-1, keepdims=True)


def attn_forward_kernel(
    width, hidden, pack, model_gains, gains, cosine, signed_sine, masks,
    normed, projected, values, attended, mixed, normed_ffn_rows,
    held, keep, send_core, recv_core, send_half, recv_half, load_sems, send_sems, recv_sems,
):
    exchange = Exchange(send_sems, recv_sems)
    exchange.greet(False)
    loads = load_pack(pack, held, load_sems)
    for load in loads:
        load.start()
    chunks, own, cols = hidden.shape
    length = 2 * own
    q_width = attended.shape[1]
    kv_width = q_width // 2
    kv_heads = kv_width // width
    group = q_width // kv_width
    rows = hidden[...].astype(f32)
    inverse = lax.rsqrt(row_mean(rows * rows) + norm_eps)
    for c in range(chunks):
        normed[c, :own] = (rows[c] * inverse[0] * model_gains[0, c][None, :]).astype(bf16)

    def project(c):
        loads[c].wait()
        accumulate(projected, normed[c], held, c * cols, 0, 2 * q_width, c == 0)

    copies = gather_then(exchange, normed, project)
    cos, sin = cosine[...], signed_sine[...]
    gain_q, gain_k = gains[0:1, :], gains[1:2, :]
    scale = width ** (-0.5)
    values[...] = projected[:, q_width + kv_width :].astype(bf16)
    for seq in range(2):
        at = slice(seq * length, (seq + 1) * length)
        allowed = masks[seq] > 0.5
        for kv in range(kv_heads):
            raw_k = projected[at, q_width + kv * width : q_width + (kv + 1) * width]
            value = values[at, kv * width : (kv + 1) * width]
            _, key_rot = rotated(raw_k, gain_k, cos, sin)
            for one in range(group):
                head = slice((kv * group + one) * width, (kv * group + one + 1) * width)
                _, query_rot = rotated(projected[at, head], gain_q, cos, sin)
                weights = softmax_rows(query_rot, key_rot, allowed, scale)
                attended[at, head] = dot_nn(weights.astype(bf16), value).astype(bf16)

    def make(c):
        return dot_nt(attended[...], held[c * cols : (c + 1) * cols, 2 * q_width :])

    def finish(c, summed):
        mixed[c] = hidden[c].astype(f32) + summed

    copies += scatter_from(exchange, make, finish, keep, send_core, recv_core, send_half, recv_half)
    rows = mixed[...]
    inverse = lax.rsqrt(row_mean(rows * rows) + norm_eps)
    for c in range(chunks):
        normed_ffn_rows[c] = (rows[c] * inverse[0] * model_gains[1, c][None, :]).astype(bf16)
    for copy in copies:
        copy.wait_send()


def ffn_forward_kernel(
    hop, rows, mixed, pack, normed, gate_up, activated, result, *rest
):
    if hop:
        arrived, rest = rest[0], rest[1:]
    (
        held, total, keep, send_core, recv_core, send_half, recv_half,
        load_sems, save_sem, send_sems, recv_sems,
    ) = rest
    exchange = Exchange(send_sems, recv_sems)
    exchange.greet(hop)
    loads = load_pack(pack, held, load_sems)
    for load in loads:
        load.start()
    chunks, own, cols = rows.shape
    units = activated.shape[1]
    for c in range(chunks):
        normed[c, :own] = rows[c]

    def project(c):
        loads[c].wait()
        accumulate(total, normed[c], held, c * cols, 0, 2 * units, c == 0)

    copies = gather_then(exchange, normed, project)
    save = pltpu.make_async_copy(total, gate_up, save_sem.at[0])
    save.start()
    blk = 256

    def activate(index, _):
        at = pl.multiple_of(index * blk, blk)
        gate = total[:, pl.ds(at, blk)]
        upward = total[:, pl.ds(units + at, blk)]
        activated[:, pl.ds(at, blk)] = (gate * jax.nn.sigmoid(gate) * upward).astype(bf16)
        return 0

    lax.fori_loop(0, units // blk, activate, 0)
    hops = []

    def make(c):
        return dot_nt(activated[...], held[c * cols : (c + 1) * cols, 2 * units :])

    def finish(c, summed):
        result[c] = (mixed[c] + summed).astype(bf16)
        if hop:
            hops.append(exchange.copy(result.at[c], arrived.at[c], exchange.section, 4, c))
            hops[-1].start()

    copies += scatter_from(exchange, make, finish, keep, send_core, recv_core, send_half, recv_half)
    save.wait()
    for copy in hops:
        copy.wait()
    for copy in copies:
        copy.wait_send()


def ffn_backward_kernel(
    rows, mixed, gate_up, pack, model_gains, grad_down, grads, grad_mixed, grad_proj_rows, gain_grad,
    held, pre, total, keep, send_core, recv_core, send_half, recv_half,
    load_sems, save_sem, send_sems, recv_sems,
):
    exchange = Exchange(send_sems, recv_sems)
    exchange.greet(False)
    loads = load_pack(pack, held, load_sems)
    for load in loads:
        load.start()
    fetch = pltpu.make_async_copy(gate_up, pre, save_sem.at[0])
    fetch.start()
    chunks, own, cols = rows.shape
    units = grads.shape[1] // 2
    for c in range(chunks):
        grad_down[c, :own] = rows[c]

    def project(c):
        loads[c].wait()
        accumulate(total, grad_down[c], held, c * cols, 2 * units, units, c == 0)

    copies = gather_then(exchange, grad_down, project)
    fetch.wait()
    blk = 256

    def activate(index, _):
        at = pl.multiple_of(index * blk, blk)
        gate = pre[:, pl.ds(at, blk)]
        upward = pre[:, pl.ds(units + at, blk)]
        grad_act = total[:, pl.ds(at, blk)]
        sig = jax.nn.sigmoid(gate)
        grads[:, pl.ds(at, blk)] = (grad_act * upward * sig * (1.0 + gate * (1.0 - sig))).astype(bf16)
        grads[:, pl.ds(units + at, blk)] = (grad_act * gate * sig).astype(bf16)
        return 0

    lax.fori_loop(0, units // blk, activate, 0)

    def make(c):
        return dot_nt(grads[...], held[c * cols : (c + 1) * cols, : 2 * units])

    def finish(c, summed):
        grad_mixed[c] = summed

    copies += scatter_from(exchange, make, finish, keep, send_core, recv_core, send_half, recv_half)
    norm_step(mixed[...], grad_mixed[...], model_gains, 1, rows, grad_mixed, gain_grad)
    for c in range(chunks):
        grad_proj_rows[c] = grad_mixed[c].astype(bf16)
    for copy in copies:
        copy.wait_send()


def norm_step(values, grad_out, model_gains, which, base, out, gain_grad):
    inverse = lax.rsqrt(row_mean(values * values) + norm_eps)
    gain = jnp.concatenate([model_gains[which, c][None, None, :] for c in range(out.shape[0])], axis=0)
    scaled = grad_out * gain
    centre = row_mean(scaled * values) * inverse * inverse
    out[...] = (base[...].astype(f32) + inverse * (scaled - values * centre)).astype(out.dtype)
    for c in range(out.shape[0]):
        gain_grad[c, :] = jnp.sum(grad_out[c] * values[c] * inverse[0], axis=0)


def attn_backward_kernel(
    width, hop, rows, grad_mixed, hidden, projected, values, pack, model_gains, gains, cosine,
    signed_sine, masks, grad_proj, grads, grad_hidden, gain_grad, head_gain_grads, *rest
):
    if hop:
        arrived, rest = rest[0], rest[1:]
    (
        held, total, summed_rows, keep, send_core, recv_core, send_half, recv_half,
        load_sems, send_sems, recv_sems,
    ) = rest
    exchange = Exchange(send_sems, recv_sems)
    exchange.greet(hop)
    loads = load_pack(pack, held, load_sems)
    for load in loads:
        load.start()
    chunks, own, cols = rows.shape
    length = 2 * own
    q_width = grads.shape[1] // 2
    kv_width = q_width // 2
    kv_heads = kv_width // width
    group = q_width // kv_width
    for c in range(chunks):
        grad_proj[c, :own] = rows[c]

    def project(c):
        loads[c].wait()
        accumulate(total, grad_proj[c], held, c * cols, 2 * q_width, q_width, c == 0)

    copies = gather_then(exchange, grad_proj, project)
    cos, sin = cosine[...], signed_sine[...]
    gain_q, gain_k = gains[0:1, :], gains[1:2, :]
    scale = width ** (-0.5)
    gain_q_sum = jnp.zeros((1, width), f32)
    gain_k_sum = jnp.zeros((1, width), f32)
    for seq in range(2):
        at = slice(seq * length, (seq + 1) * length)
        allowed = masks[seq] > 0.5
        for kv in range(kv_heads):
            raw_k = projected[at, q_width + kv * width : q_width + (kv + 1) * width]
            value = values[at, kv * width : (kv + 1) * width]
            inverse_k, key_rot = rotated(raw_k, gain_k, cos, sin)
            grad_key = jnp.zeros((length, width), f32)
            grad_value = jnp.zeros((length, width), f32)
            for one in range(group):
                head = slice((kv * group + one) * width, (kv * group + one + 1) * width)
                raw_q = projected[at, head]
                grad_head = total[at, head].astype(bf16)
                inverse_q, query_rot = rotated(raw_q, gain_q, cos, sin)
                weights = softmax_rows(query_rot, key_rot, allowed, scale)
                grad_weights = dot_nt(grad_head, value)
                delta = jnp.sum(weights * grad_weights, axis=-1, keepdims=True)
                grad_scores = (weights * (grad_weights - delta)).astype(bf16)
                grad_value += dot_tn(weights.astype(bf16), grad_head)
                grad_key += dot_tn(grad_scores, query_rot)
                grad_query = dot_nn(grad_scores, key_rot) * scale
                grad_query = grad_query * cos - pltpu.roll(grad_query, 64, 1) * sin
                gain_q_sum += jnp.sum(grad_query * raw_q * inverse_q, axis=0, keepdims=True)
                grads[at, head] = norm_back(grad_query, raw_q, inverse_q, gain_q).astype(bf16)
            grad_key = grad_key * scale
            grad_key = grad_key * cos - pltpu.roll(grad_key, 64, 1) * sin
            gain_k_sum += jnp.sum(grad_key * raw_k * inverse_k, axis=0, keepdims=True)
            first = q_width + kv * width
            grads[at, first : first + width] = norm_back(grad_key, raw_k, inverse_k, gain_k).astype(bf16)
            first += kv_width
            grads[at, first : first + width] = grad_value.astype(bf16)
    head_gain_grads[...] = jnp.concatenate(
        [gain_q_sum, gain_k_sum, jnp.zeros((6, width), f32)], axis=0
    )

    def make(c):
        return dot_nt(grads[...], held[c * cols : (c + 1) * cols, : 2 * q_width])

    def finish(c, summed):
        summed_rows[c] = summed

    copies += scatter_from(exchange, make, finish, keep, send_core, recv_core, send_half, recv_half)
    norm_step(
        hidden[...].astype(f32), summed_rows[...], model_gains, 0, grad_mixed, grad_hidden, gain_grad
    )
    if hop:
        hops = [
            exchange.copy(grad_hidden.at[c], arrived.at[c], exchange.section, 4, c)
            for c in range(chunks)
        ]
        for copy in hops:
            copy.start()
        for copy in hops:
            copy.wait()
    for copy in copies:
        copy.wait_send()


def weight_grad_kernel(split, first_a, first_b, second_a, second_b, main_a, main_b, last_a, last_b, out):
    step = pl.program_id(0)

    @pl.when(step < split)
    def _():
        out[...] = (dot_nn(first_a[...], main_a[...]) + dot_nn(first_b[...], main_b[...])).astype(bf16)

    @pl.when(step >= split)
    def _():
        out[...] = (dot_nn(second_a[...], last_a[...]) + dot_nn(second_b[...], last_b[...])).astype(bf16)


VMEM_SPEC = pl.BlockSpec(memory_space=pltpu.VMEM)
ANY_SPEC = pl.BlockSpec(memory_space=pl.ANY)


def shape(dims, kind):
    return jax.ShapeDtypeStruct(dims, kind)


def exchange_scratch(chunks, own, cols):
    return [
        pltpu.VMEM((chunks, 2 * own, cols), f32),
        pltpu.VMEM((chunks, 2 * own, cols), bf16),
        pltpu.VMEM((chunks, 2 * own, cols), bf16),
        pltpu.VMEM((chunks, own, cols), bf16),
        pltpu.VMEM((chunks, own, cols), bf16),
        pltpu.SemaphoreType.DMA((4,)),
    ]


def exchange_sems(chunks):
    return [pltpu.SemaphoreType.DMA((5, chunks)), pltpu.SemaphoreType.DMA((5, chunks))]


def params(mib, number=None):
    if number is None:
        return pltpu.CompilerParams(vmem_limit_bytes=mib * MIB)
    return pltpu.CompilerParams(
        vmem_limit_bytes=mib * MIB, collective_id=number, has_side_effects=True
    )


def cost(flops, size):
    return pl.CostEstimate(flops=int(flops), bytes_accessed=int(size), transcendentals=0)


def attn_forward(hidden, pack, model_gains, gains, tables, masks):
    chunks, own, cols = hidden.shape
    tokens, q_width, width = 4 * own, pack.shape[1] // 3, gains.shape[1]
    return pl.pallas_call(
        functools.partial(attn_forward_kernel, width),
        in_specs=[VMEM_SPEC, ANY_SPEC] + [VMEM_SPEC] * 5,
        out_specs=[VMEM_SPEC] * 6,
        out_shape=[
            shape((chunks, tokens, cols), bf16),
            shape((tokens, 2 * q_width), f32),
            shape((tokens, q_width // 2), bf16),
            shape((tokens, q_width), bf16),
            shape((chunks, own, cols), f32),
            shape((chunks, own, cols), bf16),
        ],
        scratch_shapes=[pltpu.VMEM(pack.shape, bf16)]
        + exchange_scratch(chunks, own, cols)
        + exchange_sems(chunks),
        compiler_params=params(40, 0),
        cost_estimate=cost(2 * tokens * pack.size, pack.size * 2),
        name="attn_forward",
    )(hidden, pack, model_gains, gains, *tables, masks)


def ffn_forward(rows, mixed, pack, hop):
    chunks, own, cols = rows.shape
    tokens, units = 4 * own, pack.shape[1] // 3
    scratch = exchange_scratch(chunks, own, cols)
    return pl.pallas_call(
        functools.partial(ffn_forward_kernel, hop),
        in_specs=[VMEM_SPEC, VMEM_SPEC, ANY_SPEC],
        out_specs=[VMEM_SPEC, ANY_SPEC] + [VMEM_SPEC] * (3 if hop else 2),
        out_shape=[
            shape((chunks, tokens, cols), bf16),
            shape((tokens, 2 * units), f32),
            shape((tokens, units), bf16),
        ]
        + [shape((chunks, own, cols), bf16)] * (2 if hop else 1),
        scratch_shapes=[pltpu.VMEM(pack.shape, bf16), pltpu.VMEM((tokens, 2 * units), f32)]
        + scratch
        + [pltpu.SemaphoreType.DMA((1,))]
        + exchange_sems(chunks),
        compiler_params=params(52, 1 if hop else 2),
        cost_estimate=cost(2 * tokens * pack.size, pack.size * 2),
        name="ffn_forward",
    )(rows, mixed, pack)


def ffn_backward(rows, mixed, gate_up, pack, model_gains):
    chunks, own, cols = rows.shape
    tokens, units = 4 * own, pack.shape[1] // 3
    return pl.pallas_call(
        ffn_backward_kernel,
        in_specs=[VMEM_SPEC, VMEM_SPEC, ANY_SPEC, ANY_SPEC, VMEM_SPEC],
        out_specs=[VMEM_SPEC] * 5,
        out_shape=[
            shape((chunks, tokens, cols), bf16),
            shape((tokens, 2 * units), bf16),
            shape((chunks, own, cols), f32),
            shape((chunks, own, cols), bf16),
            shape((chunks, cols), f32),
        ],
        scratch_shapes=[
            pltpu.VMEM(pack.shape, bf16),
            pltpu.VMEM((tokens, 2 * units), f32),
            pltpu.VMEM((tokens, units), f32),
        ]
        + exchange_scratch(chunks, own, cols)
        + [pltpu.SemaphoreType.DMA((1,))]
        + exchange_sems(chunks),
        compiler_params=params(56, 3),
        cost_estimate=cost(2 * tokens * pack.size, pack.size * 2),
        name="ffn_backward",
    )(rows, mixed, gate_up, pack, model_gains)


def attn_backward(
    rows, grad_mixed, hidden, projected, values, pack, model_gains, gains, tables, masks, hop
):
    chunks, own, cols = rows.shape
    tokens, q_width, width = 4 * own, pack.shape[1] // 3, gains.shape[1]
    return pl.pallas_call(
        functools.partial(attn_backward_kernel, width, hop),
        in_specs=[VMEM_SPEC] * 5 + [ANY_SPEC] + [VMEM_SPEC] * 5,
        out_specs=[VMEM_SPEC] * (6 if hop else 5),
        out_shape=[
            shape((chunks, tokens, cols), bf16),
            shape((tokens, 2 * q_width), bf16),
            shape((chunks, own, cols), bf16),
            shape((chunks, cols), f32),
            shape((8, width), f32),
        ]
        + [shape((chunks, own, cols), bf16)] * (1 if hop else 0),
        scratch_shapes=[
            pltpu.VMEM(pack.shape, bf16),
            pltpu.VMEM((tokens, q_width), f32),
            pltpu.VMEM((chunks, own, cols), f32),
        ]
        + exchange_scratch(chunks, own, cols)
        + exchange_sems(chunks),
        compiler_params=params(40, 4 if hop else 5),
        cost_estimate=cost(2 * tokens * pack.size, pack.size * 2),
        name="attn_backward",
    )(rows, grad_mixed, hidden, projected, values, pack, model_gains, gains, *tables, masks)


def weight_grad(first, second, main, last):
    depth, tokens = first[0].shape
    blk = 512
    split, rest = main[0].shape[1] // blk, last[0].shape[1] // blk
    turned = pl.BlockSpec((depth, tokens), lambda step: (0, 0))
    main_spec = pl.BlockSpec((tokens, blk), lambda step: (0, jnp.minimum(step, split - 1)))
    last_spec = pl.BlockSpec((tokens, blk), lambda step: (0, jnp.maximum(step - split, 0)))
    width = (split + rest) * blk
    return pl.pallas_call(
        functools.partial(weight_grad_kernel, split),
        grid=(split + rest,),
        in_specs=[turned] * 4 + [main_spec] * 2 + [last_spec] * 2,
        out_specs=pl.BlockSpec((depth, blk), lambda step: (0, step)),
        out_shape=shape((depth, width), bf16),
        compiler_params=params(40),
        cost_estimate=cost(4 * depth * tokens * width, 2 * depth * width),
        name="weight_grad",
    )(*first, *second, *main, *last)


def rope_tables(position, head_width):
    exponent = jnp.arange(0, head_width, 2).astype(f32) / head_width
    inverse = rope_base ** (-exponent)
    angles = position.astype(f32)[:, None] * inverse[None, :]
    cosine, sine = jnp.cos(angles), jnp.sin(angles)
    return (
        jnp.concatenate([cosine, cosine], axis=-1),
        jnp.concatenate([-sine, sine], axis=-1),
    )


def per_device(
    block_input,
    segment_ids,
    out_cotangent,
    attn_norm,
    q_weight,
    k_weight,
    v_weight,
    o_weight,
    q_norm,
    k_norm,
    ffn_norm,
    gate_weight,
    up_weight,
    down_weight,
):
    section = lax.axis_index("section")
    place = lax.axis_index("dp")
    core = place % 2
    half = lax.axis_index("tensor")
    n_dp = lax.axis_size("dp")
    n_chip = n_dp // 2
    micro_count, own_rows, depth = block_input.shape
    length = 2 * own_rows
    head_width = q_norm.shape[1]
    first_core = core == 0
    swap_core = [(i, i ^ 1) for i in range(n_dp)]
    swap_half = [(0, 1), (1, 0)]
    chip_groups = [[2 * chip + one for chip in range(n_chip)] for one in (0, 1)]

    def to_core(values):
        return lax.ppermute(values, "dp", swap_core)

    def to_half(values):
        return lax.ppermute(values, "tensor", swap_half)

    def split_columns(weight):
        side = weight.shape[1] // 2
        left, right = weight[:, :side], weight[:, side:]
        return jnp.where(first_core, left, right), jnp.where(first_core, right, left)

    def split_rows(weight):
        side = weight.shape[0] // 2
        left, right = weight[:side].T, weight[side:].T
        return jnp.where(first_core, left, right), jnp.where(first_core, right, left)

    def gathered(pairs):
        mine = jnp.concatenate([pair[0] for pair in pairs], axis=1)
        theirs = to_core(jnp.concatenate([pair[1] for pair in pairs], axis=1))
        chip_block = jnp.concatenate(
            [jnp.where(first_core, mine, theirs), jnp.where(first_core, theirs, mine)], axis=0
        )
        return lax.all_gather(
            chip_block, "dp", axis=0, tiled=True, axis_index_groups=chip_groups
        )

    attn_pack = gathered(
        [
            split_columns(q_weight[0]),
            split_columns(k_weight[0]),
            split_columns(v_weight[0]),
            split_rows(o_weight[0]),
        ]
    )
    ffn_pack = gathered(
        [split_columns(gate_weight[0]), split_columns(up_weight[0]), split_rows(down_weight[0])]
    )

    cols = depth // row_chunks
    model_gains = jnp.concatenate([attn_norm, ffn_norm], axis=0).reshape(2, row_chunks, cols)
    head_gains = jnp.concatenate([q_norm, k_norm, jnp.zeros((6, head_width), f32)], axis=0)

    def chunked(rows):
        return rows.reshape(rows.shape[0], row_chunks, cols).transpose(1, 0, 2)

    def joined(rows):
        return rows.transpose(1, 0, 2).reshape(rows.shape[1], depth)

    def turned(rows):
        return rows.transpose(0, 2, 1).reshape(depth, rows.shape[1])

    inputs = [chunked(block_input[micro]) for micro in range(2)]
    cotangents = [chunked(out_cotangent[micro]) for micro in range(2)]

    def arranged(values):
        sides = values[..., :own_rows], values[..., own_rows:]
        return jnp.concatenate(
            [jnp.where(half == 0, *sides), jnp.where(half == 0, *sides[::-1])], axis=-1
        )

    position = arranged(jnp.arange(length, dtype=jnp.int32))
    tables = rope_tables(position, head_width)
    ids = arranged(jnp.stack([segment_ids, to_core(segment_ids)], axis=1))
    causal = position[:, None] >= position[None, :]
    masks = (causal & (ids[..., :, None] == ids[..., None, :])).astype(f32)

    at_first = section == 0

    def pick(first, second):
        return jax.tree.map(lambda a, b: jnp.where(at_first, a, b), first, second)

    zero_rows = jnp.zeros_like(inputs[0])
    forward_masks = [masks[0], pick(masks[1], masks[0]), masks[1]]
    results, backs, saves, arrived = [], [], [], zero_rows
    for step in range(3):
        hidden = inputs[step] if step < 2 else zero_rows
        if step > 0:
            hidden = pick(hidden, arrived)
        normed, projected, values, attended, mixed, rows = attn_forward(
            hidden, attn_pack, model_gains, head_gains, tables, forward_masks[step]
        )
        normed_ffn, gate_up, activated, result, *rest = ffn_forward(rows, mixed, ffn_pack, step < 2)
        arrived = rest[0] if rest else None
        results.append(result)
        backs.append((hidden, projected, values, mixed, gate_up))
        saves.append((normed, attended, normed_ffn, activated))
    def forward_pair(item):
        return [pick(saves[micro][item], saves[micro + 1][item]) for micro in range(2)]

    def backward_pair(table, item):
        return [pick(table[micro + 1][item], table[micro][item]) for micro in range(2)]

    def turned_pair(pair):
        return [turned(rows) for rows in pair]

    backward_masks = [masks[0], pick(masks[0], masks[1]), masks[1]]
    grads, ffn_saves, attn_saves, gain_total, arrived = [], [], [], None, zero_rows
    for step in range(3):
        rows = pick(arrived, cotangents[step] if step < 2 else zero_rows)
        back = pick(backs[0], backs[2]) if step == 1 else backs[1]
        hidden, projected, values, mixed, gate_up = back
        grad_down, ffn_grads, grad_mixed, proj_rows, ffn_gain_grad = ffn_backward(
            rows, mixed, gate_up, ffn_pack, model_gains
        )
        ffn_saves.append((grad_down, ffn_grads))
        if step == 2:
            ffn_partial = weight_grad(
                turned_pair(forward_pair(2)),
                turned_pair(backward_pair(ffn_saves, 0)),
                backward_pair(ffn_saves, 1),
                forward_pair(3),
            )
            proj_rows, ffn_partial = lax.optimization_barrier((proj_rows, ffn_partial))
        grad_proj, attn_grads, grad_hidden, attn_gain_grad, head_gain_grads, *rest = attn_backward(
            proj_rows, grad_mixed, hidden, projected, values, attn_pack, model_gains, head_gains,
            tables, backward_masks[step], step < 2,
        )
        arrived = rest[0] if rest else None
        grads.append(grad_hidden)
        attn_saves.append((grad_proj, attn_grads))
        gains = (attn_gain_grad, ffn_gain_grad, head_gain_grads)
        gain_total = gains if gain_total is None else jax.tree.map(jnp.add, gain_total, gains)

    section_outputs = jnp.stack(
        [joined(pick(results[micro], results[micro + 1])) for micro in range(2)]
    )[None]
    section_input_grads = jnp.stack(
        [joined(pick(grads[micro + 1], grads[micro])) for micro in range(2)]
    )[None]

    def scattered(partial):
        return lax.psum_scatter(
            partial, "dp", scatter_dimension=0, tiled=True, axis_index_groups=chip_groups
        )

    def owned(rows):
        side = rows.shape[0] // 2
        own = jnp.where(first_core, rows[:side], rows[side:])
        other = to_core(jnp.where(first_core, rows[side:], rows[:side]))
        return (
            jnp.where(first_core, own, other).astype(f32),
            jnp.where(first_core, other, own).astype(f32),
        )

    attn_partial = weight_grad(
        turned_pair(forward_pair(0)),
        turned_pair(backward_pair(attn_saves, 0)),
        backward_pair(attn_saves, 1),
        forward_pair(1),
    )
    attn_partial, ffn_rows = lax.optimization_barrier((attn_partial, scattered(ffn_partial)))
    ffn_sides = owned(ffn_rows)
    attn_sides = owned(scattered(attn_partial))
    units = gate_weight.shape[2] // 2
    q_width = q_weight.shape[2] // 2
    kv_width = k_weight.shape[2] // 2

    def across(sides, first, width):
        return jnp.concatenate([side[:, first : first + width] for side in sides], axis=1)[None]

    def down(sides, first):
        return jnp.concatenate([side[:, first:].T for side in sides], axis=0)[None]

    packed = jnp.concatenate(
        [
            gain_total[0].reshape(-1),
            gain_total[1].reshape(-1),
            gain_total[2][0],
            gain_total[2][1],
        ]
    ).reshape(-1, head_width)
    packed = packed + to_core(packed)
    packed = packed + to_half(packed)
    reach = 2
    while reach < n_dp:
        packed = packed + lax.ppermute(packed, "dp", [(i, i ^ reach) for i in range(n_dp)])
        reach *= 2
    packed = packed.reshape(-1)
    return (
        section_outputs,
        section_input_grads,
        packed[None, :depth],
        across(attn_sides, 0, q_width),
        across(attn_sides, q_width, kv_width),
        across(attn_sides, q_width + kv_width, kv_width),
        down(attn_sides, 2 * q_width),
        packed[None, 2 * depth : 2 * depth + head_width],
        packed[None, 2 * depth + head_width :],
        packed[None, depth : 2 * depth],
        across(ffn_sides, 0, units),
        across(ffn_sides, units, units),
        down(ffn_sides, 2 * units),
    )


def solution(mesh):
    rows = P(None, ("dp", "tensor"), None)
    out_rows = P("section", None, ("dp", "tensor"), None)
    gain = P("section", None)
    wide = P("section", "dp", "tensor")
    tall = P("section", "tensor", "dp")
    return jax.shard_map(
        per_device,
        mesh=mesh,
        in_specs=(
            rows, P(None, "dp"), rows, gain, wide, wide, wide, tall, gain, gain, gain, wide, wide, tall,
        ),
        out_specs=(
            out_rows, out_rows, gain, wide, wide, wide, tall, gain, gain, gain, wide, wide, tall,
        ),
        check_vma=False,
    )
```

```python
import functools

import jax
import jax.numpy as jnp
from jax import lax
from jax.experimental import pallas as pl
from jax.experimental.pallas import tpu as pltpu
from jax.sharding import PartitionSpec as P

norm_eps = 1e-06
rope_base = 1000000.0
masked_score = -1e30
row_chunks = 4
f32 = jnp.float32
bf16 = jnp.bfloat16
MIB = 1024 * 1024
MESH = pl.DeviceIdType.MESH


def dot_nn(left, right):
    return lax.dot_general(left, right, (((1,), (0,)), ((), ())), preferred_element_type=f32)


def dot_nt(left, right):
    return lax.dot_general(left, right, (((1,), (1,)), ((), ())), preferred_element_type=f32)


def dot_tn(left, right):
    return lax.dot_general(left, right, (((0,), (0,)), ((), ())), preferred_element_type=f32)


def inverse_rms(values):
    return lax.rsqrt(jnp.mean(values * values, axis=-1, keepdims=True) + norm_eps)


def norm_back(grad_out, values, inverse, gain_vec):
    scaled = grad_out * gain_vec
    return inverse * (
        scaled - values * inverse * inverse * jnp.mean(scaled * values, axis=-1, keepdims=True)
    )


class Exchange:
    def __init__(self, send_sems, recv_sems):
        place = lax.axis_index("dp")
        self.core = {"dp": place + 1 - 2 * (place % 2)}
        self.half = {"tensor": 1 - lax.axis_index("tensor")}
        self.section = {"section": 1 - lax.axis_index("section")}
        core, chip = place % 2, place // 2
        across, along = chip % 2, chip // 2
        self.chip = chip
        numbers = (chip + 1 - 2 * across, chip + 2 - 4 * along, 3 - chip)
        self.chips = [(number, {"dp": 2 * number + core}) for number in numbers]
        self.send_sems, self.recv_sems = send_sems, recv_sems

    def greet(self, with_section, with_chips=False):
        others = [self.core, self.half] + ([self.section] if with_section else [])
        self.meet(others + ([device for _, device in self.chips] if with_chips else []))

    def meet(self, others):
        barrier = pltpu.get_barrier_semaphore()
        for other in others:
            pl.semaphore_signal(barrier, inc=1, device_id=other, device_id_type=MESH)
        pl.semaphore_wait(barrier, len(others))

    def copy(self, source, target, other, stage, chunk):
        return pltpu.make_async_remote_copy(
            src_ref=source,
            dst_ref=target,
            send_sem=self.send_sems.at[stage, chunk],
            recv_sem=self.recv_sems.at[stage, chunk],
            device_id=other,
            device_id_type=MESH,
        )


def gather_then(exchange, rows, use):
    chunks, total, _ = rows.shape
    own = total // 4
    first = [
        exchange.copy(rows.at[c, pl.ds(0, own)], rows.at[c, pl.ds(own, own)], exchange.half, 0, c)
        for c in range(chunks)
    ]
    second = [
        exchange.copy(
            rows.at[c, pl.ds(0, 2 * own)], rows.at[c, pl.ds(2 * own, 2 * own)], exchange.core, 1, c
        )
        for c in range(chunks)
    ]
    for c in range(chunks):
        first[c].start()
    for c in range(chunks):
        first[c].wait_recv()
        second[c].start()
        if c > 0:
            second[c - 1].wait_recv()
            use(c - 1)
    second[chunks - 1].wait_recv()
    use(chunks - 1)
    return first + second


def scatter_from(exchange, make, idle, finish, keep, send_core, recv_core, send_half, recv_half):
    chunks, pair, _ = keep.shape
    own = pair // 2
    first = [
        exchange.copy(send_core.at[c], recv_core.at[c], exchange.core, 2, c) for c in range(chunks)
    ]
    second = [
        exchange.copy(send_half.at[c], recv_half.at[c], exchange.half, 3, c) for c in range(chunks)
    ]

    def middle(c):
        first[c].wait_recv()
        summed = keep[c] + recv_core[c].astype(f32)
        send_half[c] = summed[own:].astype(bf16)
        second[c].start()
        keep[c, :own] = summed[:own]

    for c in range(chunks):
        product = make(c)
        send_core[c] = product[pair:].astype(bf16)
        first[c].start()
        keep[c] = product[:pair]
        if c > 0:
            middle(c - 1)
    middle(chunks - 1)
    for c in range(chunks):
        idle(c)
        second[c].wait_recv()
        finish(c, keep[c, :own] + recv_half[c].astype(f32))
    return first + second


def chip_gather_kernel(block, out, local_sems, send_sems, recv_sems):
    exchange, local = Exchange(send_sems, recv_sems), Local(local_sems)
    (across, across_device), (along, along_device), _ = exchange.chips
    exchange.meet([across_device, along_device])
    half = block.shape[0] // 2
    first, last = pl.ds(0, half), pl.ds(half, half)
    target = out.at[exchange.chip]
    direct = [
        exchange.copy(block, target, across_device, 0, 0),
        exchange.copy(block, target, along_device, 0, 1),
    ]
    for copy in direct:
        copy.start()
    local.save(block, target)
    passed = [
        exchange.copy(out.at[across, first], out.at[across, first], along_device, 0, 2),
        exchange.copy(out.at[along, last], out.at[along, last], across_device, 0, 3),
    ]
    for copy, onward in zip(direct, passed):
        copy.wait_recv()
        onward.start()
    for copy in passed:
        copy.wait_recv()
    for copy in direct + passed:
        copy.wait_send()
    local.finish()


def chip_gather(block):
    return pl.pallas_call(
        chip_gather_kernel,
        in_specs=[HBM_SPEC],
        out_specs=HBM_SPEC,
        out_shape=shape((4,) + block.shape, bf16),
        scratch_shapes=[
            pltpu.SemaphoreType.DMA((1,)),
            pltpu.SemaphoreType.DMA((1, 4)),
            pltpu.SemaphoreType.DMA((1, 4)),
        ],
        compiler_params=params(6),
        cost_estimate=cost(0, 300 * block.size),
        name="chip_gather",
    )(block)


def load_pack(pack, held, local):
    depth = held.shape[0] // row_chunks
    return [
        local.load(pack.at[pl.ds(c * depth, depth)], held.at[pl.ds(c * depth, depth)])
        for c in range(row_chunks)
    ]


class Local:
    def __init__(self, sems):
        self.sems, self.used, self.saves = sems, 0, []

    def copy(self, source, target):
        self.used += 1
        return pltpu.make_async_copy(source, target, self.sems.at[self.used - 1])

    def load(self, source, target):
        copy = self.copy(source, target)
        copy.start()
        return copy

    def load_either(self, at_first, first, second, target):
        one = self.copy(first, target)
        other = pltpu.make_async_copy(second, target, self.sems.at[self.used - 1])

        @pl.when(at_first)
        def _():
            one.start()

        @pl.when(jnp.logical_not(at_first))
        def _():
            other.start()

        return one

    def save(self, source, target):
        self.saves.append(self.load(source, target))

    def finish(self):
        for copy in self.saves:
            copy.wait()


def row_mean(values):
    size = values.shape[0] * values.shape[2]
    return jnp.sum(jnp.sum(values, axis=0), axis=-1, keepdims=True)[None] * (1.0 / size)


def accumulate(total, left, weights, first_row, first_col, width, start):
    depth = left.shape[1]
    blk = 512 if width % 512 == 0 else 256

    def body(index, _):
        at = pl.multiple_of(index * blk, blk)
        product = dot_nn(left, weights[pl.ds(first_row, depth), pl.ds(first_col + at, blk)])
        if start:
            total[:, pl.ds(at, blk)] = product
        else:
            total[:, pl.ds(at, blk)] += product
        return 0

    lax.fori_loop(0, width // blk, body, 0)


def rotated(raw, gain, cosine, signed_sine):
    inverse = inverse_rms(raw)
    scaled = raw * inverse * gain
    turned = scaled * cosine + pltpu.roll(scaled, 64, 1) * signed_sine
    return inverse, turned.astype(bf16)


def softmax_rows(query_rot, key_rot, allowed, scale):
    scores = jnp.where(allowed, dot_nt(query_rot, key_rot) * scale, masked_score)
    exponent = jnp.exp(scores - jnp.max(scores, axis=-1, keepdims=True))
    return exponent / jnp.sum(exponent, axis=-1, keepdims=True)


def turn_chunk(rows, target, c):
    cols = rows.shape[2]
    target[pl.ds(c * cols, cols), :] = rows[c].T


def attn_forward_kernel(
    width, carry, *refs
):
    if carry:
        carried, refs = refs[0], refs[1:]
    (
        hidden, pack, model_gains, gains, tables_in, masks_in,
        turned_out, projected_out, values_out, attended_out, mixed_out, normed_ffn_rows,
    ), refs = refs[:12], refs[12:]
    if carry:
        arrived, refs = refs[0], refs[1:]
    (
        tables, masks, normed, turned, projected, values, attended, mixed,
        held, keep, send_core, recv_core, send_half, recv_half, local_sems, send_sems, recv_sems,
    ) = refs
    exchange, local = Exchange(send_sems, recv_sems), Local(local_sems)
    exchange.greet(carry)
    loads = load_pack(pack, held, local)
    extra = [local.load(tables_in, tables), local.load(masks_in, masks)]
    chunks, own, cols = hidden.shape
    length = 2 * own
    q_width = attended.shape[1]
    kv_width = q_width // 2
    kv_heads = kv_width // width
    group = q_width // kv_width
    rows = hidden[...].astype(f32)
    inverse = lax.rsqrt(row_mean(rows * rows) + norm_eps)
    for c in range(chunks):
        normed[c, :own] = (rows[c] * inverse[0] * model_gains[0, c][None, :]).astype(bf16)

    def project(c):
        loads[c].wait()
        accumulate(projected, normed[c], held, c * cols, 0, 2 * q_width, c == 0)

    copies = gather_then(exchange, normed, project)
    hops = []
    if carry:
        hops = [exchange.copy(carried, arrived, exchange.section, 4, 0)]
        hops[0].start()
    local.save(projected, projected_out)
    for load in extra:
        load.wait()
    cos, sin = tables[0], tables[1]
    gain_q, gain_k = gains[0:1, :], gains[1:2, :]
    scale = width ** (-0.5)
    values[...] = projected[:, q_width + kv_width :].astype(bf16)
    local.save(values, values_out)
    for seq in range(2):
        at = slice(seq * length, (seq + 1) * length)
        allowed = masks[seq] > 0.5
        for kv in range(kv_heads):
            raw_k = projected[at, q_width + kv * width : q_width + (kv + 1) * width]
            value = values[at, kv * width : (kv + 1) * width]
            _, key_rot = rotated(raw_k, gain_k, cos, sin)
            for one in range(group):
                head = slice((kv * group + one) * width, (kv * group + one + 1) * width)
                _, query_rot = rotated(projected[at, head], gain_q, cos, sin)
                weights = softmax_rows(query_rot, key_rot, allowed, scale)
                attended[at, head] = dot_nn(weights.astype(bf16), value).astype(bf16)
    local.save(attended, attended_out)

    def make(c):
        return dot_nt(attended[...], held[c * cols : (c + 1) * cols, 2 * q_width :])

    def idle(c):
        turn_chunk(normed, turned, c)

    def finish(c, summed):
        mixed[c] = hidden[c].astype(f32) + summed

    copies += scatter_from(
        exchange, make, idle, finish, keep, send_core, recv_core, send_half, recv_half
    )
    local.save(turned, turned_out)
    local.save(mixed, mixed_out)
    rows = mixed[...]
    inverse = lax.rsqrt(row_mean(rows * rows) + norm_eps)
    for c in range(chunks):
        normed_ffn_rows[c] = (rows[c] * inverse[0] * model_gains[1, c][None, :]).astype(bf16)
    for copy in hops:
        copy.wait()
    for copy in copies:
        copy.wait_send()
    local.finish()


def ffn_forward_kernel(
    hop, rows, mixed_in, pack, turned_out, gate_up_out, activated_out, result, *rest
):
    if hop:
        arrived, rest = rest[0], rest[1:]
    (
        normed, turned, mixed, activated, total,
        held, keep, send_core, recv_core, send_half, recv_half, local_sems, send_sems, recv_sems,
    ) = rest
    exchange, local = Exchange(send_sems, recv_sems), Local(local_sems)
    exchange.greet(hop)
    loads = load_pack(pack, held, local)
    mixed_load = local.load(mixed_in, mixed)
    chunks, own, cols = rows.shape
    units = activated.shape[1]
    for c in range(chunks):
        normed[c, :own] = rows[c]

    def project(c):
        loads[c].wait()
        accumulate(total, normed[c], held, c * cols, 0, 2 * units, c == 0)

    copies = gather_then(exchange, normed, project)
    local.save(total, gate_up_out)
    blk = 256

    def activate(index, _):
        at = pl.multiple_of(index * blk, blk)
        gate = total[:, pl.ds(at, blk)]
        upward = total[:, pl.ds(units + at, blk)]
        activated[:, pl.ds(at, blk)] = (gate * jax.nn.sigmoid(gate) * upward).astype(bf16)
        return 0

    lax.fori_loop(0, units // blk, activate, 0)
    local.save(activated, activated_out)
    mixed_load.wait()
    hops = []

    def make(c):
        return dot_nt(activated[...], held[c * cols : (c + 1) * cols, 2 * units :])

    def idle(c):
        turn_chunk(normed, turned, c)

    def finish(c, summed):
        result[c] = (mixed[c] + summed).astype(bf16)
        if hop:
            hops.append(exchange.copy(result.at[c], arrived.at[c], exchange.section, 4, c))
            hops[-1].start()

    copies += scatter_from(
        exchange, make, idle, finish, keep, send_core, recv_core, send_half, recv_half
    )
    local.save(turned, turned_out)
    for copy in hops:
        copy.wait()
    for copy in copies:
        copy.wait_send()
    local.finish()


def ffn_backward_kernel(spread, carry, *refs):
    if carry:
        carried, refs = refs[0], refs[1:]
    (
        rows, mixed_a, mixed_b, gate_up_a, gate_up_b, pack, model_gains,
        moved_out, grads_out, grad_mixed, grad_proj_rows, gain_grad,
    ), refs = refs[:12], refs[12:]
    if carry:
        arrived, refs = refs[0], refs[1:]
    (
        grad_down, moved, mixed, grads, pre, total,
        held, keep, send_core, recv_core, send_half, recv_half, local_sems, send_sems, recv_sems,
    ) = refs
    exchange, local = Exchange(send_sems, recv_sems), Local(local_sems)
    exchange.greet(carry, spread)
    at_first = lax.axis_index("section") == 0
    loads = load_pack(pack, held, local)
    pre_load = local.load_either(at_first, gate_up_a, gate_up_b, pre)
    mixed_load = local.load_either(at_first, mixed_a, mixed_b, mixed)
    chunks, own, cols = rows.shape
    units = grads.shape[1] // 2
    for c in range(chunks):
        grad_down[c, :own] = rows[c]

    def project(c):
        loads[c].wait()
        accumulate(total, grad_down[c], held, c * cols, 2 * units, units, c == 0)

    copies = gather_then(exchange, grad_down, project)
    hops = []
    if carry:
        hops = [exchange.copy(carried, arrived, exchange.section, 4, 0)]
        hops[0].start()
    side = 2 * own
    arrivals, onward = [], []
    if spread:
        for index, (number, device) in enumerate(exchange.chips):
            arrivals.append(
                exchange.copy(
                    grad_down.at[number, pl.ds(0, side)],
                    moved.at[exchange.chip, pl.ds(0, side)],
                    device, 5, index,
                )
            )
            arrivals[-1].start()
            onward.append(
                exchange.copy(
                    moved.at[number, pl.ds(0, side)],
                    moved.at[number, pl.ds(side, side)],
                    exchange.core, 6, index,
                )
            )
        moved[exchange.chip] = grad_down[exchange.chip]
    pre_load.wait()
    blk = 256

    def activate(index, _):
        at = pl.multiple_of(index * blk, blk)
        gate = pre[:, pl.ds(at, blk)]
        upward = pre[:, pl.ds(units + at, blk)]
        grad_act = total[:, pl.ds(at, blk)]
        sig = jax.nn.sigmoid(gate)
        grads[:, pl.ds(at, blk)] = (grad_act * upward * sig * (1.0 + gate * (1.0 - sig))).astype(bf16)
        grads[:, pl.ds(units + at, blk)] = (grad_act * gate * sig).astype(bf16)
        return 0

    lax.fori_loop(0, units // blk, activate, 0)
    local.save(grads, grads_out)

    def make(c):
        return dot_nt(grads[...], held[c * cols : (c + 1) * cols, : 2 * units])

    def idle(c):
        if not spread:
            turn_chunk(grad_down, moved, c)
        elif c > 0:
            arrivals[c - 1].wait_recv()
            onward[c - 1].start()

    def finish(c, summed):
        grad_mixed[c] = summed

    copies += scatter_from(
        exchange, make, idle, finish, keep, send_core, recv_core, send_half, recv_half
    )
    for copy in onward:
        copy.wait_recv()
    copies += arrivals + onward
    local.save(moved, moved_out)
    mixed_load.wait()
    norm_step(mixed[...], grad_mixed[...], model_gains, 1, rows, grad_mixed, gain_grad)
    for c in range(chunks):
        grad_proj_rows[c] = grad_mixed[c].astype(bf16)
    for copy in hops:
        copy.wait()
    for copy in copies:
        copy.wait_send()
    local.finish()


def norm_step(values, grad_out, model_gains, which, base, out, gain_grad):
    inverse = lax.rsqrt(row_mean(values * values) + norm_eps)
    gain = jnp.concatenate([model_gains[which, c][None, None, :] for c in range(out.shape[0])], axis=0)
    scaled = grad_out * gain
    centre = row_mean(scaled * values) * inverse * inverse
    out[...] = (base[...].astype(f32) + inverse * (scaled - values * centre)).astype(out.dtype)
    for c in range(out.shape[0]):
        gain_grad[c, :] = jnp.sum(grad_out[c] * values[c] * inverse[0], axis=0)


def attn_backward_kernel(
    width, hop, rows, grad_mixed, hidden_a, hidden_b, projected_a, projected_b, values_a, values_b,
    pack, model_gains, gains, tables_in, masks_in,
    turned_out, grads_out, grad_hidden, gain_grad, head_gain_grads, *rest
):
    if hop:
        arrived, rest = rest[0], rest[1:]
    (
        tables, masks, grad_proj, turned, grads, hidden, projected, values, total, summed_rows,
        held, keep, send_core, recv_core, send_half, recv_half, local_sems, send_sems, recv_sems,
    ) = rest
    exchange, local = Exchange(send_sems, recv_sems), Local(local_sems)
    exchange.greet(hop)
    at_first = lax.axis_index("section") == 0
    loads = load_pack(pack, held, local)
    extra = [local.load(tables_in, tables), local.load(masks_in, masks)]
    projected_load = local.load_either(at_first, projected_a, projected_b, projected)
    values_load = local.load_either(at_first, values_a, values_b, values)
    hidden_load = local.load_either(at_first, hidden_a, hidden_b, hidden)
    chunks, own, cols = rows.shape
    length = 2 * own
    q_width = grads.shape[1] // 2
    kv_width = q_width // 2
    kv_heads = kv_width // width
    group = q_width // kv_width
    for c in range(chunks):
        grad_proj[c, :own] = rows[c]

    def project(c):
        loads[c].wait()
        accumulate(total, grad_proj[c], held, c * cols, 2 * q_width, q_width, c == 0)

    copies = gather_then(exchange, grad_proj, project)
    projected_load.wait()
    values_load.wait()
    for load in extra:
        load.wait()
    cos, sin = tables[0], tables[1]
    gain_q, gain_k = gains[0:1, :], gains[1:2, :]
    scale = width ** (-0.5)
    gain_q_sum = jnp.zeros((1, width), f32)
    gain_k_sum = jnp.zeros((1, width), f32)
    for seq in range(2):
        at = slice(seq * length, (seq + 1) * length)
        allowed = masks[seq] > 0.5
        for kv in range(kv_heads):
            raw_k = projected[at, q_width + kv * width : q_width + (kv + 1) * width]
            value = values[at, kv * width : (kv + 1) * width]
            inverse_k, key_rot = rotated(raw_k, gain_k, cos, sin)
            grad_key = jnp.zeros((length, width), f32)
            grad_value = jnp.zeros((length, width), f32)
            for one in range(group):
                head = slice((kv * group + one) * width, (kv * group + one + 1) * width)
                raw_q = projected[at, head]
                grad_head = total[at, head].astype(bf16)
                inverse_q, query_rot = rotated(raw_q, gain_q, cos, sin)
                weights = softmax_rows(query_rot, key_rot, allowed, scale)
                grad_weights = dot_nt(grad_head, value)
                delta = jnp.sum(weights * grad_weights, axis=-1, keepdims=True)
                grad_scores = (weights * (grad_weights - delta)).astype(bf16)
                grad_value += dot_tn(weights.astype(bf16), grad_head)
                grad_key += dot_tn(grad_scores, query_rot)
                grad_query = dot_nn(grad_scores, key_rot) * scale
                grad_query = grad_query * cos - pltpu.roll(grad_query, 64, 1) * sin
                gain_q_sum += jnp.sum(grad_query * raw_q * inverse_q, axis=0, keepdims=True)
                grads[at, head] = norm_back(grad_query, raw_q, inverse_q, gain_q).astype(bf16)
            grad_key = grad_key * scale
            grad_key = grad_key * cos - pltpu.roll(grad_key, 64, 1) * sin
            gain_k_sum += jnp.sum(grad_key * raw_k * inverse_k, axis=0, keepdims=True)
            first = q_width + kv * width
            grads[at, first : first + width] = norm_back(grad_key, raw_k, inverse_k, gain_k).astype(bf16)
            first += kv_width
            grads[at, first : first + width] = grad_value.astype(bf16)
    local.save(grads, grads_out)
    head_gain_grads[...] = jnp.concatenate(
        [gain_q_sum, gain_k_sum, jnp.zeros((6, width), f32)], axis=0
    )

    def make(c):
        return dot_nt(grads[...], held[c * cols : (c + 1) * cols, : 2 * q_width])

    def idle(c):
        turn_chunk(grad_proj, turned, c)

    def finish(c, summed):
        summed_rows[c] = summed

    copies += scatter_from(
        exchange, make, idle, finish, keep, send_core, recv_core, send_half, recv_half
    )
    local.save(turned, turned_out)
    hidden_load.wait()
    norm_step(
        hidden[...].astype(f32), summed_rows[...], model_gains, 0, grad_mixed, grad_hidden, gain_grad
    )
    if hop:
        hops = [
            exchange.copy(grad_hidden.at[c], arrived.at[c], exchange.section, 4, c)
            for c in range(chunks)
        ]
        for copy in hops:
            copy.start()
        for copy in hops:
            copy.wait()
    for copy in copies:
        copy.wait_send()
    local.finish()


def weight_grad_kernel(blk, sides, *refs):
    lefts, rights, refs = refs[: 3 * sides], refs[3 * sides : 6 * sides], refs[6 * sides :]
    out, left, right = refs[0], refs[1 : 1 + sides], refs[1 + sides : 1 + 2 * sides]
    held, local_sems = refs[1 + 2 * sides :]
    local = Local(local_sems)
    at_first = lax.axis_index("section") == 0
    tokens = rights[0].shape[0]
    loads = []
    for side in range(sides):
        left_steps = pairs_of(lefts[3 * side : 3 * side + 3], side == 1)
        right_steps = pairs_of(rights[3 * side : 3 * side + 3], side == 0)
        for micro in range(2):
            at = pl.ds(micro * tokens, tokens)
            loads.append(
                [
                    local.load_either(
                        at_first, left_steps[0][micro], left_steps[1][micro], left[side].at[:, at]
                    ),
                    local.load_either(
                        at_first, right_steps[0][micro], right_steps[1][micro], right[side].at[at]
                    ),
                ]
            )
    saves, number = [None, None], 0
    for side in range(sides):
        for micro in range(2):
            for load in loads[2 * side + micro]:
                load.wait()
        for block in range(right[side].shape[1] // blk):
            slot = number % 2
            if saves[slot] is not None:
                saves[slot].wait()
            at = pl.ds(block * blk, blk)
            held[slot] = dot_nn(left[side][...], right[side][:, at]).astype(bf16)
            saves[slot] = local.load(held.at[slot], out.at[:, pl.ds(number * blk, blk)])
            number += 1
    for save in saves:
        save.wait()


def pairs_of(steps, backward):
    early, late = (steps[0], steps[1]), (steps[1], steps[2])
    return (late, early) if backward else (early, late)


VMEM_SPEC = pl.BlockSpec(memory_space=pltpu.VMEM)
HBM_SPEC = pl.BlockSpec(memory_space=pltpu.HBM)


def shape(dims, kind):
    return jax.ShapeDtypeStruct(dims, kind)


def exchange_scratch(chunks, own, cols):
    return [
        pltpu.VMEM((chunks, 2 * own, cols), f32),
        pltpu.VMEM((chunks, 2 * own, cols), bf16),
        pltpu.VMEM((chunks, 2 * own, cols), bf16),
        pltpu.VMEM((chunks, own, cols), bf16),
        pltpu.VMEM((chunks, own, cols), bf16),
        pltpu.SemaphoreType.DMA((12,)),
        pltpu.SemaphoreType.DMA((7, chunks)),
        pltpu.SemaphoreType.DMA((7, chunks)),
    ]


def params(number=None):
    if number is None:
        return pltpu.CompilerParams(vmem_limit_bytes=62 * MIB)
    return pltpu.CompilerParams(
        vmem_limit_bytes=62 * MIB, collective_id=number, has_side_effects=True
    )


def cost(flops, size):
    return pl.CostEstimate(flops=int(flops), bytes_accessed=int(size), transcendentals=0)


def attn_forward(hidden, pack, model_gains, gains, tables, masks, carried):
    chunks, own, cols = hidden.shape
    tokens, q_width, width = 4 * own, pack.shape[1] // 3, gains.shape[1]
    depth = chunks * cols
    carry = carried is not None
    rows = shape((chunks, own, cols), bf16)
    return pl.pallas_call(
        functools.partial(attn_forward_kernel, width, carry),
        in_specs=[HBM_SPEC] * carry + [VMEM_SPEC, HBM_SPEC] + [VMEM_SPEC] * 2 + [HBM_SPEC] * 2,
        out_specs=[HBM_SPEC] * 5 + [VMEM_SPEC] + [HBM_SPEC] * carry,
        out_shape=[
            shape((depth, tokens), bf16),
            shape((tokens, 2 * q_width), f32),
            shape((tokens, q_width // 2), bf16),
            shape((tokens, q_width), bf16),
            shape((chunks, own, cols), f32),
            rows,
        ]
        + [rows] * carry,
        scratch_shapes=[
            pltpu.VMEM(tables.shape, f32),
            pltpu.VMEM(masks.shape, f32),
            pltpu.VMEM((chunks, tokens, cols), bf16),
            pltpu.VMEM((depth, tokens), bf16),
            pltpu.VMEM((tokens, 2 * q_width), f32),
            pltpu.VMEM((tokens, q_width // 2), bf16),
            pltpu.VMEM((tokens, q_width), bf16),
            pltpu.VMEM((chunks, own, cols), f32),
            pltpu.VMEM(pack.shape, bf16),
        ]
        + exchange_scratch(chunks, own, cols),
        compiler_params=params(8 if carry else 0),
        cost_estimate=cost(2 * tokens * pack.size, pack.size * 2),
        name="attn_forward",
    )(*([carried] if carry else []), hidden, pack, model_gains, gains, tables, masks)


def ffn_forward(rows, mixed, pack, hop):
    chunks, own, cols = rows.shape
    tokens, units = 4 * own, pack.shape[1] // 3
    depth = chunks * cols
    return pl.pallas_call(
        functools.partial(ffn_forward_kernel, hop),
        in_specs=[VMEM_SPEC, HBM_SPEC, HBM_SPEC],
        out_specs=[HBM_SPEC] * 3 + [VMEM_SPEC] * (2 if hop else 1),
        out_shape=[
            shape((depth, tokens), bf16),
            shape((tokens, 2 * units), f32),
            shape((tokens, units), bf16),
        ]
        + [shape((chunks, own, cols), bf16)] * (2 if hop else 1),
        scratch_shapes=[
            pltpu.VMEM((chunks, tokens, cols), bf16),
            pltpu.VMEM((depth, tokens), bf16),
            pltpu.VMEM((chunks, own, cols), f32),
            pltpu.VMEM((tokens, units), bf16),
            pltpu.VMEM((tokens, 2 * units), f32),
            pltpu.VMEM(pack.shape, bf16),
        ]
        + exchange_scratch(chunks, own, cols),
        compiler_params=params(1 if hop else 2),
        cost_estimate=cost(2 * tokens * pack.size, pack.size * 2),
        name="ffn_forward",
    )(rows, mixed, pack)


def ffn_backward(rows, mixed, gate_up, pack, model_gains, spread, carried):
    chunks, own, cols = rows.shape
    tokens, units = 4 * own, pack.shape[1] // 3
    moved = (chunks, tokens, cols) if spread else (chunks * cols, tokens)
    carry = carried is not None
    return pl.pallas_call(
        functools.partial(ffn_backward_kernel, spread, carry),
        in_specs=[HBM_SPEC] * carry + [VMEM_SPEC] + [HBM_SPEC] * 5 + [VMEM_SPEC],
        out_specs=[HBM_SPEC] * 2 + [VMEM_SPEC] * 3 + [HBM_SPEC] * carry,
        out_shape=[
            shape(moved, bf16),
            shape((tokens, 2 * units), bf16),
            shape((chunks, own, cols), f32),
            shape((chunks, own, cols), bf16),
            shape((chunks, cols), f32),
        ]
        + [shape((chunks, own, cols), bf16)] * carry,
        scratch_shapes=[
            pltpu.VMEM((chunks, tokens, cols), bf16),
            pltpu.VMEM(moved, bf16),
            pltpu.VMEM((chunks, own, cols), f32),
            pltpu.VMEM((tokens, 2 * units), bf16),
            pltpu.VMEM((tokens, 2 * units), f32),
            pltpu.VMEM((tokens, units), f32),
            pltpu.VMEM(pack.shape, bf16),
        ]
        + exchange_scratch(chunks, own, cols),
        compiler_params=params(9 if carry else 3),
        cost_estimate=cost(2 * tokens * pack.size, pack.size * 2),
        name="ffn_backward",
    )(*([carried] if carry else []), rows, *mixed, *gate_up, pack, model_gains)


def attn_backward(
    rows, grad_mixed, hidden, projected, values, pack, model_gains, gains, tables, masks, hop
):
    chunks, own, cols = rows.shape
    tokens, q_width, width = 4 * own, pack.shape[1] // 3, gains.shape[1]
    depth = chunks * cols
    return pl.pallas_call(
        functools.partial(attn_backward_kernel, width, hop),
        in_specs=[VMEM_SPEC] * 2 + [HBM_SPEC] * 7 + [VMEM_SPEC] * 2 + [HBM_SPEC] * 2,
        out_specs=[HBM_SPEC] * 2 + [VMEM_SPEC] * (4 if hop else 3),
        out_shape=[
            shape((depth, tokens), bf16),
            shape((tokens, 2 * q_width), bf16),
            shape((chunks, own, cols), bf16),
            shape((chunks, cols), f32),
            shape((8, width), f32),
        ]
        + [shape((chunks, own, cols), bf16)] * (1 if hop else 0),
        scratch_shapes=[
            pltpu.VMEM(tables.shape, f32),
            pltpu.VMEM(masks.shape, f32),
            pltpu.VMEM((chunks, tokens, cols), bf16),
            pltpu.VMEM((depth, tokens), bf16),
            pltpu.VMEM((tokens, 2 * q_width), bf16),
            pltpu.VMEM((chunks, own, cols), bf16),
            pltpu.VMEM((tokens, 2 * q_width), f32),
            pltpu.VMEM((tokens, q_width // 2), bf16),
            pltpu.VMEM((tokens, q_width), f32),
            pltpu.VMEM((chunks, own, cols), f32),
            pltpu.VMEM(pack.shape, bf16),
        ]
        + exchange_scratch(chunks, own, cols),
        compiler_params=params(4 if hop else 5),
        cost_estimate=cost(2 * tokens * pack.size, pack.size * 2),
        name="attn_backward",
    )(
        rows, grad_mixed, *hidden, *projected, *values, pack, model_gains, gains, tables, masks
    )


def weight_grad(lefts, rights):
    depth, tokens = lefts[0][0].shape
    blk = 512
    widths = [right[0].shape[1] for right in rights]
    return pl.pallas_call(
        functools.partial(weight_grad_kernel, blk, len(lefts)),
        in_specs=[HBM_SPEC] * (6 * len(lefts)),
        out_specs=HBM_SPEC,
        out_shape=shape((depth, sum(widths)), bf16),
        scratch_shapes=[pltpu.VMEM((depth, 2 * tokens), bf16) for _ in lefts]
        + [pltpu.VMEM((2 * tokens, width), bf16) for width in widths]
        + [
            pltpu.VMEM((2, depth, blk), bf16),
            pltpu.SemaphoreType.DMA((4 * len(lefts) + sum(widths) // blk,)),
        ],
        compiler_params=params(),
        cost_estimate=cost(4 * depth * tokens * sum(widths), 2 * depth * sum(widths)),
        name="weight_grad",
    )(*sum(lefts, []), *sum(rights, []))


def rope_tables(position, head_width):
    exponent = jnp.arange(0, head_width, 2).astype(f32) / head_width
    inverse = rope_base ** (-exponent)
    angles = position.astype(f32)[:, None] * inverse[None, :]
    cosine, sine = jnp.cos(angles), jnp.sin(angles)
    return (
        jnp.concatenate([cosine, cosine], axis=-1),
        jnp.concatenate([-sine, sine], axis=-1),
    )


def per_device(
    block_input,
    segment_ids,
    out_cotangent,
    attn_norm,
    q_weight,
    k_weight,
    v_weight,
    o_weight,
    q_norm,
    k_norm,
    ffn_norm,
    gate_weight,
    up_weight,
    down_weight,
):
    section = lax.axis_index("section")
    place = lax.axis_index("dp")
    core = place % 2
    half = lax.axis_index("tensor")
    n_dp = lax.axis_size("dp")
    n_chip = n_dp // 2
    micro_count, own_rows, depth = block_input.shape
    length = 2 * own_rows
    head_width = q_norm.shape[1]
    first_core = core == 0
    swap_core = [(i, i ^ 1) for i in range(n_dp)]
    swap_half = [(0, 1), (1, 0)]
    chip_groups = [[2 * chip + one for chip in range(n_chip)] for one in (0, 1)]

    def to_core(values):
        return lax.ppermute(values, "dp", swap_core)

    def to_half(values):
        return lax.ppermute(values, "tensor", swap_half)

    def split_columns(weight):
        side = weight.shape[1] // 2
        left, right = weight[:, :side], weight[:, side:]
        return jnp.where(first_core, left, right), jnp.where(first_core, right, left)

    def split_rows(weight):
        side = weight.shape[0] // 2
        left, right = weight[:side].T, weight[side:].T
        return jnp.where(first_core, left, right), jnp.where(first_core, right, left)

    def chip_block(pairs):
        mine = jnp.concatenate([pair[0] for pair in pairs], axis=1)
        theirs = to_core(jnp.concatenate([pair[1] for pair in pairs], axis=1))
        return jnp.concatenate(
            [jnp.where(first_core, mine, theirs), jnp.where(first_core, theirs, mine)], axis=0
        )

    def gathered(block):
        return lax.all_gather(block, "dp", axis=0, tiled=True, axis_index_groups=chip_groups)

    square = n_chip == row_chunks
    attn_block = chip_block(
        [
            split_columns(q_weight[0]),
            split_columns(k_weight[0]),
            split_columns(v_weight[0]),
            split_rows(o_weight[0]),
        ]
    )
    ffn_block = chip_block(
        [split_columns(gate_weight[0]), split_columns(up_weight[0]), split_rows(down_weight[0])]
    )
    if square:
        attn_block, ffn_block = lax.optimization_barrier((attn_block, ffn_block))
        attn_pack = chip_gather(attn_block).reshape(depth, -1)
    else:
        attn_pack = gathered(attn_block)
    ffn_pack = gathered(ffn_block)

    cols = depth // row_chunks
    model_gains = jnp.concatenate([attn_norm, ffn_norm], axis=0).reshape(2, row_chunks, cols)
    head_gains = jnp.concatenate([q_norm, k_norm, jnp.zeros((6, head_width), f32)], axis=0)

    def chunked(rows):
        return rows.reshape(rows.shape[0], row_chunks, cols).transpose(1, 0, 2)

    def joined(rows):
        return rows.transpose(1, 0, 2).reshape(rows.shape[1], depth)

    inputs = [chunked(block_input[micro]) for micro in range(2)]
    cotangents = [chunked(out_cotangent[micro]) for micro in range(2)]

    def arranged(values):
        sides = values[..., :own_rows], values[..., own_rows:]
        return jnp.concatenate(
            [jnp.where(half == 0, *sides), jnp.where(half == 0, *sides[::-1])], axis=-1
        )

    position = arranged(jnp.arange(length, dtype=jnp.int32))
    tables = jnp.stack(rope_tables(position, head_width))
    ids = arranged(jnp.stack([segment_ids, to_core(segment_ids)], axis=1))
    causal = position[:, None] >= position[None, :]
    masks = (causal & (ids[..., :, None] == ids[..., None, :])).astype(f32)

    at_first = section == 0

    def pick(first, second):
        return jax.tree.map(lambda a, b: jnp.where(at_first, a, b), first, second)

    zero_rows = jnp.zeros_like(inputs[0])
    forward_masks = [masks[0], pick(masks[1], masks[0]), masks[1]]
    backward_masks = [masks[0], pick(masks[0], masks[1]), masks[1]]
    results, backs, saves = [], [], []
    grads, ffn_saves, attn_saves, gains = [], [], [], []

    def forward_step(step, arrived, hop, carried=None):
        hidden = inputs[step] if step < 2 else zero_rows
        if step > 0:
            hidden = pick(hidden, arrived)
        turned_in, projected, values, attended, mixed, rows, *carried = attn_forward(
            hidden, attn_pack, model_gains, head_gains, tables, forward_masks[step], carried
        )
        turned_mid, gate_up, activated, result, *rest = ffn_forward(rows, mixed, ffn_pack, hop)
        results.append(result)
        backs.append((hidden, projected, values, mixed, gate_up))
        saves.append((turned_in, attended, turned_mid, activated))
        return (rest + carried + [None])[0]

    def back_ffn(step, arrived, carried=None):
        rows = pick(arrived, cotangents[step] if step < 2 else zero_rows)
        *_, mixed, gate_up = zip(backs[0], backs[2]) if step == 1 else zip(backs[1], backs[1])
        turned_rows, ffn_grads, grad_mixed, proj_rows, gain_grad, *carried = ffn_backward(
            rows, mixed, gate_up, ffn_pack, model_gains, square, carried
        )
        ffn_saves.append((turned_rows, ffn_grads))
        return proj_rows, grad_mixed, gain_grad, *carried

    def back_attn(step, proj_rows, grad_mixed, ffn_gain_grad, hop):
        hidden, projected, values, *_ = (
            zip(backs[0], backs[2]) if step == 1 else zip(backs[1], backs[1])
        )
        turned_rows, attn_grads, grad_hidden, attn_gain_grad, head_gain_grads, *rest = attn_backward(
            proj_rows, grad_mixed, hidden, projected, values, attn_pack, model_gains, head_gains,
            tables, backward_masks[step], hop,
        )
        attn_saves.append((turned_rows, attn_grads))
        grads.append(grad_hidden)
        gains.append((attn_gain_grad, ffn_gain_grad, head_gain_grads))
        return rest[0] if hop else None

    def column(table, item):
        return [row[item] for row in table]

    arrived = forward_step(0, zero_rows, True)
    forward_step(1, arrived, False)
    *others, arrived = back_ffn(0, zero_rows, results[1])
    back_attn(0, *others, False)
    grad_arrived = forward_step(2, arrived, False, grads[0])
    grad_arrived, results[2] = lax.optimization_barrier((grad_arrived, results[2]))
    grad_arrived = back_attn(1, *back_ffn(1, grad_arrived), True)
    if square:
        active = [pick(saves[micro][3], saves[micro + 1][3]) for micro in range(2)]
        active_all = gathered(jnp.concatenate(active, axis=0))
    proj_rows, *others = back_ffn(2, grad_arrived)
    if square:
        ffn_partial = weight_grad([column(saves, 2)], [column(ffn_saves, 1)])
        ffn_partial, active_all = lax.optimization_barrier((ffn_partial, active_all))
    else:
        ffn_partial = weight_grad(
            [column(saves, 2), column(ffn_saves, 0)], [column(ffn_saves, 1), column(saves, 3)]
        )
    proj_rows, ffn_partial = lax.optimization_barrier((proj_rows, ffn_partial))
    back_attn(2, proj_rows, *others, False)
    attn_partial = weight_grad(
        [column(saves, 0), column(attn_saves, 0)], [column(attn_saves, 1), column(saves, 1)]
    )
    gain_total = functools.reduce(lambda a, b: jax.tree.map(jnp.add, a, b), gains)

    section_outputs = jnp.stack(
        [joined(pick(results[micro], results[micro + 1])) for micro in range(2)]
    )[None]
    section_input_grads = jnp.stack(
        [joined(pick(grads[micro + 1], grads[micro])) for micro in range(2)]
    )[None]

    def scattered(partial):
        return lax.psum_scatter(
            partial, "dp", scatter_dimension=0, tiled=True, axis_index_groups=chip_groups
        )

    def owned(rows):
        side = rows.shape[0] // 2
        own = jnp.where(first_core, rows[:side], rows[side:])
        other = to_core(jnp.where(first_core, rows[side:], rows[:side]))
        return (
            jnp.where(first_core, own, other).astype(f32),
            jnp.where(first_core, other, own).astype(f32),
        )

    attn_partial, ffn_rows = lax.optimization_barrier((attn_partial, scattered(ffn_partial)))
    ffn_sides = owned(ffn_rows)
    attn_sides = owned(scattered(attn_partial))
    units = gate_weight.shape[2] // 2
    if square:
        spread_rows = jnp.concatenate(
            [pick(ffn_saves[micro + 1][0], ffn_saves[micro][0]) for micro in range(2)], axis=1
        ).reshape(-1, cols)
        down_sides = owned(dot_tn(spread_rows, active_all))
    else:
        down_sides = [side[:, 2 * units :] for side in ffn_sides]
    attn_sides = owned(scattered(attn_partial))
    q_width = q_weight.shape[2] // 2
    kv_width = k_weight.shape[2] // 2

    def across(sides, first, width):
        return jnp.concatenate([side[:, first : first + width] for side in sides], axis=1)[None]

    def down(sides, first):
        return jnp.concatenate([side[:, first:].T for side in sides], axis=0)[None]

    packed = jnp.concatenate(
        [
            gain_total[0].reshape(-1),
            gain_total[1].reshape(-1),
            gain_total[2][0],
            gain_total[2][1],
        ]
    ).reshape(-1, head_width)
    packed = packed + to_core(packed)
    packed = packed + to_half(packed)
    reach = 2
    while reach < n_dp:
        packed = packed + lax.ppermute(packed, "dp", [(i, i ^ reach) for i in range(n_dp)])
        reach *= 2
    packed = packed.reshape(-1)
    return (
        section_outputs,
        section_input_grads,
        packed[None, :depth],
        across(attn_sides, 0, q_width),
        across(attn_sides, q_width, kv_width),
        across(attn_sides, q_width + kv_width, kv_width),
        down(attn_sides, 2 * q_width),
        packed[None, 2 * depth : 2 * depth + head_width],
        packed[None, 2 * depth + head_width :],
        packed[None, depth : 2 * depth],
        across(ffn_sides, 0, units),
        across(ffn_sides, units, units),
        down(down_sides, 0),
    )


def solution(mesh):
    rows = P(None, ("dp", "tensor"), None)
    out_rows = P("section", None, ("dp", "tensor"), None)
    gain = P("section", None)
    wide = P("section", "dp", "tensor")
    tall = P("section", "tensor", "dp")
    return jax.shard_map(
        per_device,
        mesh=mesh,
        in_specs=(
            rows, P(None, "dp"), rows, gain, wide, wide, wide, tall, gain, gain, gain, wide, wide, tall,
        ),
        out_specs=(
            out_rows, out_rows, gain, wide, wide, wide, tall, gain, gain, gain, wide, wide, tall,
        ),
        check_vma=False,
    )
```

```python
import functools

import jax
import jax.numpy as jnp
from jax import lax
from jax.experimental import pallas as pl
from jax.experimental.pallas import tpu as pltpu
from jax.sharding import PartitionSpec as P

norm_eps = 1e-06
rope_base = 1000000.0
masked_score = -1e30
row_chunks = 4
background_size = 4 * 384 * 960
f32 = jnp.float32
bf16 = jnp.bfloat16
MIB = 1024 * 1024
MESH = pl.DeviceIdType.MESH


def dot_nn(left, right):
    return lax.dot_general(left, right, (((1,), (0,)), ((), ())), preferred_element_type=f32)


def dot_nt(left, right):
    return lax.dot_general(left, right, (((1,), (1,)), ((), ())), preferred_element_type=f32)


def dot_tn(left, right):
    return lax.dot_general(left, right, (((0,), (0,)), ((), ())), preferred_element_type=f32)


def inverse_rms(values):
    return lax.rsqrt(jnp.mean(values * values, axis=-1, keepdims=True) + norm_eps)


def norm_back(grad_out, values, inverse, gain_vec):
    scaled = grad_out * gain_vec
    return inverse * (
        scaled - values * inverse * inverse * jnp.mean(scaled * values, axis=-1, keepdims=True)
    )


class Exchange:
    def __init__(self, send_sems, recv_sems):
        place = lax.axis_index("dp")
        self.core = {"dp": place + 1 - 2 * (place % 2)}
        self.half = {"tensor": 1 - lax.axis_index("tensor")}
        self.section = {"section": 1 - lax.axis_index("section")}
        core, chip = place % 2, place // 2
        across, along = chip % 2, chip // 2
        self.chip = chip
        numbers = (chip + 1 - 2 * across, chip + 2 - 4 * along, 3 - chip)
        self.chips = [(number, {"dp": 2 * number + core}) for number in numbers]
        self.send_sems, self.recv_sems = send_sems, recv_sems

    def greet(self, with_section, with_chips):
        others = [self.core, self.half] + ([self.section] if with_section else [])
        self.meet(others + [device for _, device in self.chips[:with_chips]])

    def meet(self, others):
        barrier = pltpu.get_barrier_semaphore()
        for other in others:
            pl.semaphore_signal(barrier, inc=1, device_id=other, device_id_type=MESH)
        pl.semaphore_wait(barrier, len(others))

    def copy(self, source, target, other, stage, chunk):
        return pltpu.make_async_remote_copy(
            src_ref=source,
            dst_ref=target,
            send_sem=self.send_sems.at[stage, chunk],
            recv_sem=self.recv_sems.at[stage, chunk],
            device_id=other,
            device_id_type=MESH,
        )


def gather_then(exchange, rows, use):
    chunks, total, _ = rows.shape
    own = total // 4
    first = [
        exchange.copy(rows.at[c, pl.ds(0, own)], rows.at[c, pl.ds(own, own)], exchange.half, 0, c)
        for c in range(chunks)
    ]
    second = [
        exchange.copy(
            rows.at[c, pl.ds(0, 2 * own)], rows.at[c, pl.ds(2 * own, 2 * own)], exchange.core, 1, c
        )
        for c in range(chunks)
    ]
    for c in range(chunks):
        first[c].start()
    for c in range(chunks):
        first[c].wait_recv()
        second[c].start()
        if c > 0:
            second[c - 1].wait_recv()
            use(c - 1)
    second[chunks - 1].wait_recv()
    use(chunks - 1)
    return first + second


def scatter_from(exchange, make, idle, finish, keep, send_core, recv_core, send_half, recv_half):
    chunks, pair, _ = keep.shape
    own = pair // 2
    first = [
        exchange.copy(send_core.at[c], recv_core.at[c], exchange.core, 2, c) for c in range(chunks)
    ]
    second = [
        exchange.copy(send_half.at[c], recv_half.at[c], exchange.half, 3, c) for c in range(chunks)
    ]

    def middle(c):
        first[c].wait_recv()
        summed = keep[c] + recv_core[c].astype(f32)
        send_half[c] = summed[own:].astype(bf16)
        second[c].start()
        keep[c, :own] = summed[:own]

    for c in range(chunks):
        product = make(c)
        send_core[c] = product[pair:].astype(bf16)
        first[c].start()
        keep[c] = product[:pair]
        if c > 0:
            middle(c - 1)
    middle(chunks - 1)
    for c in range(chunks):
        idle(c)
        second[c].wait_recv()
        finish(c, keep[c, :own] + recv_half[c].astype(f32))
    return first + second


class ChipGather:
    def __init__(self, exchange, local, blocks, out, stage):
        (across, across_device), (along, along_device), _ = exchange.chips
        at_first = lax.axis_index("section") == 0
        half = blocks[0].shape[0] // 2
        first, last = pl.ds(0, half), pl.ds(half, half)
        target = out.at[exchange.chip]
        choices = [
            [
                exchange.copy(block, target, across_device, stage, 0),
                exchange.copy(block, target, along_device, stage, 1),
            ]
            for block in blocks
        ]
        self.direct = choices[0]
        self.passed = [
            exchange.copy(out.at[across, first], out.at[across, first], along_device, stage, 2),
            exchange.copy(out.at[along, last], out.at[along, last], across_device, stage, 3),
        ]
        for index, block in enumerate(blocks):
            here = at_first if index == 0 else jnp.logical_not(at_first)

            def start(index=index):
                for copy in choices[index]:
                    copy.start()

            if len(blocks) > 1:
                pl.when(here)(start)
            else:
                start()

        if len(blocks) > 1:
            local.saves.append(local.load_either(at_first, *blocks, target))
        else:
            local.save(blocks[0], target)

    def pass_on(self):
        for copy, onward in zip(self.direct, self.passed):
            copy.wait_recv()
            onward.start()

    def finish(self):
        for copy in self.passed:
            copy.wait_recv()
        return self.direct + self.passed


class Background:
    def __init__(self, exchange, local, spans, sources, targets):
        self.gathers = [
            ChipGather(
                exchange,
                local,
                [source.at[pl.ds(first, count)] for source in sources[2 * index : 2 * index + 2]],
                target,
                7 + index,
            )
            for index, ((first, count), target) in enumerate(zip(spans, targets))
        ]

        self.late = sum(s.size for s in targets) > background_size

    def pass_on(self, late):
        if late == self.late:
            for gather in self.gathers:
                gather.pass_on()

    def finish(self):
        return sum([gather.finish() for gather in self.gathers], [])


def chip_gather_kernel(*refs):
    *blocks, out, local_sems, send_sems, recv_sems = refs
    exchange, local = Exchange(send_sems, recv_sems), Local(local_sems)
    exchange.meet([device for _, device in exchange.chips[:2]])
    gather = ChipGather(exchange, local, blocks, out, 0)
    gather.pass_on()
    for copy in gather.finish():
        copy.wait_send()
    local.finish()


def chip_gather(blocks, number):
    return pl.pallas_call(
        chip_gather_kernel,
        in_specs=[HBM_SPEC] * len(blocks),
        out_specs=HBM_SPEC,
        out_shape=shape((4,) + blocks[0].shape, bf16),
        scratch_shapes=[
            pltpu.SemaphoreType.DMA((1,)),
            pltpu.SemaphoreType.DMA((1, 4)),
            pltpu.SemaphoreType.DMA((1, 4)),
        ],
        compiler_params=params(number),
        cost_estimate=cost(0, 300 * blocks[0].size),
        name="chip_gather",
    )(*blocks)


def load_pack(pack, held, local):
    depth = held.shape[0] // row_chunks
    return [
        local.load(pack.at[pl.ds(c * depth, depth)], held.at[pl.ds(c * depth, depth)])
        for c in range(row_chunks)
    ]


class Local:
    def __init__(self, sems):
        self.sems, self.used, self.saves = sems, 0, []

    def copy(self, source, target):
        self.used += 1
        return pltpu.make_async_copy(source, target, self.sems.at[self.used - 1])

    def load(self, source, target):
        copy = self.copy(source, target)
        copy.start()
        return copy

    def load_either(self, at_first, first, second, target):
        one = self.copy(first, target)
        other = pltpu.make_async_copy(second, target, self.sems.at[self.used - 1])

        @pl.when(at_first)
        def _():
            one.start()

        @pl.when(jnp.logical_not(at_first))
        def _():
            other.start()

        return one

    def save(self, source, target):
        self.saves.append(self.load(source, target))

    def finish(self):
        for copy in self.saves:
            copy.wait()


def row_mean(values):
    size = values.shape[0] * values.shape[2]
    return jnp.sum(jnp.sum(values, axis=0), axis=-1, keepdims=True)[None] * (1.0 / size)


def accumulate(total, left, weights, first_row, first_col, width, start):
    depth = left.shape[1]
    blk = 512 if width % 512 == 0 else 256

    def body(index, _):
        at = pl.multiple_of(index * blk, blk)
        product = dot_nn(left, weights[pl.ds(first_row, depth), pl.ds(first_col + at, blk)])
        if start:
            total[:, pl.ds(at, blk)] = product
        else:
            total[:, pl.ds(at, blk)] += product
        return 0

    lax.fori_loop(0, width // blk, body, 0)


def rotated(raw, gain, cosine, signed_sine):
    inverse = inverse_rms(raw)
    scaled = raw * inverse * gain
    turned = scaled * cosine + pltpu.roll(scaled, 64, 1) * signed_sine
    return inverse, turned.astype(bf16)


def softmax_rows(query_rot, key_rot, allowed, scale):
    scores = jnp.where(allowed, dot_nt(query_rot, key_rot) * scale, masked_score)
    exponent = jnp.exp(scores - jnp.max(scores, axis=-1, keepdims=True))
    return exponent / jnp.sum(exponent, axis=-1, keepdims=True)


class Spread:
    def __init__(self, exchange, local, rows, moved):
        side = rows.shape[1] // 2
        self.own = local.load(rows.at[exchange.chip], moved.at[exchange.chip])
        self.arrivals, self.onward = [], []
        for index, (number, device) in enumerate(exchange.chips):
            self.arrivals.append(
                exchange.copy(
                    rows.at[number, pl.ds(0, side)],
                    moved.at[exchange.chip, pl.ds(0, side)],
                    device, 5, index,
                )
            )
            self.arrivals[-1].start()
            self.onward.append(
                exchange.copy(
                    moved.at[number, pl.ds(0, side)],
                    moved.at[number, pl.ds(side, side)],
                    exchange.core, 6, index,
                )
            )

    def pass_on(self, index):
        self.arrivals[index].wait_recv()
        self.onward[index].start()

    def finish(self):
        self.own.wait()
        for copy in self.onward:
            copy.wait_recv()
        return self.arrivals + self.onward


def turn_chunk(rows, target, c):
    cols = rows.shape[2]
    target[pl.ds(c * cols, cols), :] = rows[c].T


def attn_forward_kernel(
    width, spread, hold, spans, carry, *refs
):
    sources, refs = refs[: 2 * len(spans)], refs[2 * len(spans) :]
    if carry:
        carried, refs = refs[0], refs[1:]
    (
        hidden, pack, model_gains, gains, tables_in, masks_in,
        moved_out, projected_out, values_out, attended_out, mixed_out, normed_ffn_rows,
    ), refs = refs[:12], refs[12:]
    if carry:
        arrived, refs = refs[0], refs[1:]
    targets, refs = refs[: len(spans)], refs[len(spans) :]
    (
        tables, masks, normed, moved, projected, values, attended, mixed,
        held, keep, send_core, recv_core, send_half, recv_half, local_sems, send_sems, recv_sems,
    ) = refs
    exchange, local = Exchange(send_sems, recv_sems), Local(local_sems)
    exchange.greet(carry, (3 if spread else 2 if spans else 0))
    loads = load_pack(pack, held, local)
    background = Background(exchange, local, spans, sources, targets)
    extra = [local.load(tables_in, tables), local.load(masks_in, masks)]
    chunks, own, cols = hidden.shape
    length = 2 * own
    q_width = attended.shape[1]
    kv_width = q_width // 2
    kv_heads = kv_width // width
    group = q_width // kv_width
    rows = hidden[...].astype(f32)
    inverse = lax.rsqrt(row_mean(rows * rows) + norm_eps)
    for c in range(chunks):
        normed[c, :own] = (rows[c] * inverse[0] * model_gains[0, c][None, :]).astype(bf16)

    def project(c):
        loads[c].wait()
        accumulate(projected, normed[c], held, c * cols, 0, 2 * q_width, c == 0)

    copies = gather_then(exchange, normed, project)
    moving = Spread(exchange, local, normed, moved) if spread else None
    hops = []
    if carry:
        hops = [exchange.copy(carried, arrived, exchange.section, 4, 0)]
        hops[0].start()
    local.save(projected, projected_out)
    for load in extra:
        load.wait()
    cos, sin = tables[0], tables[1]
    gain_q, gain_k = gains[0:1, :], gains[1:2, :]
    scale = width ** (-0.5)
    values[...] = projected[:, q_width + kv_width :].astype(bf16)
    local.save(values, values_out)
    for seq in range(2):
        at = slice(seq * length, (seq + 1) * length)
        allowed = masks[seq] > 0.5
        for kv in range(kv_heads):
            raw_k = projected[at, q_width + kv * width : q_width + (kv + 1) * width]
            value = values[at, kv * width : (kv + 1) * width]
            _, key_rot = rotated(raw_k, gain_k, cos, sin)
            for one in range(group):
                head = slice((kv * group + one) * width, (kv * group + one + 1) * width)
                _, query_rot = rotated(projected[at, head], gain_q, cos, sin)
                weights = softmax_rows(query_rot, key_rot, allowed, scale)
                attended[at, head] = dot_nn(weights.astype(bf16), value).astype(bf16)
    local.save(attended, attended_out)
    background.pass_on(False)

    def make(c):
        return dot_nt(attended[...], held[c * cols : (c + 1) * cols, 2 * q_width :])

    def idle(c):
        if not (spread or hold):
            turn_chunk(normed, moved, c)
        elif spread and c > 0:
            moving.pass_on(c - 1)
        if c == chunks - 2:
            background.pass_on(True)

    def finish(c, summed):
        mixed[c] = hidden[c].astype(f32) + summed

    copies += scatter_from(
        exchange, make, idle, finish, keep, send_core, recv_core, send_half, recv_half
    )
    if spread:
        copies += moving.finish()
    local.save(normed if hold else moved, moved_out)
    local.save(mixed, mixed_out)
    rows = mixed[...]
    inverse = lax.rsqrt(row_mean(rows * rows) + norm_eps)
    for c in range(chunks):
        normed_ffn_rows[c] = (rows[c] * inverse[0] * model_gains[1, c][None, :]).astype(bf16)
    for copy in hops:
        copy.wait()
    copies += background.finish()
    for copy in copies:
        copy.wait_send()
    local.finish()


def ffn_forward_kernel(
    hop, spread, spans, *refs
):
    if spread:
        held_rows, refs = refs[0], refs[1:]
    sources, refs = refs[: 2 * len(spans)], refs[2 * len(spans) :]
    rows, mixed_in, pack, turned_out, gate_up_out, activated_out, result, *rest = refs
    if hop:
        arrived, rest = rest[0], rest[1:]
    if spread:
        moved, rest = rest[0], rest[1:]
    targets, rest = rest[: len(spans)], rest[len(spans) :]
    (
        normed, turned, mixed, activated, total,
        held, keep, send_core, recv_core, send_half, recv_half, local_sems, send_sems, recv_sems,
    ) = rest
    exchange, local = Exchange(send_sems, recv_sems), Local(local_sems)
    exchange.greet(hop, 3 if spread else 2 if spans else 0)
    loads = load_pack(pack, held, local)
    moving = Spread(exchange, local, held_rows, moved) if spread else None
    background = Background(exchange, local, spans, sources, targets)
    mixed_load = local.load(mixed_in, mixed)
    chunks, own, cols = rows.shape
    units = activated.shape[1]
    for c in range(chunks):
        normed[c, :own] = rows[c]

    def project(c):
        loads[c].wait()
        accumulate(total, normed[c], held, c * cols, 0, 2 * units, c == 0)

    copies = gather_then(exchange, normed, project)
    local.save(total, gate_up_out)
    blk = 256

    def activate(index, _):
        at = pl.multiple_of(index * blk, blk)
        gate = total[:, pl.ds(at, blk)]
        upward = total[:, pl.ds(units + at, blk)]
        activated[:, pl.ds(at, blk)] = (gate * jax.nn.sigmoid(gate) * upward).astype(bf16)
        return 0

    lax.fori_loop(0, units // blk, activate, 0)
    local.save(activated, activated_out)
    background.pass_on(False)
    mixed_load.wait()
    hops = []

    def make(c):
        return dot_nt(activated[...], held[c * cols : (c + 1) * cols, 2 * units :])

    def idle(c):
        turn_chunk(normed, turned, c)
        if spread and c > 0:
            moving.pass_on(c - 1)
        if c == chunks - 2:
            background.pass_on(True)

    def finish(c, summed):
        result[c] = (mixed[c] + summed).astype(bf16)
        if hop:
            hops.append(exchange.copy(result.at[c], arrived.at[c], exchange.section, 4, c))
            hops[-1].start()

    copies += scatter_from(
        exchange, make, idle, finish, keep, send_core, recv_core, send_half, recv_half
    )
    local.save(turned, turned_out)
    for copy in hops:
        copy.wait()
    copies += background.finish()
    if spread:
        copies += moving.finish()
    for copy in copies:
        copy.wait_send()
    local.finish()


def ffn_backward_kernel(spread, spans, carry, *refs):
    sources, refs = refs[: 2 * len(spans)], refs[2 * len(spans) :]
    if carry:
        carried, refs = refs[0], refs[1:]
    (
        rows, mixed_a, mixed_b, gate_up_a, gate_up_b, pack, model_gains,
        moved_out, grads_out, grad_mixed, grad_proj_rows, gain_grad,
    ), refs = refs[:12], refs[12:]
    if carry:
        arrived, refs = refs[0], refs[1:]
    targets, refs = refs[: len(spans)], refs[len(spans) :]
    (
        grad_down, moved, mixed, grads, pre, total,
        held, keep, send_core, recv_core, send_half, recv_half, local_sems, send_sems, recv_sems,
    ) = refs
    exchange, local = Exchange(send_sems, recv_sems), Local(local_sems)
    exchange.greet(carry, 3 if spread else 0)
    at_first = lax.axis_index("section") == 0
    loads = load_pack(pack, held, local)
    background = Background(exchange, local, spans, sources, targets)
    pre_load = local.load_either(at_first, gate_up_a, gate_up_b, pre)
    mixed_load = local.load_either(at_first, mixed_a, mixed_b, mixed)
    chunks, own, cols = rows.shape
    units = grads.shape[1] // 2
    for c in range(chunks):
        grad_down[c, :own] = rows[c]

    def project(c):
        loads[c].wait()
        accumulate(total, grad_down[c], held, c * cols, 2 * units, units, c == 0)

    copies = gather_then(exchange, grad_down, project)
    hops = []
    if carry:
        hops = [exchange.copy(carried, arrived, exchange.section, 4, 0)]
        hops[0].start()
    moving = Spread(exchange, local, grad_down, moved) if spread else None
    pre_load.wait()
    blk = 256

    def activate(index, _):
        at = pl.multiple_of(index * blk, blk)
        gate = pre[:, pl.ds(at, blk)]
        upward = pre[:, pl.ds(units + at, blk)]
        grad_act = total[:, pl.ds(at, blk)]
        sig = jax.nn.sigmoid(gate)
        grads[:, pl.ds(at, blk)] = (grad_act * upward * sig * (1.0 + gate * (1.0 - sig))).astype(bf16)
        grads[:, pl.ds(units + at, blk)] = (grad_act * gate * sig).astype(bf16)
        return 0

    lax.fori_loop(0, units // blk, activate, 0)
    local.save(grads, grads_out)
    background.pass_on(False)

    def make(c):
        return dot_nt(grads[...], held[c * cols : (c + 1) * cols, : 2 * units])

    def idle(c):
        if not spread:
            turn_chunk(grad_down, moved, c)
        elif c > 0:
            moving.pass_on(c - 1)
        if c == chunks - 2:
            background.pass_on(True)

    def finish(c, summed):
        grad_mixed[c] = summed

    copies += scatter_from(
        exchange, make, idle, finish, keep, send_core, recv_core, send_half, recv_half
    )
    if spread:
        copies += moving.finish()
    local.save(moved, moved_out)
    mixed_load.wait()
    norm_step(mixed[...], grad_mixed[...], model_gains, 1, rows, grad_mixed, gain_grad)
    for c in range(chunks):
        grad_proj_rows[c] = grad_mixed[c].astype(bf16)
    for copy in hops:
        copy.wait()
    copies += background.finish()
    for copy in copies:
        copy.wait_send()
    local.finish()


def norm_step(values, grad_out, model_gains, which, base, out, gain_grad):
    inverse = lax.rsqrt(row_mean(values * values) + norm_eps)
    gain = jnp.concatenate([model_gains[which, c][None, None, :] for c in range(out.shape[0])], axis=0)
    scaled = grad_out * gain
    centre = row_mean(scaled * values) * inverse * inverse
    out[...] = (base[...].astype(f32) + inverse * (scaled - values * centre)).astype(out.dtype)
    for c in range(out.shape[0]):
        gain_grad[c, :] = jnp.sum(grad_out[c] * values[c] * inverse[0], axis=0)


def attn_backward_kernel(
    width, spread, spans, hop, *refs
):
    sources, refs = refs[: 2 * len(spans)], refs[2 * len(spans) :]
    (
        rows, grad_mixed, hidden_a, hidden_b, projected_a, projected_b, values_a, values_b,
        pack, model_gains, gains, tables_in, masks_in,
        moved_out, grads_out, grad_hidden, gain_grad, head_gain_grads, *rest
    ) = refs
    if hop:
        arrived, rest = rest[0], rest[1:]
    targets, rest = rest[: len(spans)], rest[len(spans) :]
    (
        tables, masks, grad_proj, moved, grads, hidden, projected, values, total, summed_rows,
        held, keep, send_core, recv_core, send_half, recv_half, local_sems, send_sems, recv_sems,
    ) = rest
    exchange, local = Exchange(send_sems, recv_sems), Local(local_sems)
    exchange.greet(hop, 3 if spread else 0)
    at_first = lax.axis_index("section") == 0
    loads = load_pack(pack, held, local)
    background = Background(exchange, local, spans, sources, targets)
    extra = [local.load(tables_in, tables), local.load(masks_in, masks)]
    projected_load = local.load_either(at_first, projected_a, projected_b, projected)
    values_load = local.load_either(at_first, values_a, values_b, values)
    hidden_load = local.load_either(at_first, hidden_a, hidden_b, hidden)
    chunks, own, cols = rows.shape
    length = 2 * own
    q_width = grads.shape[1] // 2
    kv_width = q_width // 2
    kv_heads = kv_width // width
    group = q_width // kv_width
    for c in range(chunks):
        grad_proj[c, :own] = rows[c]

    def project(c):
        loads[c].wait()
        accumulate(total, grad_proj[c], held, c * cols, 2 * q_width, q_width, c == 0)

    copies = gather_then(exchange, grad_proj, project)
    moving = Spread(exchange, local, grad_proj, moved) if spread else None
    projected_load.wait()
    values_load.wait()
    for load in extra:
        load.wait()
    cos, sin = tables[0], tables[1]
    gain_q, gain_k = gains[0:1, :], gains[1:2, :]
    scale = width ** (-0.5)
    gain_q_sum = jnp.zeros((1, width), f32)
    gain_k_sum = jnp.zeros((1, width), f32)
    for seq in range(2):
        at = slice(seq * length, (seq + 1) * length)
        allowed = masks[seq] > 0.5
        for kv in range(kv_heads):
            raw_k = projected[at, q_width + kv * width : q_width + (kv + 1) * width]
            value = values[at, kv * width : (kv + 1) * width]
            inverse_k, key_rot = rotated(raw_k, gain_k, cos, sin)
            grad_key = jnp.zeros((length, width), f32)
            grad_value = jnp.zeros((length, width), f32)
            for one in range(group):
                head = slice((kv * group + one) * width, (kv * group + one + 1) * width)
                raw_q = projected[at, head]
                grad_head = total[at, head].astype(bf16)
                inverse_q, query_rot = rotated(raw_q, gain_q, cos, sin)
                weights = softmax_rows(query_rot, key_rot, allowed, scale)
                grad_weights = dot_nt(grad_head, value)
                delta = jnp.sum(weights * grad_weights, axis=-1, keepdims=True)
                grad_scores = (weights * (grad_weights - delta)).astype(bf16)
                grad_value += dot_tn(weights.astype(bf16), grad_head)
                grad_key += dot_tn(grad_scores, query_rot)
                grad_query = dot_nn(grad_scores, key_rot) * scale
                grad_query = grad_query * cos - pltpu.roll(grad_query, 64, 1) * sin
                gain_q_sum += jnp.sum(grad_query * raw_q * inverse_q, axis=0, keepdims=True)
                grads[at, head] = norm_back(grad_query, raw_q, inverse_q, gain_q).astype(bf16)
            grad_key = grad_key * scale
            grad_key = grad_key * cos - pltpu.roll(grad_key, 64, 1) * sin
            gain_k_sum += jnp.sum(grad_key * raw_k * inverse_k, axis=0, keepdims=True)
            first = q_width + kv * width
            grads[at, first : first + width] = norm_back(grad_key, raw_k, inverse_k, gain_k).astype(bf16)
            first += kv_width
            grads[at, first : first + width] = grad_value.astype(bf16)
    local.save(grads, grads_out)
    background.pass_on(False)
    head_gain_grads[...] = jnp.concatenate(
        [gain_q_sum, gain_k_sum, jnp.zeros((6, width), f32)], axis=0
    )

    def make(c):
        return dot_nt(grads[...], held[c * cols : (c + 1) * cols, : 2 * q_width])

    def idle(c):
        if not spread:
            turn_chunk(grad_proj, moved, c)
        elif c > 0:
            moving.pass_on(c - 1)
        if c == chunks - 2:
            background.pass_on(True)

    def finish(c, summed):
        summed_rows[c] = summed

    copies += scatter_from(
        exchange, make, idle, finish, keep, send_core, recv_core, send_half, recv_half
    )
    if spread:
        copies += moving.finish()
    local.save(moved, moved_out)
    hidden_load.wait()
    norm_step(
        hidden[...].astype(f32), summed_rows[...], model_gains, 0, grad_mixed, grad_hidden, gain_grad
    )
    if hop:
        hops = [
            exchange.copy(grad_hidden.at[c], arrived.at[c], exchange.section, 4, c)
            for c in range(chunks)
        ]
        for copy in hops:
            copy.start()
        for copy in hops:
            copy.wait()
    copies += background.finish()
    for copy in copies:
        copy.wait_send()
    local.finish()


def weight_grad_kernel(blk, sides, *refs):
    lefts, rights, refs = refs[: 3 * sides], refs[3 * sides : 6 * sides], refs[6 * sides :]
    out, left, right = refs[0], refs[1 : 1 + sides], refs[1 + sides : 1 + 2 * sides]
    held, local_sems = refs[1 + 2 * sides :]
    local = Local(local_sems)
    at_first = lax.axis_index("section") == 0
    tokens = rights[0].shape[0]
    loads = []
    for side in range(sides):
        left_steps = pairs_of(lefts[3 * side : 3 * side + 3], side == 1)
        right_steps = pairs_of(rights[3 * side : 3 * side + 3], side == 0)
        for micro in range(2):
            at = pl.ds(micro * tokens, tokens)
            loads.append(
                [
                    local.load_either(
                        at_first, left_steps[0][micro], left_steps[1][micro], left[side].at[:, at]
                    ),
                    local.load_either(
                        at_first, right_steps[0][micro], right_steps[1][micro], right[side].at[at]
                    ),
                ]
            )
    saves, number = [None, None], 0
    for side in range(sides):
        for micro in range(2):
            for load in loads[2 * side + micro]:
                load.wait()
        for block in range(right[side].shape[1] // blk):
            slot = number % 2
            if saves[slot] is not None:
                saves[slot].wait()
            at = pl.ds(block * blk, blk)
            held[slot] = dot_nn(left[side][...], right[side][:, at]).astype(bf16)
            saves[slot] = local.load(held.at[slot], out.at[:, pl.ds(number * blk, blk)])
            number += 1
    for save in saves:
        save.wait()


def pairs_of(steps, backward):
    early, late = (steps[0], steps[1]), (steps[1], steps[2])
    return (late, early) if backward else (early, late)


VMEM_SPEC = pl.BlockSpec(memory_space=pltpu.VMEM)
HBM_SPEC = pl.BlockSpec(memory_space=pltpu.HBM)


def shape(dims, kind):
    return jax.ShapeDtypeStruct(dims, kind)


def exchange_scratch(chunks, own, cols):
    return [
        pltpu.VMEM((chunks, 2 * own, cols), f32),
        pltpu.VMEM((chunks, 2 * own, cols), bf16),
        pltpu.VMEM((chunks, 2 * own, cols), bf16),
        pltpu.VMEM((chunks, own, cols), bf16),
        pltpu.VMEM((chunks, own, cols), bf16),
        pltpu.SemaphoreType.DMA((16,)),
        pltpu.SemaphoreType.DMA((9, chunks)),
        pltpu.SemaphoreType.DMA((9, chunks)),
    ]


def params(number=None):
    if number is None:
        return pltpu.CompilerParams(vmem_limit_bytes=62 * MIB)
    return pltpu.CompilerParams(
        vmem_limit_bytes=62 * MIB, collective_id=number, has_side_effects=True
    )


class Numbers(dict):
    def of(self, *key):
        return self.setdefault(key, len(self))


def spans_of(background):
    return tuple((first, count) for _, first, count in background)


def gather_shapes(background):
    return [shape((4, count, blocks[0].shape[1]), bf16) for blocks, _, count in background]


def cost(flops, size):
    return pl.CostEstimate(flops=int(flops), bytes_accessed=int(size), transcendentals=0)


def attn_forward(hidden, pack, model_gains, gains, tables, masks, spread, hold, carried, background, numbers):
    chunks, own, cols = hidden.shape
    tokens, q_width, width = 4 * own, pack.shape[1] // 3, gains.shape[1]
    moved = (chunks, tokens, cols) if spread or hold else (chunks * cols, tokens)
    carry, spans = carried is not None, spans_of(background)
    rows = shape((chunks, own, cols), bf16)
    return pl.pallas_call(
        functools.partial(attn_forward_kernel, width, spread, hold, spans, carry),
        in_specs=[HBM_SPEC] * (2 * len(spans) + carry) + [VMEM_SPEC, HBM_SPEC] + [VMEM_SPEC] * 2 + [HBM_SPEC] * 2,
        out_specs=[HBM_SPEC] * 5 + [VMEM_SPEC] + [HBM_SPEC] * (carry + len(spans)),
        out_shape=[
            shape(moved, bf16),
            shape((tokens, 2 * q_width), f32),
            shape((tokens, q_width // 2), bf16),
            shape((tokens, q_width), bf16),
            shape((chunks, own, cols), f32),
            rows,
        ]
        + [rows] * carry
        + gather_shapes(background),
        scratch_shapes=[
            pltpu.VMEM(tables.shape, f32),
            pltpu.VMEM(masks.shape, f32),
            pltpu.VMEM((chunks, tokens, cols), bf16),
            pltpu.VMEM(moved, bf16),
            pltpu.VMEM((tokens, 2 * q_width), f32),
            pltpu.VMEM((tokens, q_width // 2), bf16),
            pltpu.VMEM((tokens, q_width), bf16),
            pltpu.VMEM((chunks, own, cols), f32),
            pltpu.VMEM(pack.shape, bf16),
        ]
        + exchange_scratch(chunks, own, cols),
        compiler_params=params(numbers.of("attn_forward", hold, carry, spans)),
        cost_estimate=cost(2 * tokens * pack.size, pack.size * 2),
        name="attn_forward",
    )(*sum([list(blocks) for blocks, *_ in background], []), *([carried] if carry else []), hidden, pack, model_gains, gains, tables, masks)


def ffn_forward(rows, mixed, pack, hop, held_rows, background, numbers):
    chunks, own, cols = rows.shape
    tokens, units = 4 * own, pack.shape[1] // 3
    depth = chunks * cols
    spans, spread = spans_of(background), held_rows is not None
    return pl.pallas_call(
        functools.partial(ffn_forward_kernel, hop, spread, spans),
        in_specs=[HBM_SPEC] * (spread + 2 * len(spans)) + [VMEM_SPEC, HBM_SPEC, HBM_SPEC],
        out_specs=[HBM_SPEC] * 3 + [VMEM_SPEC] * (2 if hop else 1) + [HBM_SPEC] * (spread + len(spans)),
        out_shape=[
            shape((depth, tokens), bf16),
            shape((tokens, 2 * units), f32),
            shape((tokens, units), bf16),
        ]
        + [shape((chunks, own, cols), bf16)] * (2 if hop else 1)
        + [shape((chunks, tokens, cols), bf16)] * spread
        + gather_shapes(background),
        scratch_shapes=[
            pltpu.VMEM((chunks, tokens, cols), bf16),
            pltpu.VMEM((depth, tokens), bf16),
            pltpu.VMEM((chunks, own, cols), f32),
            pltpu.VMEM((tokens, units), bf16),
            pltpu.VMEM((tokens, 2 * units), f32),
            pltpu.VMEM(pack.shape, bf16),
        ]
        + exchange_scratch(chunks, own, cols),
        compiler_params=params(numbers.of("ffn_forward", hop, spread, spans)),
        cost_estimate=cost(2 * tokens * pack.size, pack.size * 2),
        name="ffn_forward",
    )(*([held_rows] if spread else []), *sum([list(blocks) for blocks, *_ in background], []), rows, mixed, pack)


def ffn_backward(rows, mixed, gate_up, pack, model_gains, spread, carried, background, numbers):
    chunks, own, cols = rows.shape
    tokens, units = 4 * own, pack.shape[1] // 3
    moved = (chunks, tokens, cols) if spread else (chunks * cols, tokens)
    carry, spans = carried is not None, spans_of(background)
    return pl.pallas_call(
        functools.partial(ffn_backward_kernel, spread, spans, carry),
        in_specs=[HBM_SPEC] * (2 * len(spans) + carry) + [VMEM_SPEC] + [HBM_SPEC] * 5 + [VMEM_SPEC],
        out_specs=[HBM_SPEC] * 2 + [VMEM_SPEC] * 3 + [HBM_SPEC] * (carry + len(spans)),
        out_shape=[
            shape(moved, bf16),
            shape((tokens, 2 * units), bf16),
            shape((chunks, own, cols), f32),
            shape((chunks, own, cols), bf16),
            shape((chunks, cols), f32),
        ]
        + [shape((chunks, own, cols), bf16)] * carry
        + gather_shapes(background),
        scratch_shapes=[
            pltpu.VMEM((chunks, tokens, cols), bf16),
            pltpu.VMEM(moved, bf16),
            pltpu.VMEM((chunks, own, cols), f32),
            pltpu.VMEM((tokens, 2 * units), bf16),
            pltpu.VMEM((tokens, 2 * units), f32),
            pltpu.VMEM((tokens, units), f32),
            pltpu.VMEM(pack.shape, bf16),
        ]
        + exchange_scratch(chunks, own, cols),
        compiler_params=params(numbers.of("ffn_backward", carry, spans)),
        cost_estimate=cost(2 * tokens * pack.size, pack.size * 2),
        name="ffn_backward",
    )(*sum([list(blocks) for blocks, *_ in background], []), *([carried] if carry else []), rows, *mixed, *gate_up, pack, model_gains)


def attn_backward(
    rows, grad_mixed, hidden, projected, values, pack, model_gains, gains, tables, masks, spread, hop,
    background, numbers
):
    chunks, own, cols = rows.shape
    tokens, q_width, width = 4 * own, pack.shape[1] // 3, gains.shape[1]
    moved = (chunks, tokens, cols) if spread else (chunks * cols, tokens)
    spans = spans_of(background)
    return pl.pallas_call(
        functools.partial(attn_backward_kernel, width, spread, spans, hop),
        in_specs=[HBM_SPEC] * (2 * len(spans)) + [VMEM_SPEC] * 2 + [HBM_SPEC] * 7 + [VMEM_SPEC] * 2 + [HBM_SPEC] * 2,
        out_specs=[HBM_SPEC] * 2 + [VMEM_SPEC] * (4 if hop else 3) + [HBM_SPEC] * len(spans),
        out_shape=[
            shape(moved, bf16),
            shape((tokens, 2 * q_width), bf16),
            shape((chunks, own, cols), bf16),
            shape((chunks, cols), f32),
            shape((8, width), f32),
        ]
        + [shape((chunks, own, cols), bf16)] * (1 if hop else 0)
        + gather_shapes(background),
        scratch_shapes=[
            pltpu.VMEM(tables.shape, f32),
            pltpu.VMEM(masks.shape, f32),
            pltpu.VMEM((chunks, tokens, cols), bf16),
            pltpu.VMEM(moved, bf16),
            pltpu.VMEM((tokens, 2 * q_width), bf16),
            pltpu.VMEM((chunks, own, cols), bf16),
            pltpu.VMEM((tokens, 2 * q_width), f32),
            pltpu.VMEM((tokens, q_width // 2), bf16),
            pltpu.VMEM((tokens, q_width), f32),
            pltpu.VMEM((chunks, own, cols), f32),
            pltpu.VMEM(pack.shape, bf16),
        ]
        + exchange_scratch(chunks, own, cols),
        compiler_params=params(numbers.of("attn_backward", hop, spans)),
        cost_estimate=cost(2 * tokens * pack.size, pack.size * 2),
        name="attn_backward",
    )(
        *sum([list(blocks) for blocks, *_ in background], []), rows, grad_mixed, *hidden, *projected, *values, pack, model_gains, gains, tables, masks
    )


def weight_grad(lefts, rights):
    depth, tokens = lefts[0][0].shape
    blk = 512
    widths = [right[0].shape[1] for right in rights]
    return pl.pallas_call(
        functools.partial(weight_grad_kernel, blk, len(lefts)),
        in_specs=[HBM_SPEC] * (6 * len(lefts)),
        out_specs=HBM_SPEC,
        out_shape=shape((depth, sum(widths)), bf16),
        scratch_shapes=[pltpu.VMEM((depth, 2 * tokens), bf16) for _ in lefts]
        + [pltpu.VMEM((2 * tokens, width), bf16) for width in widths]
        + [
            pltpu.VMEM((2, depth, blk), bf16),
            pltpu.SemaphoreType.DMA((4 * len(lefts) + sum(widths) // blk,)),
        ],
        compiler_params=params(),
        cost_estimate=cost(4 * depth * tokens * sum(widths), 2 * depth * sum(widths)),
        name="weight_grad",
    )(*sum(lefts, []), *sum(rights, []))


def rope_tables(position, head_width):
    exponent = jnp.arange(0, head_width, 2).astype(f32) / head_width
    inverse = rope_base ** (-exponent)
    angles = position.astype(f32)[:, None] * inverse[None, :]
    cosine, sine = jnp.cos(angles), jnp.sin(angles)
    return (
        jnp.concatenate([cosine, cosine], axis=-1),
        jnp.concatenate([-sine, sine], axis=-1),
    )


def per_device(
    block_input,
    segment_ids,
    out_cotangent,
    attn_norm,
    q_weight,
    k_weight,
    v_weight,
    o_weight,
    q_norm,
    k_norm,
    ffn_norm,
    gate_weight,
    up_weight,
    down_weight,
):
    section = lax.axis_index("section")
    place = lax.axis_index("dp")
    core = place % 2
    half = lax.axis_index("tensor")
    n_dp = lax.axis_size("dp")
    n_chip = n_dp // 2
    micro_count, own_rows, depth = block_input.shape
    length = 2 * own_rows
    head_width = q_norm.shape[1]
    first_core = core == 0
    swap_core = [(i, i ^ 1) for i in range(n_dp)]
    swap_half = [(0, 1), (1, 0)]
    chip_groups = [[2 * chip + one for chip in range(n_chip)] for one in (0, 1)]

    def to_core(values):
        return lax.ppermute(values, "dp", swap_core)

    def to_half(values):
        return lax.ppermute(values, "tensor", swap_half)

    def split_columns(weight):
        side = weight.shape[1] // 2
        left, right = weight[:, :side], weight[:, side:]
        return jnp.where(first_core, left, right), jnp.where(first_core, right, left)

    def split_rows(weight):
        side = weight.shape[0] // 2
        left, right = weight[:side].T, weight[side:].T
        return jnp.where(first_core, left, right), jnp.where(first_core, right, left)

    def chip_block(pairs):
        mine = jnp.concatenate([pair[0] for pair in pairs], axis=1)
        theirs = to_core(jnp.concatenate([pair[1] for pair in pairs], axis=1))
        return jnp.concatenate(
            [jnp.where(first_core, mine, theirs), jnp.where(first_core, theirs, mine)], axis=0
        )

    def gathered(block):
        return lax.all_gather(block, "dp", axis=0, tiled=True, axis_index_groups=chip_groups)

    square = n_chip == row_chunks
    numbers = Numbers()
    attn_block = chip_block(
        [
            split_columns(q_weight[0]),
            split_columns(k_weight[0]),
            split_columns(v_weight[0]),
            split_rows(o_weight[0]),
        ]
    )
    ffn_block = chip_block(
        [split_columns(gate_weight[0]), split_columns(up_weight[0]), split_rows(down_weight[0])]
    )
    if square:
        attn_block, ffn_block = lax.optimization_barrier((attn_block, ffn_block))
        attn_pack = chip_gather([attn_block], numbers.of("chip_gather", 0)).reshape(depth, -1)
    else:
        attn_pack = gathered(attn_block)
    ffn_pack = gathered(ffn_block)

    cols = depth // row_chunks
    model_gains = jnp.concatenate([attn_norm, ffn_norm], axis=0).reshape(2, row_chunks, cols)
    head_gains = jnp.concatenate([q_norm, k_norm, jnp.zeros((6, head_width), f32)], axis=0)

    def chunked(rows):
        return rows.reshape(rows.shape[0], row_chunks, cols).transpose(1, 0, 2)

    def joined(rows):
        return rows.transpose(1, 0, 2).reshape(rows.shape[1], depth)

    inputs = [chunked(block_input[micro]) for micro in range(2)]
    cotangents = [chunked(out_cotangent[micro]) for micro in range(2)]

    def arranged(values):
        sides = values[..., :own_rows], values[..., own_rows:]
        return jnp.concatenate(
            [jnp.where(half == 0, *sides), jnp.where(half == 0, *sides[::-1])], axis=-1
        )

    position = arranged(jnp.arange(length, dtype=jnp.int32))
    tables = jnp.stack(rope_tables(position, head_width))
    ids = arranged(jnp.stack([segment_ids, to_core(segment_ids)], axis=1))
    causal = position[:, None] >= position[None, :]
    masks = (causal & (ids[..., :, None] == ids[..., None, :])).astype(f32)

    at_first = section == 0

    def pick(first, second):
        return jax.tree.map(lambda a, b: jnp.where(at_first, a, b), first, second)

    zero_rows = jnp.zeros_like(inputs[0])
    forward_masks = [masks[0], pick(masks[1], masks[0]), masks[1]]
    backward_masks = [masks[0], pick(masks[0], masks[1]), masks[1]]
    results, backs, saves = [], [], []
    grads, ffn_saves, attn_saves, gains = [], [], [], []

    def forward_step(step, arrived, hop, carried=None, attn_work=(), ffn_work=()):
        hidden = inputs[step] if step < 2 else zero_rows
        if step > 0:
            hidden = pick(hidden, arrived)
        turned_in, projected, values, attended, mixed, rows, *more = attn_forward(
            hidden, attn_pack, model_gains, head_gains, tables, forward_masks[step],
            square and step > 0, square and step == 0, carried, attn_work, numbers,
        )
        turned_mid, gate_up, activated, result, *rest = ffn_forward(
            rows, mixed, ffn_pack, hop, turned_in if square and step == 0 else None, ffn_work, numbers
        )
        if square and step == 0:
            turned_in = rest.pop(1)
        results.append(result)
        backs.append((hidden, projected, values, mixed, gate_up))
        saves.append((turned_in, attended, turned_mid, activated))
        return more + rest

    def back_ffn(step, arrived, carried=None, work=()):
        rows = pick(arrived, cotangents[step] if step < 2 else zero_rows)
        *_, mixed, gate_up = zip(backs[0], backs[2]) if step == 1 else zip(backs[1], backs[1])
        turned_rows, ffn_grads, grad_mixed, proj_rows, gain_grad, *more = ffn_backward(
            rows, mixed, gate_up, ffn_pack, model_gains, square, carried, work, numbers
        )
        ffn_saves.append((turned_rows, ffn_grads))
        return (proj_rows, grad_mixed, gain_grad), more

    def back_attn(step, proj_rows, grad_mixed, ffn_gain_grad, hop, work=()):
        hidden, projected, values, *_ = (
            zip(backs[0], backs[2]) if step == 1 else zip(backs[1], backs[1])
        )
        turned_rows, attn_grads, grad_hidden, attn_gain_grad, head_gain_grads, *rest = attn_backward(
            proj_rows, grad_mixed, hidden, projected, values, attn_pack, model_gains, head_gains,
            tables, backward_masks[step], square, hop, work, numbers,
        )
        attn_saves.append((turned_rows, attn_grads))
        grads.append(grad_hidden)
        gains.append((attn_gain_grad, ffn_gain_grad, head_gain_grads))
        return rest

    def column(table, item):
        return [row[item] for row in table]

    def work(*items):
        return items if square else ()

    def of_micro(micro, item):
        return saves[micro][item], saves[micro + 1][item]

    tokens = 2 * length
    (arrived,) = forward_step(0, zero_rows, True)
    forward_step(1, arrived, False)
    active, attended = of_micro(0, 3), of_micro(0, 1)
    part = tokens // 4
    others, (arrived, *pieces) = back_ffn(0, zero_rows, results[1], work((active, 0, part)))
    active_pieces = [(0, pieces)]
    pieces = back_attn(0, *others, False, work((active, part, part)))
    active_pieces.append((part, pieces))
    grad_arrived, *pieces = forward_step(
        2, arrived, False, grads[0], work((active, 2 * part, part)),
        work((active, 3 * part, part), (attended, 0, tokens)),
    )
    active_pieces += [(2 * part, pieces[:1]), (3 * part, pieces[1:2])]
    attended_all = [pieces[2:]]
    active, attended = of_micro(1, 3), of_micro(1, 1)
    side = tokens // 2
    grad_arrived, results[2] = lax.optimization_barrier((grad_arrived, results[2]))
    others, pieces = back_ffn(1, grad_arrived, None, work((active, 0, side)))
    late_pieces = [(0, pieces)]
    grad_arrived, *pieces = back_attn(
        1, *others, True, work((active, side, side), (attended, 0, tokens))
    )
    late_pieces.append((side, pieces[:1]))
    attended_all.append(pieces[1:])
    early_block = attn_saves[1][1], attn_saves[0][1]
    (proj_rows, *others), early_grads = back_ffn(2, grad_arrived, None, work((early_block, 0, tokens)))
    if square:
        ffn_partial = weight_grad([column(saves, 2)], [column(ffn_saves, 1)])
    else:
        ffn_partial = weight_grad(
            [column(saves, 2), column(ffn_saves, 0)], [column(ffn_saves, 1), column(saves, 3)]
        )
    proj_rows, ffn_partial = lax.optimization_barrier((proj_rows, ffn_partial))
    back_attn(2, proj_rows, *others, False)
    if not square:
        attn_partial = weight_grad(
            [column(saves, 0), column(attn_saves, 0)], [column(attn_saves, 1), column(saves, 1)]
        )
    gain_total = functools.reduce(lambda a, b: jax.tree.map(jnp.add, a, b), gains)

    section_outputs = jnp.stack(
        [joined(pick(results[micro], results[micro + 1])) for micro in range(2)]
    )[None]
    section_input_grads = jnp.stack(
        [joined(pick(grads[micro + 1], grads[micro])) for micro in range(2)]
    )[None]

    def scattered(partial):
        return lax.psum_scatter(
            partial, "dp", scatter_dimension=0, tiled=True, axis_index_groups=chip_groups
        )

    def owned(rows):
        side = rows.shape[0] // 2
        own = jnp.where(first_core, rows[:side], rows[side:])
        other = to_core(jnp.where(first_core, rows[side:], rows[:side]))
        return (
            jnp.where(first_core, own, other).astype(f32),
            jnp.where(first_core, other, own).astype(f32),
        )

    units = gate_weight.shape[2] // 2
    if square:
        late_grads = chip_gather([attn_saves[2][1], attn_saves[1][1]], numbers.of("chip_gather", 1))

        def flat(rows):
            return rows.reshape(-1, rows.shape[-1])

        def summed(rows, pieces):
            return sum(
                dot_tn(flat(rows[:, first : first + piece.shape[1]]), flat(piece))
                for first, (piece,) in pieces
            )

        def forward_rows(micro):
            return pick(saves[micro][0], saves[micro + 1][0])

        def backward_rows(table, micro):
            return pick(table[micro + 1][0], table[micro][0])

        down_sides = owned(
            summed(backward_rows(ffn_saves, 0), active_pieces)
            + summed(backward_rows(ffn_saves, 1), late_pieces)
        )
        o_rows = sum(
            summed(backward_rows(attn_saves, micro), [(0, attended_all[micro])])
            for micro in range(2)
        )
        qkv_rows = summed(forward_rows(0), [(0, early_grads)]) + summed(
            forward_rows(1), [(0, [late_grads])]
        )
        attn_sides = owned(jnp.concatenate([qkv_rows, o_rows], axis=1))
        ffn_sides = owned(scattered(ffn_partial))
    else:
        attn_partial, ffn_rows = lax.optimization_barrier((attn_partial, scattered(ffn_partial)))
        ffn_sides = owned(ffn_rows)
        attn_sides = owned(scattered(attn_partial))
        down_sides = [side[:, 2 * units :] for side in ffn_sides]
    q_width = q_weight.shape[2] // 2
    kv_width = k_weight.shape[2] // 2

    def across(sides, first, width):
        return jnp.concatenate([side[:, first : first + width] for side in sides], axis=1)[None]

    def down(sides, first):
        return jnp.concatenate([side[:, first:].T for side in sides], axis=0)[None]

    packed = jnp.concatenate(
        [
            gain_total[0].reshape(-1),
            gain_total[1].reshape(-1),
            gain_total[2][0],
            gain_total[2][1],
        ]
    ).reshape(-1, head_width)
    packed = packed + to_core(packed)
    packed = packed + to_half(packed)
    reach = 2
    while reach < n_dp:
        packed = packed + lax.ppermute(packed, "dp", [(i, i ^ reach) for i in range(n_dp)])
        reach *= 2
    packed = packed.reshape(-1)
    return (
        section_outputs,
        section_input_grads,
        packed[None, :depth],
        across(attn_sides, 0, q_width),
        across(attn_sides, q_width, kv_width),
        across(attn_sides, q_width + kv_width, kv_width),
        down(attn_sides, 2 * q_width),
        packed[None, 2 * depth : 2 * depth + head_width],
        packed[None, 2 * depth + head_width :],
        packed[None, depth : 2 * depth],
        across(ffn_sides, 0, units),
        across(ffn_sides, units, units),
        down(down_sides, 0),
    )


def solution(mesh):
    rows = P(None, ("dp", "tensor"), None)
    out_rows = P("section", None, ("dp", "tensor"), None)
    gain = P("section", None)
    wide = P("section", "dp", "tensor")
    tall = P("section", "tensor", "dp")
    return jax.shard_map(
        per_device,
        mesh=mesh,
        in_specs=(
            rows, P(None, "dp"), rows, gain, wide, wide, wide, tall, gain, gain, gain, wide, wide, tall,
        ),
        out_specs=(
            out_rows, out_rows, gain, wide, wide, wide, tall, gain, gain, gain, wide, wide, tall,
        ),
        check_vma=False,
    )
```

```python
import functools

import jax
import jax.numpy as jnp
from jax import lax
from jax.experimental import pallas as pl
from jax.experimental.pallas import tpu as pltpu
from jax.sharding import PartitionSpec as P

norm_eps = 1e-06
rope_base = 1000000.0
masked_score = -1e30
row_chunks = 4
background_size = 4 * 384 * 960
f32 = jnp.float32
bf16 = jnp.bfloat16
MIB = 1024 * 1024
MESH = pl.DeviceIdType.MESH


def dot_nn(left, right):
    return lax.dot_general(left, right, (((1,), (0,)), ((), ())), preferred_element_type=f32)


def dot_nt(left, right):
    return lax.dot_general(left, right, (((1,), (1,)), ((), ())), preferred_element_type=f32)


def dot_tn(left, right):
    return lax.dot_general(left, right, (((0,), (0,)), ((), ())), preferred_element_type=f32)


def inverse_rms(values):
    return lax.rsqrt(jnp.mean(values * values, axis=-1, keepdims=True) + norm_eps)


def norm_back(grad_out, values, inverse, gain_vec):
    scaled = grad_out * gain_vec
    return inverse * (
        scaled - values * inverse * inverse * jnp.mean(scaled * values, axis=-1, keepdims=True)
    )


class Exchange:
    def __init__(self, send_sems, recv_sems):
        place = lax.axis_index("dp")
        self.core = {"dp": place + 1 - 2 * (place % 2)}
        self.half = {"tensor": 1 - lax.axis_index("tensor")}
        self.section = {"section": 1 - lax.axis_index("section")}
        core, chip = place % 2, place // 2
        across, along = chip % 2, chip // 2
        self.chip = chip
        numbers = (chip + 1 - 2 * across, chip + 2 - 4 * along, 3 - chip)
        self.chips = [(number, {"dp": 2 * number + core}) for number in numbers]
        self.send_sems, self.recv_sems = send_sems, recv_sems

    def greet(self, with_section, with_chips):
        others = [self.core, self.half] + ([self.section] if with_section else [])
        self.meet(others + [device for _, device in self.chips[:with_chips]])

    def meet(self, others):
        barrier = pltpu.get_barrier_semaphore()
        for other in others:
            pl.semaphore_signal(barrier, inc=1, device_id=other, device_id_type=MESH)
        pl.semaphore_wait(barrier, len(others))

    def copy(self, source, target, other, stage, chunk):
        return pltpu.make_async_remote_copy(
            src_ref=source,
            dst_ref=target,
            send_sem=self.send_sems.at[stage, chunk],
            recv_sem=self.recv_sems.at[stage, chunk],
            device_id=other,
            device_id_type=MESH,
        )


def gather_then(exchange, rows, use):
    chunks, total, _ = rows.shape
    own = total // 4
    first = [
        exchange.copy(rows.at[c, pl.ds(0, own)], rows.at[c, pl.ds(own, own)], exchange.half, 0, c)
        for c in range(chunks)
    ]
    second = [
        exchange.copy(
            rows.at[c, pl.ds(0, 2 * own)], rows.at[c, pl.ds(2 * own, 2 * own)], exchange.core, 1, c
        )
        for c in range(chunks)
    ]
    for c in range(chunks):
        first[c].start()
    for c in range(chunks):
        first[c].wait_recv()
        second[c].start()
        if c > 0:
            second[c - 1].wait_recv()
            use(c - 1)
    second[chunks - 1].wait_recv()
    use(chunks - 1)
    return first + second


def scatter_from(exchange, make, idle, finish, keep, send_core, recv_core, send_half, recv_half):
    chunks, pair, _ = keep.shape
    own = pair // 2
    first = [
        exchange.copy(send_core.at[c], recv_core.at[c], exchange.core, 2, c) for c in range(chunks)
    ]
    second = [
        exchange.copy(send_half.at[c], recv_half.at[c], exchange.half, 3, c) for c in range(chunks)
    ]

    def middle(c):
        first[c].wait_recv()
        summed = keep[c] + recv_core[c].astype(f32)
        send_half[c] = summed[own:].astype(bf16)
        second[c].start()
        keep[c, :own] = summed[:own]

    for c in range(chunks):
        product = make(c)
        send_core[c] = product[pair:].astype(bf16)
        first[c].start()
        keep[c] = product[:pair]
        if c > 0:
            middle(c - 1)
    middle(chunks - 1)
    for c in range(chunks):
        idle(c)
        second[c].wait_recv()
        finish(c, keep[c, :own] + recv_half[c].astype(f32))
    return first + second


class ChipGather:
    def __init__(self, exchange, local, blocks, out, stage):
        (across, across_device), (along, along_device), _ = exchange.chips
        at_first = lax.axis_index("section") == 0
        half = blocks[0].shape[0] // 2
        first, last = pl.ds(0, half), pl.ds(half, half)
        target = out.at[exchange.chip]
        choices = [
            [
                exchange.copy(block, target, across_device, stage, 0),
                exchange.copy(block, target, along_device, stage, 1),
            ]
            for block in blocks
        ]
        self.direct = choices[0]
        self.passed = [
            exchange.copy(out.at[across, first], out.at[across, first], along_device, stage, 2),
            exchange.copy(out.at[along, last], out.at[along, last], across_device, stage, 3),
        ]
        for index, block in enumerate(blocks):
            here = at_first if index == 0 else jnp.logical_not(at_first)

            def start(index=index):
                for copy in choices[index]:
                    copy.start()

            if len(blocks) > 1:
                pl.when(here)(start)
            else:
                start()

        if len(blocks) > 1:
            local.saves.append(local.load_either(at_first, *blocks, target))
        else:
            local.save(blocks[0], target)

    def pass_on(self):
        for copy, onward in zip(self.direct, self.passed):
            copy.wait_recv()
            onward.start()

    def finish(self):
        for copy in self.passed:
            copy.wait_recv()
        return self.direct + self.passed


class Background:
    def __init__(self, exchange, local, spans, sources, targets):
        self.gathers = [
            ChipGather(
                exchange,
                local,
                [source.at[pl.ds(first, count)] for source in sources[2 * index : 2 * index + 2]],
                target,
                7 + index,
            )
            for index, ((first, count), target) in enumerate(zip(spans, targets))
        ]

        long = sum(target.size for target in targets) > background_size
        self.late = [long and index > 0 for index in range(len(targets))]

    def pass_on(self, late):
        for gather, when in zip(self.gathers, self.late):
            if when == late:
                gather.pass_on()

    def finish(self):
        return sum([gather.finish() for gather in self.gathers], [])


def chip_gather_kernel(*refs):
    *blocks, out, local_sems, send_sems, recv_sems = refs
    exchange, local = Exchange(send_sems, recv_sems), Local(local_sems)
    exchange.meet([device for _, device in exchange.chips[:2]])
    gather = ChipGather(exchange, local, blocks, out, 0)
    gather.pass_on()
    for copy in gather.finish():
        copy.wait_send()
    local.finish()


def chip_gather(blocks, number):
    return pl.pallas_call(
        chip_gather_kernel,
        in_specs=[HBM_SPEC] * len(blocks),
        out_specs=HBM_SPEC,
        out_shape=shape((4,) + blocks[0].shape, bf16),
        scratch_shapes=[
            pltpu.SemaphoreType.DMA((1,)),
            pltpu.SemaphoreType.DMA((1, 4)),
            pltpu.SemaphoreType.DMA((1, 4)),
        ],
        compiler_params=params(number),
        cost_estimate=cost(0, 300 * blocks[0].size),
        name="chip_gather",
    )(*blocks)


def core_swap_kernel(rows, out, send_sems, recv_sems):
    exchange = Exchange(send_sems, recv_sems)
    exchange.meet([exchange.core])
    side = out.shape[0]
    theirs = pl.multiple_of((1 - lax.axis_index("dp") % 2) * side, side)
    copy = exchange.copy(rows.at[pl.ds(theirs, side)], out, exchange.core, 0, 0)
    copy.start()
    copy.wait()


def core_swap(rows, number):
    side = rows.shape[0] // 2
    return pl.pallas_call(
        core_swap_kernel,
        in_specs=[HBM_SPEC],
        out_specs=HBM_SPEC,
        out_shape=shape((side, rows.shape[1]), rows.dtype),
        scratch_shapes=[pltpu.SemaphoreType.DMA((1, 1)), pltpu.SemaphoreType.DMA((1, 1))],
        compiler_params=params(number),
        cost_estimate=cost(0, 10 * rows.size),
        name="core_swap",
    )(rows)


def place_kernel(wide, *refs):
    rows, other, refs = refs[0], refs[1], refs[2:]
    outs, (mine, theirs, *staged, local_sems) = refs[: len(wide)], refs[len(wide) :]
    local = Local(local_sems)
    core = lax.axis_index("dp") % 2
    side = other.shape[0]
    loads = [
        local.load(rows.at[pl.ds(pl.multiple_of(core * side, side), side)], mine),
        local.load(other, theirs),
    ]
    for load in loads:
        load.wait()
    for index, (source, place) in enumerate(((mine, core), (theirs, 1 - core))):
        first = 0
        for number, ((width, turned), out) in enumerate(zip(wide, outs)):
            stage = staged[number].at[index]
            block = source[:, first : first + width].astype(f32)
            at = pl.ds(pl.multiple_of(place * width, width), width)
            if turned:
                staged[number][index] = block.T
                local.save(stage, out.at[at, :])
            else:
                staged[number][index] = block
                local.save(stage, out.at[:, at])
            first += width
    local.finish()


def place_parts(rows, other, wide):
    side = other.shape[0]
    return pl.pallas_call(
        functools.partial(place_kernel, wide),
        in_specs=[HBM_SPEC] * 2,
        out_specs=[HBM_SPEC] * len(wide),
        out_shape=[
            shape((2 * width, side) if turned else (side, 2 * width), f32)
            for width, turned in wide
        ],
        scratch_shapes=[pltpu.VMEM(other.shape, other.dtype)] * 2
        + [
            pltpu.VMEM((2, width, side) if turned else (2, side, width), f32)
            for width, turned in wide
        ]
        + [pltpu.SemaphoreType.DMA((2 + 2 * len(wide),))],
        compiler_params=params(),
        cost_estimate=cost(0, 12 * other.size),
        name="place",
    )(rows, other)


def load_pack(pack, held, local):
    depth = held.shape[0] // row_chunks
    return [
        local.load(pack.at[pl.ds(c * depth, depth)], held.at[pl.ds(c * depth, depth)])
        for c in range(row_chunks)
    ]


class Local:
    def __init__(self, sems):
        self.sems, self.used, self.saves = sems, 0, []

    def copy(self, source, target):
        self.used += 1
        return pltpu.make_async_copy(source, target, self.sems.at[self.used - 1])

    def load(self, source, target):
        copy = self.copy(source, target)
        copy.start()
        return copy

    def load_either(self, at_first, first, second, target):
        one = self.copy(first, target)
        other = pltpu.make_async_copy(second, target, self.sems.at[self.used - 1])

        @pl.when(at_first)
        def _():
            one.start()

        @pl.when(jnp.logical_not(at_first))
        def _():
            other.start()

        return one

    def save(self, source, target):
        self.saves.append(self.load(source, target))

    def finish(self):
        for copy in self.saves:
            copy.wait()


def row_mean(values):
    size = values.shape[0] * values.shape[2]
    return jnp.sum(jnp.sum(values, axis=0), axis=-1, keepdims=True)[None] * (1.0 / size)


def accumulate(total, left, weights, first_row, first_col, width, start):
    depth = left.shape[1]
    blk = 512 if width % 512 == 0 else 256

    def body(index, _):
        at = pl.multiple_of(index * blk, blk)
        product = dot_nn(left, weights[pl.ds(first_row, depth), pl.ds(first_col + at, blk)])
        if start:
            total[:, pl.ds(at, blk)] = product
        else:
            total[:, pl.ds(at, blk)] += product
        return 0

    lax.fori_loop(0, width // blk, body, 0)


def rotated(raw, gain, cosine, signed_sine):
    inverse = inverse_rms(raw)
    scaled = raw * inverse * gain
    turned = scaled * cosine + pltpu.roll(scaled, 64, 1) * signed_sine
    return inverse, turned.astype(bf16)


def softmax_rows(query_rot, key_rot, allowed, scale):
    scores = jnp.where(allowed, dot_nt(query_rot, key_rot) * scale, masked_score)
    exponent = jnp.exp(scores - jnp.max(scores, axis=-1, keepdims=True))
    return exponent / jnp.sum(exponent, axis=-1, keepdims=True)


class Spread:
    def __init__(self, exchange, local, rows, moved):
        side = rows.shape[1] // 2
        self.own = local.load(rows.at[exchange.chip], moved.at[exchange.chip])
        self.arrivals, self.onward = [], []
        for index, (number, device) in enumerate(exchange.chips):
            self.arrivals.append(
                exchange.copy(
                    rows.at[number, pl.ds(0, side)],
                    moved.at[exchange.chip, pl.ds(0, side)],
                    device, 5, index,
                )
            )
            self.arrivals[-1].start()
            self.onward.append(
                exchange.copy(
                    moved.at[number, pl.ds(0, side)],
                    moved.at[number, pl.ds(side, side)],
                    exchange.core, 6, index,
                )
            )

    def pass_on(self, index):
        self.arrivals[index].wait_recv()
        self.onward[index].start()

    def finish(self):
        self.own.wait()
        for copy in self.onward:
            copy.wait_recv()
        return self.arrivals + self.onward


def turn_chunk(rows, target, c):
    cols = rows.shape[2]
    target[pl.ds(c * cols, cols), :] = rows[c].T


def attn_forward_kernel(
    width, spread, hold, spans, carry, *refs
):
    sources, refs = refs[: 2 * len(spans)], refs[2 * len(spans) :]
    if carry:
        carried, refs = refs[0], refs[1:]
    (
        hidden_in, pack, model_gains_in, gains_in, tables_in, masks_in,
        moved_out, projected_out, values_out, attended_out, mixed_out, normed_ffn_rows,
    ), refs = refs[:12], refs[12:]
    if carry:
        arrived, refs = refs[0], refs[1:]
    targets, refs = refs[: len(spans)], refs[len(spans) :]
    (
        hidden, model_gains, gains, tables, masks, normed, moved, projected, values, attended, mixed,
        held, keep, send_core, recv_core, send_half, recv_half, local_sems, send_sems, recv_sems,
    ) = refs
    exchange, local = Exchange(send_sems, recv_sems), Local(local_sems)
    first = [
        local.load(hidden_in, hidden),
        local.load(model_gains_in, model_gains),
        local.load(gains_in, gains),
    ]
    loads = load_pack(pack, held, local)
    exchange.greet(carry, (3 if spread else 2 if spans else 0))
    background = Background(exchange, local, spans, sources, targets)
    extra = [local.load(tables_in, tables), local.load(masks_in, masks)]
    chunks, own, cols = hidden.shape
    length = 2 * own
    q_width = attended.shape[1]
    kv_width = q_width // 2
    kv_heads = kv_width // width
    group = q_width // kv_width
    for load in first:
        load.wait()
    rows = hidden[...].astype(f32)
    inverse = lax.rsqrt(row_mean(rows * rows) + norm_eps)
    for c in range(chunks):
        normed[c, :own] = (rows[c] * inverse[0] * model_gains[0, c][None, :]).astype(bf16)

    def project(c):
        loads[c].wait()
        accumulate(projected, normed[c], held, c * cols, 0, 2 * q_width, c == 0)

    copies = gather_then(exchange, normed, project)
    moving = Spread(exchange, local, normed, moved) if spread else None
    hops = []
    if carry:
        hops = [exchange.copy(carried, arrived, exchange.section, 4, 0)]
        hops[0].start()
    local.save(projected, projected_out)
    for load in extra:
        load.wait()
    cos, sin = tables[0], tables[1]
    gain_q, gain_k = gains[0:1, :], gains[1:2, :]
    scale = width ** (-0.5)
    values[...] = projected[:, q_width + kv_width :].astype(bf16)
    local.save(values, values_out)
    for seq in range(2):
        at = slice(seq * length, (seq + 1) * length)
        allowed = masks[seq] > 0.5
        for kv in range(kv_heads):
            raw_k = projected[at, q_width + kv * width : q_width + (kv + 1) * width]
            value = values[at, kv * width : (kv + 1) * width]
            _, key_rot = rotated(raw_k, gain_k, cos, sin)
            for one in range(group):
                head = slice((kv * group + one) * width, (kv * group + one + 1) * width)
                _, query_rot = rotated(projected[at, head], gain_q, cos, sin)
                weights = softmax_rows(query_rot, key_rot, allowed, scale)
                attended[at, head] = dot_nn(weights.astype(bf16), value).astype(bf16)
    local.save(attended, attended_out)
    background.pass_on(False)

    def make(c):
        return dot_nt(attended[...], held[c * cols : (c + 1) * cols, 2 * q_width :])

    def idle(c):
        if not (spread or hold):
            turn_chunk(normed, moved, c)
        elif spread and c > 0:
            moving.pass_on(c - 1)
        if c == chunks - 2:
            background.pass_on(True)

    def finish(c, summed):
        mixed[c] = hidden[c].astype(f32) + summed

    copies += scatter_from(
        exchange, make, idle, finish, keep, send_core, recv_core, send_half, recv_half
    )
    if spread:
        copies += moving.finish()
    local.save(normed if hold else moved, moved_out)
    local.save(mixed, mixed_out)
    rows = mixed[...]
    inverse = lax.rsqrt(row_mean(rows * rows) + norm_eps)
    for c in range(chunks):
        normed_ffn_rows[c] = (rows[c] * inverse[0] * model_gains[1, c][None, :]).astype(bf16)
    for copy in hops:
        copy.wait()
    copies += background.finish()
    for copy in copies:
        copy.wait_send()
    local.finish()


def ffn_forward_kernel(
    hop, spread, spans, *refs
):
    if spread:
        held_rows, refs = refs[0], refs[1:]
    sources, refs = refs[: 2 * len(spans)], refs[2 * len(spans) :]
    rows, mixed_in, pack, turned_out, gate_up_out, activated_out, result, *rest = refs
    if hop:
        arrived, rest = rest[0], rest[1:]
    if spread:
        moved, rest = rest[0], rest[1:]
    targets, rest = rest[: len(spans)], rest[len(spans) :]
    (
        normed, turned, mixed, activated, total,
        held, keep, send_core, recv_core, send_half, recv_half, local_sems, send_sems, recv_sems,
    ) = rest
    exchange, local = Exchange(send_sems, recv_sems), Local(local_sems)
    own = rows.shape[1]
    first = local.load(rows, normed.at[:, pl.ds(0, own)])
    loads = load_pack(pack, held, local)
    exchange.greet(hop, 3 if spread else 2 if spans else 0)
    moving = Spread(exchange, local, held_rows, moved) if spread else None
    background = Background(exchange, local, spans, sources, targets)
    mixed_load = local.load(mixed_in, mixed)
    chunks, own, cols = rows.shape
    units = activated.shape[1]
    first.wait()

    def project(c):
        loads[c].wait()
        accumulate(total, normed[c], held, c * cols, 0, 2 * units, c == 0)

    copies = gather_then(exchange, normed, project)
    local.save(total, gate_up_out)
    blk = 256

    def activate(index, _):
        at = pl.multiple_of(index * blk, blk)
        gate = total[:, pl.ds(at, blk)]
        upward = total[:, pl.ds(units + at, blk)]
        activated[:, pl.ds(at, blk)] = (gate * jax.nn.sigmoid(gate) * upward).astype(bf16)
        return 0

    lax.fori_loop(0, units // blk, activate, 0)
    local.save(activated, activated_out)
    background.pass_on(False)
    mixed_load.wait()
    hops = []

    def make(c):
        return dot_nt(activated[...], held[c * cols : (c + 1) * cols, 2 * units :])

    def idle(c):
        turn_chunk(normed, turned, c)
        if spread and c > 0:
            moving.pass_on(c - 1)
        if c == chunks - 2:
            background.pass_on(True)

    def finish(c, summed):
        result[c] = (mixed[c] + summed).astype(bf16)
        if hop:
            hops.append(exchange.copy(result.at[c], arrived.at[c], exchange.section, 4, c))
            hops[-1].start()

    copies += scatter_from(
        exchange, make, idle, finish, keep, send_core, recv_core, send_half, recv_half
    )
    local.save(turned, turned_out)
    for copy in hops:
        copy.wait()
    copies += background.finish()
    if spread:
        copies += moving.finish()
    for copy in copies:
        copy.wait_send()
    local.finish()


def ffn_backward_kernel(spread, spans, carry, *refs):
    sources, refs = refs[: 2 * len(spans)], refs[2 * len(spans) :]
    if carry:
        carried, refs = refs[0], refs[1:]
    (
        rows, mixed_a, mixed_b, gate_up_a, gate_up_b, pack, model_gains_in,
        moved_out, grads_out, grad_mixed, grad_proj_rows, gain_grad,
    ), refs = refs[:12], refs[12:]
    if carry:
        arrived, refs = refs[0], refs[1:]
    targets, refs = refs[: len(spans)], refs[len(spans) :]
    (
        model_gains, grad_down, moved, mixed, grads, pre, total,
        held, keep, send_core, recv_core, send_half, recv_half, local_sems, send_sems, recv_sems,
    ) = refs
    exchange, local = Exchange(send_sems, recv_sems), Local(local_sems)
    own = rows.shape[1]
    first = local.load(rows, grad_down.at[:, pl.ds(0, own)])
    gains_load = local.load(model_gains_in, model_gains)
    at_first = lax.axis_index("section") == 0
    loads = load_pack(pack, held, local)
    exchange.greet(carry, 3 if spread else 0)
    background = Background(exchange, local, spans, sources, targets)
    pre_load = local.load_either(at_first, gate_up_a, gate_up_b, pre)
    mixed_load = local.load_either(at_first, mixed_a, mixed_b, mixed)
    chunks, own, cols = rows.shape
    units = grads.shape[1] // 2
    first.wait()

    def project(c):
        loads[c].wait()
        accumulate(total, grad_down[c], held, c * cols, 2 * units, units, c == 0)

    copies = gather_then(exchange, grad_down, project)
    hops = []
    if carry:
        hops = [exchange.copy(carried, arrived, exchange.section, 4, 0)]
        hops[0].start()
    moving = Spread(exchange, local, grad_down, moved) if spread else None
    pre_load.wait()
    blk = 256

    def activate(index, _):
        at = pl.multiple_of(index * blk, blk)
        gate = pre[:, pl.ds(at, blk)]
        upward = pre[:, pl.ds(units + at, blk)]
        grad_act = total[:, pl.ds(at, blk)]
        sig = jax.nn.sigmoid(gate)
        grads[:, pl.ds(at, blk)] = (grad_act * upward * sig * (1.0 + gate * (1.0 - sig))).astype(bf16)
        grads[:, pl.ds(units + at, blk)] = (grad_act * gate * sig).astype(bf16)
        return 0

    lax.fori_loop(0, units // blk, activate, 0)
    local.save(grads, grads_out)
    background.pass_on(False)

    def make(c):
        return dot_nt(grads[...], held[c * cols : (c + 1) * cols, : 2 * units])

    def idle(c):
        if not spread:
            turn_chunk(grad_down, moved, c)
        elif c > 0:
            moving.pass_on(c - 1)
        if c == chunks - 2:
            background.pass_on(True)

    def finish(c, summed):
        grad_mixed[c] = summed

    copies += scatter_from(
        exchange, make, idle, finish, keep, send_core, recv_core, send_half, recv_half
    )
    if spread:
        copies += moving.finish()
    local.save(moved, moved_out)
    mixed_load.wait()
    gains_load.wait()
    base = grad_down[:, :own]
    norm_step(mixed[...], grad_mixed[...], model_gains, 1, base, grad_mixed, gain_grad)
    for c in range(chunks):
        grad_proj_rows[c] = grad_mixed[c].astype(bf16)
    for copy in hops:
        copy.wait()
    copies += background.finish()
    for copy in copies:
        copy.wait_send()
    local.finish()


def norm_step(values, grad_out, model_gains, which, base, out, gain_grad):
    inverse = lax.rsqrt(row_mean(values * values) + norm_eps)
    gain = jnp.concatenate([model_gains[which, c][None, None, :] for c in range(out.shape[0])], axis=0)
    scaled = grad_out * gain
    centre = row_mean(scaled * values) * inverse * inverse
    out[...] = (base[...].astype(f32) + inverse * (scaled - values * centre)).astype(out.dtype)
    for c in range(out.shape[0]):
        gain_grad[c, :] = jnp.sum(grad_out[c] * values[c] * inverse[0], axis=0)


def attn_backward_kernel(
    width, spread, spans, hop, *refs
):
    sources, refs = refs[: 2 * len(spans)], refs[2 * len(spans) :]
    (
        rows, grad_mixed_in, hidden_a, hidden_b, projected_a, projected_b, values_a, values_b,
        pack, model_gains_in, gains_in, tables_in, masks_in,
        moved_out, grads_out, grad_hidden, gain_grad, head_gain_grads, *rest
    ) = refs
    if hop:
        arrived, rest = rest[0], rest[1:]
    targets, rest = rest[: len(spans)], rest[len(spans) :]
    (
        grad_mixed, model_gains, gains, tables, masks, grad_proj, moved, grads, hidden, projected, values, total, summed_rows,
        held, keep, send_core, recv_core, send_half, recv_half, local_sems, send_sems, recv_sems,
    ) = rest
    exchange, local = Exchange(send_sems, recv_sems), Local(local_sems)
    own = rows.shape[1]
    first = local.load(rows, grad_proj.at[:, pl.ds(0, own)])
    gain_loads = [
        local.load(model_gains_in, model_gains),
        local.load(gains_in, gains),
        local.load(grad_mixed_in, grad_mixed),
    ]
    at_first = lax.axis_index("section") == 0
    loads = load_pack(pack, held, local)
    exchange.greet(hop, 3 if spread else 0)
    background = Background(exchange, local, spans, sources, targets)
    extra = [local.load(tables_in, tables), local.load(masks_in, masks)]
    projected_load = local.load_either(at_first, projected_a, projected_b, projected)
    values_load = local.load_either(at_first, values_a, values_b, values)
    hidden_load = local.load_either(at_first, hidden_a, hidden_b, hidden)
    chunks, own, cols = rows.shape
    length = 2 * own
    q_width = grads.shape[1] // 2
    kv_width = q_width // 2
    kv_heads = kv_width // width
    group = q_width // kv_width
    first.wait()

    def project(c):
        loads[c].wait()
        accumulate(total, grad_proj[c], held, c * cols, 2 * q_width, q_width, c == 0)

    copies = gather_then(exchange, grad_proj, project)
    moving = Spread(exchange, local, grad_proj, moved) if spread else None
    projected_load.wait()
    values_load.wait()
    for load in extra + gain_loads:
        load.wait()
    cos, sin = tables[0], tables[1]
    gain_q, gain_k = gains[0:1, :], gains[1:2, :]
    scale = width ** (-0.5)
    gain_q_sum = jnp.zeros((1, width), f32)
    gain_k_sum = jnp.zeros((1, width), f32)
    for seq in range(2):
        at = slice(seq * length, (seq + 1) * length)
        allowed = masks[seq] > 0.5
        for kv in range(kv_heads):
            raw_k = projected[at, q_width + kv * width : q_width + (kv + 1) * width]
            value = values[at, kv * width : (kv + 1) * width]
            inverse_k, key_rot = rotated(raw_k, gain_k, cos, sin)
            grad_key = jnp.zeros((length, width), f32)
            grad_value = jnp.zeros((length, width), f32)
            for one in range(group):
                head = slice((kv * group + one) * width, (kv * group + one + 1) * width)
                raw_q = projected[at, head]
                grad_head = total[at, head].astype(bf16)
                inverse_q, query_rot = rotated(raw_q, gain_q, cos, sin)
                weights = softmax_rows(query_rot, key_rot, allowed, scale)
                grad_weights = dot_nt(grad_head, value)
                delta = jnp.sum(weights * grad_weights, axis=-1, keepdims=True)
                grad_scores = (weights * (grad_weights - delta)).astype(bf16)
                grad_value += dot_tn(weights.astype(bf16), grad_head)
                grad_key += dot_tn(grad_scores, query_rot)
                grad_query = dot_nn(grad_scores, key_rot) * scale
                grad_query = grad_query * cos - pltpu.roll(grad_query, 64, 1) * sin
                gain_q_sum += jnp.sum(grad_query * raw_q * inverse_q, axis=0, keepdims=True)
                grads[at, head] = norm_back(grad_query, raw_q, inverse_q, gain_q).astype(bf16)
            grad_key = grad_key * scale
            grad_key = grad_key * cos - pltpu.roll(grad_key, 64, 1) * sin
            gain_k_sum += jnp.sum(grad_key * raw_k * inverse_k, axis=0, keepdims=True)
            first = q_width + kv * width
            grads[at, first : first + width] = norm_back(grad_key, raw_k, inverse_k, gain_k).astype(bf16)
            first += kv_width
            grads[at, first : first + width] = grad_value.astype(bf16)
    local.save(grads, grads_out)
    background.pass_on(False)
    head_gain_grads[...] = jnp.concatenate(
        [gain_q_sum, gain_k_sum, jnp.zeros((6, width), f32)], axis=0
    )

    def make(c):
        return dot_nt(grads[...], held[c * cols : (c + 1) * cols, : 2 * q_width])

    def idle(c):
        if not spread:
            turn_chunk(grad_proj, moved, c)
        elif c > 0:
            moving.pass_on(c - 1)
        if c == chunks - 2:
            background.pass_on(True)

    def finish(c, summed):
        summed_rows[c] = summed

    copies += scatter_from(
        exchange, make, idle, finish, keep, send_core, recv_core, send_half, recv_half
    )
    if spread:
        copies += moving.finish()
    local.save(moved, moved_out)
    hidden_load.wait()
    norm_step(
        hidden[...].astype(f32), summed_rows[...], model_gains, 0, grad_mixed, grad_hidden, gain_grad
    )
    if hop:
        hops = [
            exchange.copy(grad_hidden.at[c], arrived.at[c], exchange.section, 4, c)
            for c in range(chunks)
        ]
        for copy in hops:
            copy.start()
        for copy in hops:
            copy.wait()
    copies += background.finish()
    for copy in copies:
        copy.wait_send()
    local.finish()


def weight_grad_kernel(blk, sides, *refs):
    lefts, rights, refs = refs[: 3 * sides], refs[3 * sides : 6 * sides], refs[6 * sides :]
    out, left, right = refs[0], refs[1 : 1 + sides], refs[1 + sides : 1 + 2 * sides]
    held, local_sems = refs[1 + 2 * sides :]
    local = Local(local_sems)
    at_first = lax.axis_index("section") == 0
    tokens = rights[0].shape[0]
    loads = []
    for side in range(sides):
        left_steps = pairs_of(lefts[3 * side : 3 * side + 3], side == 1)
        right_steps = pairs_of(rights[3 * side : 3 * side + 3], side == 0)
        for micro in range(2):
            at = pl.ds(micro * tokens, tokens)
            loads.append(
                [
                    local.load_either(
                        at_first, left_steps[0][micro], left_steps[1][micro], left[side].at[:, at]
                    ),
                    local.load_either(
                        at_first, right_steps[0][micro], right_steps[1][micro], right[side].at[at]
                    ),
                ]
            )
    saves, number = [None, None], 0
    for side in range(sides):
        for micro in range(2):
            for load in loads[2 * side + micro]:
                load.wait()
        for block in range(right[side].shape[1] // blk):
            slot = number % 2
            if saves[slot] is not None:
                saves[slot].wait()
            at = pl.ds(block * blk, blk)
            held[slot] = dot_nn(left[side][...], right[side][:, at]).astype(bf16)
            saves[slot] = local.load(held.at[slot], out.at[:, pl.ds(number * blk, blk)])
            number += 1
    for save in saves:
        save.wait()


def pairs_of(steps, backward):
    early, late = (steps[0], steps[1]), (steps[1], steps[2])
    return (late, early) if backward else (early, late)


VMEM_SPEC = pl.BlockSpec(memory_space=pltpu.VMEM)
HBM_SPEC = pl.BlockSpec(memory_space=pltpu.HBM)


def shape(dims, kind):
    return jax.ShapeDtypeStruct(dims, kind)


def exchange_scratch(chunks, own, cols):
    return [
        pltpu.VMEM((chunks, 2 * own, cols), f32),
        pltpu.VMEM((chunks, 2 * own, cols), bf16),
        pltpu.VMEM((chunks, 2 * own, cols), bf16),
        pltpu.VMEM((chunks, own, cols), bf16),
        pltpu.VMEM((chunks, own, cols), bf16),
        pltpu.SemaphoreType.DMA((20,)),
        pltpu.SemaphoreType.DMA((9, chunks)),
        pltpu.SemaphoreType.DMA((9, chunks)),
    ]


def params(number=None):
    if number is None:
        return pltpu.CompilerParams(vmem_limit_bytes=62 * MIB)
    return pltpu.CompilerParams(
        vmem_limit_bytes=62 * MIB, collective_id=number, has_side_effects=True
    )


class Numbers(dict):
    def of(self, *key):
        return self.setdefault(key, len(self))


def spans_of(background):
    return tuple((first, count) for _, first, count in background)


def gather_shapes(background):
    return [shape((4, count, blocks[0].shape[1]), bf16) for blocks, _, count in background]


def cost(flops, size):
    return pl.CostEstimate(flops=int(flops), bytes_accessed=int(size), transcendentals=0)


def attn_forward(hidden, pack, model_gains, gains, tables, masks, spread, hold, carried, background, numbers):
    chunks, own, cols = hidden.shape
    tokens, q_width, width = 4 * own, pack.shape[1] // 3, gains.shape[1]
    moved = (chunks, tokens, cols) if spread or hold else (chunks * cols, tokens)
    carry, spans = carried is not None, spans_of(background)
    rows = shape((chunks, own, cols), bf16)
    return pl.pallas_call(
        functools.partial(attn_forward_kernel, width, spread, hold, spans, carry),
        in_specs=[HBM_SPEC] * (2 * len(spans) + carry) + [HBM_SPEC] * 6,
        out_specs=[HBM_SPEC] * 5 + [VMEM_SPEC] + [HBM_SPEC] * (carry + len(spans)),
        out_shape=[
            shape(moved, bf16),
            shape((tokens, 2 * q_width), f32),
            shape((tokens, q_width // 2), bf16),
            shape((tokens, q_width), bf16),
            shape((chunks, own, cols), f32),
            rows,
        ]
        + [rows] * carry
        + gather_shapes(background),
        scratch_shapes=[
            pltpu.VMEM(hidden.shape, bf16),
            pltpu.VMEM(model_gains.shape, f32),
            pltpu.VMEM(gains.shape, f32),
            pltpu.VMEM(tables.shape, f32),
            pltpu.VMEM(masks.shape, f32),
            pltpu.VMEM((chunks, tokens, cols), bf16),
            pltpu.VMEM(moved, bf16),
            pltpu.VMEM((tokens, 2 * q_width), f32),
            pltpu.VMEM((tokens, q_width // 2), bf16),
            pltpu.VMEM((tokens, q_width), bf16),
            pltpu.VMEM((chunks, own, cols), f32),
            pltpu.VMEM(pack.shape, bf16),
        ]
        + exchange_scratch(chunks, own, cols),
        compiler_params=params(numbers.of("attn_forward", hold, carry, spans)),
        cost_estimate=cost(2 * tokens * pack.size, pack.size * 2),
        name="attn_forward",
    )(*sum([list(blocks) for blocks, *_ in background], []), *([carried] if carry else []), hidden, pack, model_gains, gains, tables, masks)


def ffn_forward(rows, mixed, pack, hop, held_rows, background, numbers):
    chunks, own, cols = rows.shape
    tokens, units = 4 * own, pack.shape[1] // 3
    depth = chunks * cols
    spans, spread = spans_of(background), held_rows is not None
    return pl.pallas_call(
        functools.partial(ffn_forward_kernel, hop, spread, spans),
        in_specs=[HBM_SPEC] * (spread + 2 * len(spans)) + [HBM_SPEC] * 3,
        out_specs=[HBM_SPEC] * 3 + [VMEM_SPEC] * (2 if hop else 1) + [HBM_SPEC] * (spread + len(spans)),
        out_shape=[
            shape((depth, tokens), bf16),
            shape((tokens, 2 * units), f32),
            shape((tokens, units), bf16),
        ]
        + [shape((chunks, own, cols), bf16)] * (2 if hop else 1)
        + [shape((chunks, tokens, cols), bf16)] * spread
        + gather_shapes(background),
        scratch_shapes=[
            pltpu.VMEM((chunks, tokens, cols), bf16),
            pltpu.VMEM((depth, tokens), bf16),
            pltpu.VMEM((chunks, own, cols), f32),
            pltpu.VMEM((tokens, units), bf16),
            pltpu.VMEM((tokens, 2 * units), f32),
            pltpu.VMEM(pack.shape, bf16),
        ]
        + exchange_scratch(chunks, own, cols),
        compiler_params=params(numbers.of("ffn_forward", hop, spread, spans)),
        cost_estimate=cost(2 * tokens * pack.size, pack.size * 2),
        name="ffn_forward",
    )(*([held_rows] if spread else []), *sum([list(blocks) for blocks, *_ in background], []), rows, mixed, pack)


def ffn_backward(rows, mixed, gate_up, pack, model_gains, spread, carried, background, numbers):
    chunks, own, cols = rows.shape
    tokens, units = 4 * own, pack.shape[1] // 3
    moved = (chunks, tokens, cols) if spread else (chunks * cols, tokens)
    carry, spans = carried is not None, spans_of(background)
    return pl.pallas_call(
        functools.partial(ffn_backward_kernel, spread, spans, carry),
        in_specs=[HBM_SPEC] * (2 * len(spans) + carry) + [HBM_SPEC] * 7,
        out_specs=[HBM_SPEC] * 2 + [VMEM_SPEC] * 3 + [HBM_SPEC] * (carry + len(spans)),
        out_shape=[
            shape(moved, bf16),
            shape((tokens, 2 * units), bf16),
            shape((chunks, own, cols), f32),
            shape((chunks, own, cols), bf16),
            shape((chunks, cols), f32),
        ]
        + [shape((chunks, own, cols), bf16)] * carry
        + gather_shapes(background),
        scratch_shapes=[
            pltpu.VMEM(model_gains.shape, f32),
            pltpu.VMEM((chunks, tokens, cols), bf16),
            pltpu.VMEM(moved, bf16),
            pltpu.VMEM((chunks, own, cols), f32),
            pltpu.VMEM((tokens, 2 * units), bf16),
            pltpu.VMEM((tokens, 2 * units), f32),
            pltpu.VMEM((tokens, units), f32),
            pltpu.VMEM(pack.shape, bf16),
        ]
        + exchange_scratch(chunks, own, cols),
        compiler_params=params(numbers.of("ffn_backward", carry, spans)),
        cost_estimate=cost(2 * tokens * pack.size, pack.size * 2),
        name="ffn_backward",
    )(*sum([list(blocks) for blocks, *_ in background], []), *([carried] if carry else []), rows, *mixed, *gate_up, pack, model_gains)


def attn_backward(
    rows, grad_mixed, hidden, projected, values, pack, model_gains, gains, tables, masks, spread, hop,
    background, numbers
):
    chunks, own, cols = rows.shape
    tokens, q_width, width = 4 * own, pack.shape[1] // 3, gains.shape[1]
    moved = (chunks, tokens, cols) if spread else (chunks * cols, tokens)
    spans = spans_of(background)
    return pl.pallas_call(
        functools.partial(attn_backward_kernel, width, spread, spans, hop),
        in_specs=[HBM_SPEC] * (2 * len(spans)) + [HBM_SPEC] * 13,
        out_specs=[HBM_SPEC] * 2 + [VMEM_SPEC] * (4 if hop else 3) + [HBM_SPEC] * len(spans),
        out_shape=[
            shape(moved, bf16),
            shape((tokens, 2 * q_width), bf16),
            shape((chunks, own, cols), bf16),
            shape((chunks, cols), f32),
            shape((8, width), f32),
        ]
        + [shape((chunks, own, cols), bf16)] * (1 if hop else 0)
        + gather_shapes(background),
        scratch_shapes=[
            pltpu.VMEM(grad_mixed.shape, f32),
            pltpu.VMEM(model_gains.shape, f32),
            pltpu.VMEM(gains.shape, f32),
            pltpu.VMEM(tables.shape, f32),
            pltpu.VMEM(masks.shape, f32),
            pltpu.VMEM((chunks, tokens, cols), bf16),
            pltpu.VMEM(moved, bf16),
            pltpu.VMEM((tokens, 2 * q_width), bf16),
            pltpu.VMEM((chunks, own, cols), bf16),
            pltpu.VMEM((tokens, 2 * q_width), f32),
            pltpu.VMEM((tokens, q_width // 2), bf16),
            pltpu.VMEM((tokens, q_width), f32),
            pltpu.VMEM((chunks, own, cols), f32),
            pltpu.VMEM(pack.shape, bf16),
        ]
        + exchange_scratch(chunks, own, cols),
        compiler_params=params(numbers.of("attn_backward", hop, spans)),
        cost_estimate=cost(2 * tokens * pack.size, pack.size * 2),
        name="attn_backward",
    )(
        *sum([list(blocks) for blocks, *_ in background], []), rows, grad_mixed, *hidden, *projected, *values, pack, model_gains, gains, tables, masks
    )


def weight_grad(lefts, rights):
    depth, tokens = lefts[0][0].shape
    blk = 512
    widths = [right[0].shape[1] for right in rights]
    return pl.pallas_call(
        functools.partial(weight_grad_kernel, blk, len(lefts)),
        in_specs=[HBM_SPEC] * (6 * len(lefts)),
        out_specs=HBM_SPEC,
        out_shape=shape((depth, sum(widths)), bf16),
        scratch_shapes=[pltpu.VMEM((depth, 2 * tokens), bf16) for _ in lefts]
        + [pltpu.VMEM((2 * tokens, width), bf16) for width in widths]
        + [
            pltpu.VMEM((2, depth, blk), bf16),
            pltpu.SemaphoreType.DMA((4 * len(lefts) + sum(widths) // blk,)),
        ],
        compiler_params=params(),
        cost_estimate=cost(4 * depth * tokens * sum(widths), 2 * depth * sum(widths)),
        name="weight_grad",
    )(*sum(lefts, []), *sum(rights, []))


def rope_tables(position, head_width):
    exponent = jnp.arange(0, head_width, 2).astype(f32) / head_width
    inverse = rope_base ** (-exponent)
    angles = position.astype(f32)[:, None] * inverse[None, :]
    cosine, sine = jnp.cos(angles), jnp.sin(angles)
    return (
        jnp.concatenate([cosine, cosine], axis=-1),
        jnp.concatenate([-sine, sine], axis=-1),
    )


def per_device(
    block_input,
    segment_ids,
    out_cotangent,
    attn_norm,
    q_weight,
    k_weight,
    v_weight,
    o_weight,
    q_norm,
    k_norm,
    ffn_norm,
    gate_weight,
    up_weight,
    down_weight,
):
    section = lax.axis_index("section")
    place = lax.axis_index("dp")
    core = place % 2
    half = lax.axis_index("tensor")
    n_dp = lax.axis_size("dp")
    n_chip = n_dp // 2
    micro_count, own_rows, depth = block_input.shape
    length = 2 * own_rows
    head_width = q_norm.shape[1]
    first_core = core == 0
    swap_core = [(i, i ^ 1) for i in range(n_dp)]
    swap_half = [(0, 1), (1, 0)]
    chip_groups = [[2 * chip + one for chip in range(n_chip)] for one in (0, 1)]

    def to_core(values):
        return lax.ppermute(values, "dp", swap_core)

    def to_half(values):
        return lax.ppermute(values, "tensor", swap_half)

    def split_columns(weight):
        side = weight.shape[1] // 2
        left, right = weight[:, :side], weight[:, side:]
        return jnp.where(first_core, left, right), jnp.where(first_core, right, left)

    def split_rows(weight):
        side = weight.shape[0] // 2
        left, right = weight[:side].T, weight[side:].T
        return jnp.where(first_core, left, right), jnp.where(first_core, right, left)

    def chip_block(pairs):
        mine = jnp.concatenate([pair[0] for pair in pairs], axis=1)
        theirs = to_core(jnp.concatenate([pair[1] for pair in pairs], axis=1))
        return jnp.concatenate(
            [jnp.where(first_core, mine, theirs), jnp.where(first_core, theirs, mine)], axis=0
        )

    def gathered(block):
        return lax.all_gather(block, "dp", axis=0, tiled=True, axis_index_groups=chip_groups)

    square = n_chip == row_chunks
    numbers = Numbers()
    attn_block = chip_block(
        [
            split_columns(q_weight[0]),
            split_columns(k_weight[0]),
            split_columns(v_weight[0]),
            split_rows(o_weight[0]),
        ]
    )
    ffn_block = chip_block(
        [split_columns(gate_weight[0]), split_columns(up_weight[0]), split_rows(down_weight[0])]
    )
    if square:
        attn_block, ffn_block = lax.optimization_barrier((attn_block, ffn_block))
        attn_pack = chip_gather([attn_block], numbers.of("chip_gather", 0)).reshape(depth, -1)
    else:
        attn_pack = gathered(attn_block)
    ffn_pack = gathered(ffn_block)

    cols = depth // row_chunks
    model_gains = jnp.concatenate([attn_norm, ffn_norm], axis=0).reshape(2, row_chunks, cols)
    head_gains = jnp.concatenate([q_norm, k_norm, jnp.zeros((6, head_width), f32)], axis=0)

    def chunked(rows):
        return rows.reshape(rows.shape[0], row_chunks, cols).transpose(1, 0, 2)

    def joined(rows):
        return rows.transpose(1, 0, 2).reshape(rows.shape[1], depth)

    inputs = [chunked(block_input[micro]) for micro in range(2)]
    cotangents = [chunked(out_cotangent[micro]) for micro in range(2)]

    def arranged(values):
        sides = values[..., :own_rows], values[..., own_rows:]
        return jnp.concatenate(
            [jnp.where(half == 0, *sides), jnp.where(half == 0, *sides[::-1])], axis=-1
        )

    position = arranged(jnp.arange(length, dtype=jnp.int32))
    tables = jnp.stack(rope_tables(position, head_width))
    ids = arranged(jnp.stack([segment_ids, to_core(segment_ids)], axis=1))
    causal = position[:, None] >= position[None, :]
    masks = (causal & (ids[..., :, None] == ids[..., None, :])).astype(f32)

    at_first = section == 0

    def pick(first, second):
        return jax.tree.map(lambda a, b: jnp.where(at_first, a, b), first, second)

    zero_rows = jnp.zeros_like(inputs[0])
    forward_masks = [masks[0], pick(masks[1], masks[0]), masks[1]]
    backward_masks = [masks[0], pick(masks[0], masks[1]), masks[1]]
    results, backs, saves = [], [], []
    grads, ffn_saves, attn_saves, gains = [], [], [], []

    def forward_step(step, arrived, hop, carried=None, attn_work=(), ffn_work=()):
        hidden = inputs[step] if step < 2 else zero_rows
        if step > 0:
            hidden = pick(hidden, arrived)
        turned_in, projected, values, attended, mixed, rows, *more = attn_forward(
            hidden, attn_pack, model_gains, head_gains, tables, forward_masks[step],
            square and step > 0, square and step == 0, carried, attn_work, numbers,
        )
        turned_mid, gate_up, activated, result, *rest = ffn_forward(
            rows, mixed, ffn_pack, hop, turned_in if square and step == 0 else None, ffn_work, numbers
        )
        if square and step == 0:
            turned_in = rest.pop(1)
        results.append(result)
        backs.append((hidden, projected, values, mixed, gate_up))
        saves.append((turned_in, attended, turned_mid, activated))
        return more + rest

    def back_ffn(step, arrived, carried=None, work=()):
        rows = pick(arrived, cotangents[step] if step < 2 else zero_rows)
        *_, mixed, gate_up = zip(backs[0], backs[2]) if step == 1 else zip(backs[1], backs[1])
        turned_rows, ffn_grads, grad_mixed, proj_rows, gain_grad, *more = ffn_backward(
            rows, mixed, gate_up, ffn_pack, model_gains, square, carried, work, numbers
        )
        ffn_saves.append((turned_rows, ffn_grads))
        return (proj_rows, grad_mixed, gain_grad), more

    def back_attn(step, proj_rows, grad_mixed, ffn_gain_grad, hop, work=()):
        hidden, projected, values, *_ = (
            zip(backs[0], backs[2]) if step == 1 else zip(backs[1], backs[1])
        )
        turned_rows, attn_grads, grad_hidden, attn_gain_grad, head_gain_grads, *rest = attn_backward(
            proj_rows, grad_mixed, hidden, projected, values, attn_pack, model_gains, head_gains,
            tables, backward_masks[step], square, hop, work, numbers,
        )
        attn_saves.append((turned_rows, attn_grads))
        grads.append(grad_hidden)
        gains.append((attn_gain_grad, ffn_gain_grad, head_gain_grads))
        return rest

    def column(table, item):
        return [row[item] for row in table]

    def work(*items):
        return items if square else ()

    def of_micro(micro, item):
        return saves[micro][item], saves[micro + 1][item]

    tokens = 2 * length
    (arrived,) = forward_step(0, zero_rows, True)
    forward_step(1, arrived, False)
    active, attended = of_micro(0, 3), of_micro(0, 1)
    part = tokens // 4
    others, (arrived, *pieces) = back_ffn(0, zero_rows, results[1], work((active, 0, part)))
    active_pieces = [(0, pieces)]
    pieces = back_attn(0, *others, False, work((active, part, part)))
    active_pieces.append((part, pieces))
    grad_arrived, *pieces = forward_step(
        2, arrived, False, grads[0], work((active, 2 * part, part)),
        work((active, 3 * part, part), (attended, 0, tokens)),
    )
    active_pieces += [(2 * part, pieces[:1]), (3 * part, pieces[1:2])]
    attended_all = [pieces[2:]]
    active, attended = of_micro(1, 3), of_micro(1, 1)
    side = tokens // 2
    grad_arrived, results[2] = lax.optimization_barrier((grad_arrived, results[2]))
    others, pieces = back_ffn(1, grad_arrived, None, work((active, 0, side)))
    late_pieces = [(0, pieces)]
    grad_arrived, *pieces = back_attn(
        1, *others, True, work((active, side, side), (attended, 0, tokens))
    )
    late_pieces.append((side, pieces[:1]))
    attended_all.append(pieces[1:])
    early_block = attn_saves[1][1], attn_saves[0][1]
    (proj_rows, *others), early_grads = back_ffn(
        2, grad_arrived, None, work((early_block, 0, side), (early_block, side, side))
    )
    if square:
        ffn_partial = weight_grad([column(saves, 2)], [column(ffn_saves, 1)])
    else:
        ffn_partial = weight_grad(
            [column(saves, 2), column(ffn_saves, 0)], [column(ffn_saves, 1), column(saves, 3)]
        )
    proj_rows, ffn_partial = lax.optimization_barrier((proj_rows, ffn_partial))
    back_attn(2, proj_rows, *others, False)
    if not square:
        attn_partial = weight_grad(
            [column(saves, 0), column(attn_saves, 0)], [column(attn_saves, 1), column(saves, 1)]
        )
    gain_total = functools.reduce(lambda a, b: jax.tree.map(jnp.add, a, b), gains)

    section_outputs = jnp.stack(
        [joined(pick(results[micro], results[micro + 1])) for micro in range(2)]
    )[None]
    section_input_grads = jnp.stack(
        [joined(pick(grads[micro + 1], grads[micro])) for micro in range(2)]
    )[None]

    def scattered(partial):
        return lax.psum_scatter(
            partial, "dp", scatter_dimension=0, tiled=True, axis_index_groups=chip_groups
        )

    def owned(rows):
        side = rows.shape[0] // 2
        own = jnp.where(first_core, rows[:side], rows[side:])
        other = to_core(jnp.where(first_core, rows[side:], rows[:side]))
        return (
            jnp.where(first_core, own, other).astype(f32),
            jnp.where(first_core, other, own).astype(f32),
        )

    units = gate_weight.shape[2] // 2
    if square:
        late_grads = chip_gather([attn_saves[2][1], attn_saves[1][1]], numbers.of("chip_gather", 1))

        def flat(rows):
            return rows.reshape(-1, rows.shape[-1])

        def summed(rows, pieces):
            return sum(
                dot_tn(flat(rows[:, first : first + piece.shape[1]]), flat(piece))
                for first, (piece,) in pieces
            )

        def forward_rows(micro):
            return pick(saves[micro][0], saves[micro + 1][0])

        def backward_rows(table, micro):
            return pick(table[micro + 1][0], table[micro][0])

        down_rows = summed(backward_rows(ffn_saves, 0), active_pieces) + summed(
            backward_rows(ffn_saves, 1), late_pieces
        )
        o_rows = sum(
            summed(backward_rows(attn_saves, micro), [(0, attended_all[micro])])
            for micro in range(2)
        )
        early_pieces = [(0, early_grads[:1]), (side, early_grads[1:])]
        qkv_rows = summed(forward_rows(0), early_pieces) + summed(
            forward_rows(1), [(0, [late_grads])]
        )
        attn_rows = jnp.concatenate([qkv_rows, o_rows], axis=1)
        ffn_rows = scattered(ffn_partial)
    else:
        attn_partial, ffn_rows = lax.optimization_barrier((attn_partial, scattered(ffn_partial)))
        ffn_sides = owned(ffn_rows)
        attn_sides = owned(scattered(attn_partial))
    q_width = q_weight.shape[2] // 2
    kv_width = k_weight.shape[2] // 2

    def across(sides, first, width):
        return jnp.concatenate([side[:, first : first + width] for side in sides], axis=1)[None]

    def down(sides, first):
        return jnp.concatenate([side[:, first:].T for side in sides], axis=0)[None]

    packed = jnp.concatenate(
        [
            gain_total[0].reshape(-1),
            gain_total[1].reshape(-1),
            gain_total[2][0],
            gain_total[2][1],
        ]
    ).reshape(-1, head_width)
    packed = packed + to_core(packed)
    packed = packed + to_half(packed)
    reach = 2
    while reach < n_dp:
        packed = packed + lax.ppermute(packed, "dp", [(i, i ^ reach) for i in range(n_dp)])
        reach *= 2
    packed = packed.reshape(-1)
    gain_grads = (
        packed[None, :depth],
        packed[None, 2 * depth : 2 * depth + head_width],
        packed[None, 2 * depth + head_width :],
        packed[None, depth : 2 * depth],
    )
    if square:
        attn_wide = ((q_width, False), (kv_width, False), (kv_width, False), (q_width, True))
        attn_grads = place_parts(attn_rows, core_swap(attn_rows, numbers.of("core_swap", 0)), attn_wide)
        down_swapped = core_swap(down_rows, numbers.of("core_swap", 1))
        down_grads = place_parts(down_rows, down_swapped, ((units, True),))
        others = (section_outputs, section_input_grads, gain_grads, attn_grads, down_grads)
        others, ffn_rows = lax.optimization_barrier((others, ffn_rows))
        section_outputs, section_input_grads, gain_grads, attn_grads, down_grads = others
        ffn_swapped = core_swap(ffn_rows, numbers.of("core_swap", 2))
        wide_grads = place_parts(ffn_rows, ffn_swapped, ((units, False), (units, False)))
        weight_grads = [grad[None] for grad in (*attn_grads, *wide_grads, *down_grads)]
    else:
        weight_grads = [
            across(attn_sides, 0, q_width),
            across(attn_sides, q_width, kv_width),
            across(attn_sides, q_width + kv_width, kv_width),
            down(attn_sides, 2 * q_width),
            across(ffn_sides, 0, units),
            across(ffn_sides, units, units),
            down(ffn_sides, 2 * units),
        ]
    return (
        section_outputs,
        section_input_grads,
        gain_grads[0],
        *weight_grads[:4],
        *gain_grads[1:],
        *weight_grads[4:],
    )


def solution(mesh):
    rows = P(None, ("dp", "tensor"), None)
    out_rows = P("section", None, ("dp", "tensor"), None)
    gain = P("section", None)
    wide = P("section", "dp", "tensor")
    tall = P("section", "tensor", "dp")
    return jax.shard_map(
        per_device,
        mesh=mesh,
        in_specs=(
            rows, P(None, "dp"), rows, gain, wide, wide, wide, tall, gain, gain, gain, wide, wide, tall,
        ),
        out_specs=(
            out_rows, out_rows, gain, wide, wide, wide, tall, gain, gain, gain, wide, wide, tall,
        ),
        check_vma=False,
    )
```

```python
import functools

import jax
import jax.numpy as jnp
from jax import lax
from jax.experimental import pallas as pl
from jax.experimental.pallas import tpu as pltpu
from jax.sharding import PartitionSpec as P

norm_eps = 1e-06
rope_base = 1000000.0
masked_score = -1e30
row_chunks = 4
background_size = 4 * 384 * 960
f32 = jnp.float32
bf16 = jnp.bfloat16
MIB = 1024 * 1024
MESH = pl.DeviceIdType.MESH


def dot_nn(left, right):
    return lax.dot_general(left, right, (((1,), (0,)), ((), ())), preferred_element_type=f32)


def dot_nt(left, right):
    return lax.dot_general(left, right, (((1,), (1,)), ((), ())), preferred_element_type=f32)


def dot_tn(left, right):
    return lax.dot_general(left, right, (((0,), (0,)), ((), ())), preferred_element_type=f32)


def inverse_rms(values):
    return lax.rsqrt(jnp.mean(values * values, axis=-1, keepdims=True) + norm_eps)


def norm_back(grad_out, values, inverse, gain_vec):
    scaled = grad_out * gain_vec
    return inverse * (
        scaled - values * inverse * inverse * jnp.mean(scaled * values, axis=-1, keepdims=True)
    )


class Exchange:
    def __init__(self, send_sems, recv_sems):
        place = lax.axis_index("dp")
        self.core = {"dp": place + 1 - 2 * (place % 2)}
        self.half = {"tensor": 1 - lax.axis_index("tensor")}
        self.section = {"section": 1 - lax.axis_index("section")}
        core, chip = place % 2, place // 2
        across, along = chip % 2, chip // 2
        self.chip = chip
        numbers = (chip + 1 - 2 * across, chip + 2 - 4 * along, 3 - chip)
        self.chips = [(number, {"dp": 2 * number + core}) for number in numbers]
        self.send_sems, self.recv_sems = send_sems, recv_sems

    def greet(self, with_section, with_chips):
        others = [self.core, self.half] + ([self.section] if with_section else [])
        self.meet(others + [device for _, device in self.chips[:with_chips]])

    def meet(self, others):
        barrier = pltpu.get_barrier_semaphore()
        for other in others:
            pl.semaphore_signal(barrier, inc=1, device_id=other, device_id_type=MESH)
        pl.semaphore_wait(barrier, len(others))

    def copy(self, source, target, other, stage, chunk):
        return pltpu.make_async_remote_copy(
            src_ref=source,
            dst_ref=target,
            send_sem=self.send_sems.at[stage, chunk],
            recv_sem=self.recv_sems.at[stage, chunk],
            device_id=other,
            device_id_type=MESH,
        )


def gather_then(exchange, rows, use, arrivals=()):
    chunks, total, _ = rows.shape
    own = total // 4
    first = [
        exchange.copy(rows.at[c, pl.ds(0, own)], rows.at[c, pl.ds(own, own)], exchange.half, 0, c)
        for c in range(chunks)
    ]
    second = [
        exchange.copy(
            rows.at[c, pl.ds(0, 2 * own)], rows.at[c, pl.ds(2 * own, 2 * own)], exchange.core, 1, c
        )
        for c in range(chunks)
    ]
    if not arrivals:
        for c in range(chunks):
            first[c].start()
    for c in range(chunks + 1):
        if arrivals and c < chunks:
            arrivals[c].wait_recv()
            first[c].start()
        ready = c - 1 if arrivals else c
        if 0 <= ready < chunks:
            first[ready].wait_recv()
            second[ready].start()
            if ready > 0:
                second[ready - 1].wait_recv()
                use(ready - 1)
    second[chunks - 1].wait_recv()
    use(chunks - 1)
    return first + second


def scatter_from(exchange, make, idle, finish, keep, send_core, recv_core, send_half, recv_half):
    chunks, pair, _ = keep.shape
    own = pair // 2
    first = [
        exchange.copy(send_core.at[c], recv_core.at[c], exchange.core, 2, c) for c in range(chunks)
    ]
    second = [
        exchange.copy(send_half.at[c], recv_half.at[c], exchange.half, 3, c) for c in range(chunks)
    ]

    def middle(c):
        first[c].wait_recv()
        summed = keep[c] + recv_core[c].astype(f32)
        send_half[c] = summed[own:].astype(bf16)
        second[c].start()
        keep[c, :own] = summed[:own]

    for c in range(chunks):
        product = make(c)
        send_core[c] = product[pair:].astype(bf16)
        first[c].start()
        keep[c] = product[:pair]
        if c > 0:
            middle(c - 1)
    middle(chunks - 1)
    for c in range(chunks):
        idle(c)
        second[c].wait_recv()
        finish(c, keep[c, :own] + recv_half[c].astype(f32))
    return first + second


class ChipGather:
    def __init__(self, exchange, local, blocks, out, stage):
        (across, across_device), (along, along_device), _ = exchange.chips
        at_first = lax.axis_index("section") == 0
        half = blocks[0].shape[0] // 2
        first, last = pl.ds(0, half), pl.ds(half, half)
        target = out.at[exchange.chip]
        choices = [
            [
                exchange.copy(block, target, across_device, stage, 0),
                exchange.copy(block, target, along_device, stage, 1),
            ]
            for block in blocks
        ]
        self.direct = choices[0]
        self.passed = [
            exchange.copy(out.at[across, first], out.at[across, first], along_device, stage, 2),
            exchange.copy(out.at[along, last], out.at[along, last], across_device, stage, 3),
        ]
        for index, block in enumerate(blocks):
            here = at_first if index == 0 else jnp.logical_not(at_first)

            def start(index=index):
                for copy in choices[index]:
                    copy.start()

            if len(blocks) > 1:
                pl.when(here)(start)
            else:
                start()

        if len(blocks) > 1:
            local.saves.append(local.load_either(at_first, *blocks, target))
        else:
            local.save(blocks[0], target)

    def pass_on(self):
        for copy, onward in zip(self.direct, self.passed):
            copy.wait_recv()
            onward.start()

    def finish(self):
        for copy in self.passed:
            copy.wait_recv()
        return self.direct + self.passed


class Background:
    def __init__(self, exchange, local, spans, sources, targets):
        self.gathers = [
            ChipGather(
                exchange,
                local,
                [source.at[pl.ds(first, count)] for source in sources[2 * index : 2 * index + 2]],
                target,
                7 + index,
            )
            for index, ((first, count), target) in enumerate(zip(spans, targets))
        ]

        long = sum(target.size for target in targets) > background_size
        self.late = [long and index > 0 for index in range(len(targets))]

    def pass_on(self, late):
        for gather, when in zip(self.gathers, self.late):
            if when == late:
                gather.pass_on()

    def finish(self):
        return sum([gather.finish() for gather in self.gathers], [])


def chip_gather_kernel(*refs):
    *blocks, out, local_sems, send_sems, recv_sems = refs
    exchange, local = Exchange(send_sems, recv_sems), Local(local_sems)
    exchange.meet([device for _, device in exchange.chips[:2]])
    gather = ChipGather(exchange, local, blocks, out, 0)
    gather.pass_on()
    for copy in gather.finish():
        copy.wait_send()
    local.finish()


def chip_gather(blocks, number):
    return pl.pallas_call(
        chip_gather_kernel,
        in_specs=[HBM_SPEC] * len(blocks),
        out_specs=HBM_SPEC,
        out_shape=shape((4,) + blocks[0].shape, bf16),
        scratch_shapes=[
            pltpu.SemaphoreType.DMA((1,)),
            pltpu.SemaphoreType.DMA((1, 4)),
            pltpu.SemaphoreType.DMA((1, 4)),
        ],
        compiler_params=params(number),
        cost_estimate=cost(0, 300 * blocks[0].size),
        name="chip_gather",
    )(*blocks)


def core_swap_kernel(rows, out, send_sems, recv_sems):
    exchange = Exchange(send_sems, recv_sems)
    exchange.meet([exchange.core])
    side = out.shape[0]
    theirs = pl.multiple_of((1 - lax.axis_index("dp") % 2) * side, side)
    copy = exchange.copy(rows.at[pl.ds(theirs, side)], out, exchange.core, 0, 0)
    copy.start()
    copy.wait()


def core_swap(rows, number):
    side = rows.shape[0] // 2
    return pl.pallas_call(
        core_swap_kernel,
        in_specs=[HBM_SPEC],
        out_specs=HBM_SPEC,
        out_shape=shape((side, rows.shape[1]), rows.dtype),
        scratch_shapes=[pltpu.SemaphoreType.DMA((1, 1)), pltpu.SemaphoreType.DMA((1, 1))],
        compiler_params=params(number),
        cost_estimate=cost(0, 10 * rows.size),
        name="core_swap",
    )(rows)


def place_kernel(wide, *refs):
    rows, other, refs = refs[0], refs[1], refs[2:]
    outs, (mine, theirs, *staged, local_sems) = refs[: len(wide)], refs[len(wide) :]
    local = Local(local_sems)
    core = lax.axis_index("dp") % 2
    side = other.shape[0]
    loads = [
        local.load(rows.at[pl.ds(pl.multiple_of(core * side, side), side)], mine),
        local.load(other, theirs),
    ]
    for load in loads:
        load.wait()
    for index, (source, place) in enumerate(((mine, core), (theirs, 1 - core))):
        first = 0
        for number, ((width, turned), out) in enumerate(zip(wide, outs)):
            stage = staged[number].at[index]
            block = source[:, first : first + width].astype(f32)
            at = pl.ds(pl.multiple_of(place * width, width), width)
            if turned:
                staged[number][index] = block.T
                local.save(stage, out.at[at, :])
            else:
                staged[number][index] = block
                local.save(stage, out.at[:, at])
            first += width
    local.finish()


def place_parts(rows, other, wide):
    side = other.shape[0]
    return pl.pallas_call(
        functools.partial(place_kernel, wide),
        in_specs=[HBM_SPEC] * 2,
        out_specs=[HBM_SPEC] * len(wide),
        out_shape=[
            shape((2 * width, side) if turned else (side, 2 * width), f32)
            for width, turned in wide
        ],
        scratch_shapes=[pltpu.VMEM(other.shape, other.dtype)] * 2
        + [
            pltpu.VMEM((2, width, side) if turned else (2, side, width), f32)
            for width, turned in wide
        ]
        + [pltpu.SemaphoreType.DMA((2 + 2 * len(wide),))],
        compiler_params=params(),
        cost_estimate=cost(0, 12 * other.size),
        name="place",
    )(rows, other)


def load_pack(pack, held, local):
    depth = held.shape[0] // row_chunks
    return [
        local.load(pack.at[pl.ds(c * depth, depth)], held.at[pl.ds(c * depth, depth)])
        for c in range(row_chunks)
    ]


class Local:
    def __init__(self, sems):
        self.sems, self.used, self.saves = sems, 0, []

    def copy(self, source, target):
        self.used += 1
        return pltpu.make_async_copy(source, target, self.sems.at[self.used - 1])

    def load(self, source, target):
        copy = self.copy(source, target)
        copy.start()
        return copy

    def load_either(self, at_first, first, second, target):
        one = self.copy(first, target)
        other = pltpu.make_async_copy(second, target, self.sems.at[self.used - 1])

        @pl.when(at_first)
        def _():
            one.start()

        @pl.when(jnp.logical_not(at_first))
        def _():
            other.start()

        return one

    def save(self, source, target):
        self.saves.append(self.load(source, target))

    def finish(self):
        for copy in self.saves:
            copy.wait()


def row_mean(values):
    size = values.shape[0] * values.shape[2]
    return jnp.sum(jnp.sum(values, axis=0), axis=-1, keepdims=True)[None] * (1.0 / size)


def accumulate(total, left, weights, first_row, first_col, width, start):
    depth = left.shape[1]
    blk = 512 if width % 512 == 0 else 256

    def body(index, _):
        at = pl.multiple_of(index * blk, blk)
        product = dot_nn(left, weights[pl.ds(first_row, depth), pl.ds(first_col + at, blk)])
        if start:
            total[:, pl.ds(at, blk)] = product
        else:
            total[:, pl.ds(at, blk)] += product
        return 0

    lax.fori_loop(0, width // blk, body, 0)


def rotated(raw, gain, cosine, signed_sine):
    inverse = inverse_rms(raw)
    scaled = raw * inverse * gain
    turned = scaled * cosine + pltpu.roll(scaled, 64, 1) * signed_sine
    return inverse, turned.astype(bf16)


def softmax_rows(query_rot, key_rot, allowed, scale):
    scores = jnp.where(allowed, dot_nt(query_rot, key_rot) * scale, masked_score)
    exponent = jnp.exp(scores - jnp.max(scores, axis=-1, keepdims=True))
    return exponent / jnp.sum(exponent, axis=-1, keepdims=True)


class Spread:
    def __init__(self, exchange, local, rows, moved):
        side = rows.shape[1] // 2
        self.own = local.load(rows.at[exchange.chip], moved.at[exchange.chip])
        self.arrivals, self.onward = [], []
        for index, (number, device) in enumerate(exchange.chips):
            self.arrivals.append(
                exchange.copy(
                    rows.at[number, pl.ds(0, side)],
                    moved.at[exchange.chip, pl.ds(0, side)],
                    device, 5, index,
                )
            )
            self.arrivals[-1].start()
            self.onward.append(
                exchange.copy(
                    moved.at[number, pl.ds(0, side)],
                    moved.at[number, pl.ds(side, side)],
                    exchange.core, 6, index,
                )
            )

    def pass_on(self, index):
        self.arrivals[index].wait_recv()
        self.onward[index].start()

    def finish(self):
        self.own.wait()
        for copy in self.onward:
            copy.wait_recv()
        return self.arrivals + self.onward


def turn_chunk(rows, target, c):
    cols = rows.shape[2]
    target[pl.ds(c * cols, cols), :] = rows[c].T


def attn_forward_kernel(
    width, spread, hold, spans, carry, *refs
):
    sources, refs = refs[: 2 * len(spans)], refs[2 * len(spans) :]
    if carry:
        carried, refs = refs[0], refs[1:]
    (
        hidden_in, pack, model_gains_in, gains_in, tables_in, masks_in,
        moved_out, projected_out, values_out, attended_out, mixed_out, normed_ffn_rows,
    ), refs = refs[:12], refs[12:]
    if carry:
        arrived, refs = refs[0], refs[1:]
    targets, refs = refs[: len(spans)], refs[len(spans) :]
    (
        hidden, model_gains, gains, tables, masks, normed, moved, projected, values, attended, mixed,
        held, keep, send_core, recv_core, send_half, recv_half, local_sems, send_sems, recv_sems,
    ) = refs
    exchange, local = Exchange(send_sems, recv_sems), Local(local_sems)
    first = [
        local.load(hidden_in, hidden),
        local.load(model_gains_in, model_gains),
        local.load(gains_in, gains),
    ]
    loads = load_pack(pack, held, local)
    exchange.greet(carry, (3 if spread else 2 if spans else 0))
    background = Background(exchange, local, spans, sources, targets)
    extra = [local.load(tables_in, tables), local.load(masks_in, masks)]
    chunks, own, cols = hidden.shape
    length = 2 * own
    q_width = attended.shape[1]
    kv_width = q_width // 2
    kv_heads = kv_width // width
    group = q_width // kv_width
    for load in first:
        load.wait()
    rows = hidden[...].astype(f32)
    inverse = lax.rsqrt(row_mean(rows * rows) + norm_eps)
    for c in range(chunks):
        normed[c, :own] = (rows[c] * inverse[0] * model_gains[0, c][None, :]).astype(bf16)

    def project(c):
        loads[c].wait()
        accumulate(projected, normed[c], held, c * cols, 0, 2 * q_width, c == 0)

    copies = gather_then(exchange, normed, project)
    moving = Spread(exchange, local, normed, moved) if spread else None
    hops = []
    if carry:
        hops = [exchange.copy(carried, arrived, exchange.section, 4, 0)]
        hops[0].start()
    local.save(projected, projected_out)
    for load in extra:
        load.wait()
    cos, sin = tables[0], tables[1]
    gain_q, gain_k = gains[0:1, :], gains[1:2, :]
    scale = width ** (-0.5)
    values[...] = projected[:, q_width + kv_width :].astype(bf16)
    local.save(values, values_out)
    for seq in range(2):
        at = slice(seq * length, (seq + 1) * length)
        allowed = masks[seq] > 0.5
        for kv in range(kv_heads):
            raw_k = projected[at, q_width + kv * width : q_width + (kv + 1) * width]
            value = values[at, kv * width : (kv + 1) * width]
            _, key_rot = rotated(raw_k, gain_k, cos, sin)
            for one in range(group):
                head = slice((kv * group + one) * width, (kv * group + one + 1) * width)
                _, query_rot = rotated(projected[at, head], gain_q, cos, sin)
                weights = softmax_rows(query_rot, key_rot, allowed, scale)
                attended[at, head] = dot_nn(weights.astype(bf16), value).astype(bf16)
    local.save(attended, attended_out)
    background.pass_on(False)

    def make(c):
        return dot_nt(attended[...], held[c * cols : (c + 1) * cols, 2 * q_width :])

    def idle(c):
        if not (spread or hold):
            turn_chunk(normed, moved, c)
        elif spread and c > 0:
            moving.pass_on(c - 1)
        if c == chunks - 2:
            background.pass_on(True)

    def finish(c, summed):
        mixed[c] = hidden[c].astype(f32) + summed

    copies += scatter_from(
        exchange, make, idle, finish, keep, send_core, recv_core, send_half, recv_half
    )
    if spread:
        copies += moving.finish()
    local.save(normed if hold else moved, moved_out)
    local.save(mixed, mixed_out)
    rows = mixed[...]
    inverse = lax.rsqrt(row_mean(rows * rows) + norm_eps)
    for c in range(chunks):
        normed_ffn_rows[c] = (rows[c] * inverse[0] * model_gains[1, c][None, :]).astype(bf16)
    for copy in hops:
        copy.wait()
    copies += background.finish()
    for copy in copies:
        copy.wait_send()
    local.finish()


def ffn_forward_kernel(
    hop, spread, spans, *refs
):
    if spread:
        held_rows, refs = refs[0], refs[1:]
    sources, refs = refs[: 2 * len(spans)], refs[2 * len(spans) :]
    rows, mixed_in, pack, turned_out, gate_up_out, activated_out, result, *rest = refs
    if hop:
        arrived, rest = rest[0], rest[1:]
    if spread:
        moved, rest = rest[0], rest[1:]
    targets, rest = rest[: len(spans)], rest[len(spans) :]
    (
        normed, turned, mixed, activated, total,
        held, keep, send_core, recv_core, send_half, recv_half, local_sems, send_sems, recv_sems,
    ) = rest
    exchange, local = Exchange(send_sems, recv_sems), Local(local_sems)
    own = rows.shape[1]
    first = local.load(rows, normed.at[:, pl.ds(0, own)])
    loads = load_pack(pack, held, local)
    exchange.greet(hop, 3 if spread else 2 if spans else 0)
    moving = Spread(exchange, local, held_rows, moved) if spread else None
    background = Background(exchange, local, spans, sources, targets)
    mixed_load = local.load(mixed_in, mixed)
    chunks, own, cols = rows.shape
    units = activated.shape[1]
    first.wait()

    def project(c):
        loads[c].wait()
        accumulate(total, normed[c], held, c * cols, 0, 2 * units, c == 0)

    copies = gather_then(exchange, normed, project)
    local.save(total, gate_up_out)
    blk = 256

    def activate(index, _):
        at = pl.multiple_of(index * blk, blk)
        gate = total[:, pl.ds(at, blk)]
        upward = total[:, pl.ds(units + at, blk)]
        activated[:, pl.ds(at, blk)] = (gate * jax.nn.sigmoid(gate) * upward).astype(bf16)
        return 0

    lax.fori_loop(0, units // blk, activate, 0)
    local.save(activated, activated_out)
    background.pass_on(False)
    mixed_load.wait()
    hops = []

    def make(c):
        return dot_nt(activated[...], held[c * cols : (c + 1) * cols, 2 * units :])

    def idle(c):
        turn_chunk(normed, turned, c)
        if spread and c > 0:
            moving.pass_on(c - 1)
        if c == chunks - 2:
            background.pass_on(True)

    def finish(c, summed):
        result[c] = (mixed[c] + summed).astype(bf16)
        if hop:
            hops.append(exchange.copy(result.at[c], arrived.at[c], exchange.section, 4, c))
            hops[-1].start()

    copies += scatter_from(
        exchange, make, idle, finish, keep, send_core, recv_core, send_half, recv_half
    )
    local.save(turned, turned_out)
    for copy in hops:
        copy.wait()
    copies += background.finish()
    if spread:
        copies += moving.finish()
    for copy in copies:
        copy.wait_send()
    local.finish()


def ffn_backward_kernel(spread, spans, carry, handed, *refs):
    sources, refs = refs[: 2 * len(spans)], refs[2 * len(spans) :]
    if carry:
        carried, refs = refs[0], refs[1:]
    (
        rows, mixed_a, mixed_b, gate_up_a, gate_up_b, pack, model_gains_in,
        moved_out, grads_out, grad_mixed, grad_proj_rows, gain_grad,
    ), refs = refs[:12], refs[12:]
    if carry:
        arrived, refs = refs[0], refs[1:]
    targets, refs = refs[: len(spans)], refs[len(spans) :]
    (
        model_gains, grad_down, moved, mixed, grads, pre, total,
        held, keep, send_core, recv_core, send_half, recv_half, local_sems, send_sems, recv_sems,
    ) = refs
    exchange, local = Exchange(send_sems, recv_sems), Local(local_sems)
    own = rows.shape[1]
    first = None if handed else local.load(rows, grad_down.at[:, pl.ds(0, own)])
    gains_load = local.load(model_gains_in, model_gains)
    at_first = lax.axis_index("section") == 0
    loads = load_pack(pack, held, local)
    exchange.greet(carry or handed, 3 if spread else 0)
    arrivals = []
    if handed:
        arrivals = [
            exchange.copy(rows.at[c], grad_down.at[c, pl.ds(0, own)], exchange.section, 4, c)
            for c in range(rows.shape[0])
        ]
        for copy in arrivals:
            copy.start()
    background = Background(exchange, local, spans, sources, targets)
    pre_load = local.load_either(at_first, gate_up_a, gate_up_b, pre)
    mixed_load = local.load_either(at_first, mixed_a, mixed_b, mixed)
    chunks, own, cols = rows.shape
    units = grads.shape[1] // 2
    if first is not None:
        first.wait()

    def project(c):
        loads[c].wait()
        accumulate(total, grad_down[c], held, c * cols, 2 * units, units, c == 0)

    copies = gather_then(exchange, grad_down, project, arrivals) + arrivals
    if handed:
        background.late = [False] * len(background.late)
    hops = []
    if carry:
        hops = [exchange.copy(carried, arrived, exchange.section, 4, 0)]
        hops[0].start()
    moving = Spread(exchange, local, grad_down, moved) if spread else None
    pre_load.wait()
    blk = 256

    def activate(index, _):
        at = pl.multiple_of(index * blk, blk)
        gate = pre[:, pl.ds(at, blk)]
        upward = pre[:, pl.ds(units + at, blk)]
        grad_act = total[:, pl.ds(at, blk)]
        sig = jax.nn.sigmoid(gate)
        grads[:, pl.ds(at, blk)] = (grad_act * upward * sig * (1.0 + gate * (1.0 - sig))).astype(bf16)
        grads[:, pl.ds(units + at, blk)] = (grad_act * gate * sig).astype(bf16)
        return 0

    lax.fori_loop(0, units // blk, activate, 0)
    local.save(grads, grads_out)
    background.pass_on(False)

    def make(c):
        return dot_nt(grads[...], held[c * cols : (c + 1) * cols, : 2 * units])

    def idle(c):
        if not spread:
            turn_chunk(grad_down, moved, c)
        elif c > 0:
            moving.pass_on(c - 1)
        if c == chunks - 2:
            background.pass_on(True)

    def finish(c, summed):
        grad_mixed[c] = summed

    copies += scatter_from(
        exchange, make, idle, finish, keep, send_core, recv_core, send_half, recv_half
    )
    if spread:
        copies += moving.finish()
    local.save(moved, moved_out)
    mixed_load.wait()
    gains_load.wait()
    base = grad_down[:, :own]
    norm_step(mixed[...], grad_mixed[...], model_gains, 1, base, grad_mixed, gain_grad)
    for c in range(chunks):
        grad_proj_rows[c] = grad_mixed[c].astype(bf16)
    for copy in hops:
        copy.wait()
    copies += background.finish()
    for copy in copies:
        copy.wait_send()
    local.finish()


def norm_step(values, grad_out, model_gains, which, base, out, gain_grad):
    inverse = lax.rsqrt(row_mean(values * values) + norm_eps)
    gain = jnp.concatenate([model_gains[which, c][None, None, :] for c in range(out.shape[0])], axis=0)
    scaled = grad_out * gain
    centre = row_mean(scaled * values) * inverse * inverse
    out[...] = (base[...].astype(f32) + inverse * (scaled - values * centre)).astype(out.dtype)
    for c in range(out.shape[0]):
        gain_grad[c, :] = jnp.sum(grad_out[c] * values[c] * inverse[0], axis=0)


def attn_backward_kernel(
    width, spread, spans, hop, *refs
):
    sources, refs = refs[: 2 * len(spans)], refs[2 * len(spans) :]
    (
        rows, grad_mixed_in, hidden_a, hidden_b, projected_a, projected_b, values_a, values_b,
        pack, model_gains_in, gains_in, tables_in, masks_in,
        moved_out, grads_out, grad_hidden, gain_grad, head_gain_grads, *rest
    ) = refs
    if hop:
        arrived, rest = rest[0], rest[1:]
    targets, rest = rest[: len(spans)], rest[len(spans) :]
    (
        grad_mixed, model_gains, gains, tables, masks, grad_proj, moved, grads, hidden, projected, values, total, summed_rows,
        held, keep, send_core, recv_core, send_half, recv_half, local_sems, send_sems, recv_sems,
    ) = rest
    exchange, local = Exchange(send_sems, recv_sems), Local(local_sems)
    own = rows.shape[1]
    first = local.load(rows, grad_proj.at[:, pl.ds(0, own)])
    gain_loads = [
        local.load(model_gains_in, model_gains),
        local.load(gains_in, gains),
        local.load(grad_mixed_in, grad_mixed),
    ]
    at_first = lax.axis_index("section") == 0
    loads = load_pack(pack, held, local)
    exchange.greet(hop, 3 if spread else 0)
    background = Background(exchange, local, spans, sources, targets)
    extra = [local.load(tables_in, tables), local.load(masks_in, masks)]
    projected_load = local.load_either(at_first, projected_a, projected_b, projected)
    values_load = local.load_either(at_first, values_a, values_b, values)
    hidden_load = local.load_either(at_first, hidden_a, hidden_b, hidden)
    chunks, own, cols = rows.shape
    length = 2 * own
    q_width = grads.shape[1] // 2
    kv_width = q_width // 2
    kv_heads = kv_width // width
    group = q_width // kv_width
    first.wait()

    def project(c):
        loads[c].wait()
        accumulate(total, grad_proj[c], held, c * cols, 2 * q_width, q_width, c == 0)

    copies = gather_then(exchange, grad_proj, project)
    moving = Spread(exchange, local, grad_proj, moved) if spread else None
    projected_load.wait()
    values_load.wait()
    for load in extra + gain_loads:
        load.wait()
    cos, sin = tables[0], tables[1]
    gain_q, gain_k = gains[0:1, :], gains[1:2, :]
    scale = width ** (-0.5)
    gain_q_sum = jnp.zeros((1, width), f32)
    gain_k_sum = jnp.zeros((1, width), f32)
    for seq in range(2):
        at = slice(seq * length, (seq + 1) * length)
        allowed = masks[seq] > 0.5
        for kv in range(kv_heads):
            raw_k = projected[at, q_width + kv * width : q_width + (kv + 1) * width]
            value = values[at, kv * width : (kv + 1) * width]
            inverse_k, key_rot = rotated(raw_k, gain_k, cos, sin)
            grad_key = jnp.zeros((length, width), f32)
            grad_value = jnp.zeros((length, width), f32)
            for one in range(group):
                head = slice((kv * group + one) * width, (kv * group + one + 1) * width)
                raw_q = projected[at, head]
                grad_head = total[at, head].astype(bf16)
                inverse_q, query_rot = rotated(raw_q, gain_q, cos, sin)
                weights = softmax_rows(query_rot, key_rot, allowed, scale)
                grad_weights = dot_nt(grad_head, value)
                delta = jnp.sum(weights * grad_weights, axis=-1, keepdims=True)
                grad_scores = (weights * (grad_weights - delta)).astype(bf16)
                grad_value += dot_tn(weights.astype(bf16), grad_head)
                grad_key += dot_tn(grad_scores, query_rot)
                grad_query = dot_nn(grad_scores, key_rot) * scale
                grad_query = grad_query * cos - pltpu.roll(grad_query, 64, 1) * sin
                gain_q_sum += jnp.sum(grad_query * raw_q * inverse_q, axis=0, keepdims=True)
                grads[at, head] = norm_back(grad_query, raw_q, inverse_q, gain_q).astype(bf16)
            grad_key = grad_key * scale
            grad_key = grad_key * cos - pltpu.roll(grad_key, 64, 1) * sin
            gain_k_sum += jnp.sum(grad_key * raw_k * inverse_k, axis=0, keepdims=True)
            first = q_width + kv * width
            grads[at, first : first + width] = norm_back(grad_key, raw_k, inverse_k, gain_k).astype(bf16)
            first += kv_width
            grads[at, first : first + width] = grad_value.astype(bf16)
    local.save(grads, grads_out)
    background.pass_on(False)
    head_gain_grads[...] = jnp.concatenate(
        [gain_q_sum, gain_k_sum, jnp.zeros((6, width), f32)], axis=0
    )

    def make(c):
        return dot_nt(grads[...], held[c * cols : (c + 1) * cols, : 2 * q_width])

    def idle(c):
        if not spread:
            turn_chunk(grad_proj, moved, c)
        elif c > 0:
            moving.pass_on(c - 1)
        if c == chunks - 2:
            background.pass_on(True)

    def finish(c, summed):
        summed_rows[c] = summed

    copies += scatter_from(
        exchange, make, idle, finish, keep, send_core, recv_core, send_half, recv_half
    )
    if spread:
        copies += moving.finish()
    local.save(moved, moved_out)
    hidden_load.wait()
    norm_step(
        hidden[...].astype(f32), summed_rows[...], model_gains, 0, grad_mixed, grad_hidden, gain_grad
    )
    if hop:
        hops = [
            exchange.copy(grad_hidden.at[c], arrived.at[c], exchange.section, 4, c)
            for c in range(chunks)
        ]
        for copy in hops:
            copy.start()
        for copy in hops:
            copy.wait()
    copies += background.finish()
    for copy in copies:
        copy.wait_send()
    local.finish()


def weight_grad_kernel(blk, sides, *refs):
    lefts, rights, refs = refs[: 3 * sides], refs[3 * sides : 6 * sides], refs[6 * sides :]
    out, left, right = refs[0], refs[1 : 1 + sides], refs[1 + sides : 1 + 2 * sides]
    held, local_sems = refs[1 + 2 * sides :]
    local = Local(local_sems)
    at_first = lax.axis_index("section") == 0
    tokens = rights[0].shape[0]
    loads = []
    for side in range(sides):
        left_steps = pairs_of(lefts[3 * side : 3 * side + 3], side == 1)
        right_steps = pairs_of(rights[3 * side : 3 * side + 3], side == 0)
        for micro in range(2):
            at = pl.ds(micro * tokens, tokens)
            loads.append(
                [
                    local.load_either(
                        at_first, left_steps[0][micro], left_steps[1][micro], left[side].at[:, at]
                    ),
                    local.load_either(
                        at_first, right_steps[0][micro], right_steps[1][micro], right[side].at[at]
                    ),
                ]
            )
    saves, number = [None, None], 0
    for side in range(sides):
        for micro in range(2):
            for load in loads[2 * side + micro]:
                load.wait()
        for block in range(right[side].shape[1] // blk):
            slot = number % 2
            if saves[slot] is not None:
                saves[slot].wait()
            at = pl.ds(block * blk, blk)
            held[slot] = dot_nn(left[side][...], right[side][:, at]).astype(bf16)
            saves[slot] = local.load(held.at[slot], out.at[:, pl.ds(number * blk, blk)])
            number += 1
    for save in saves:
        save.wait()


def pairs_of(steps, backward):
    early, late = (steps[0], steps[1]), (steps[1], steps[2])
    return (late, early) if backward else (early, late)


VMEM_SPEC = pl.BlockSpec(memory_space=pltpu.VMEM)
HBM_SPEC = pl.BlockSpec(memory_space=pltpu.HBM)


def shape(dims, kind):
    return jax.ShapeDtypeStruct(dims, kind)


def exchange_scratch(chunks, own, cols):
    return [
        pltpu.VMEM((chunks, 2 * own, cols), f32),
        pltpu.VMEM((chunks, 2 * own, cols), bf16),
        pltpu.VMEM((chunks, 2 * own, cols), bf16),
        pltpu.VMEM((chunks, own, cols), bf16),
        pltpu.VMEM((chunks, own, cols), bf16),
        pltpu.SemaphoreType.DMA((20,)),
        pltpu.SemaphoreType.DMA((9, chunks)),
        pltpu.SemaphoreType.DMA((9, chunks)),
    ]


def params(number=None):
    if number is None:
        return pltpu.CompilerParams(vmem_limit_bytes=62 * MIB)
    return pltpu.CompilerParams(
        vmem_limit_bytes=62 * MIB, collective_id=number, has_side_effects=True
    )


class Numbers(dict):
    def of(self, *key):
        return self.setdefault(key, len(self))


def spans_of(background):
    return tuple((first, count) for _, first, count in background)


def gather_shapes(background):
    return [shape((4, count, blocks[0].shape[1]), bf16) for blocks, _, count in background]


def cost(flops, size):
    return pl.CostEstimate(flops=int(flops), bytes_accessed=int(size), transcendentals=0)


def attn_forward(hidden, pack, model_gains, gains, tables, masks, spread, hold, carried, background, numbers):
    chunks, own, cols = hidden.shape
    tokens, q_width, width = 4 * own, pack.shape[1] // 3, gains.shape[1]
    moved = (chunks, tokens, cols) if spread or hold else (chunks * cols, tokens)
    carry, spans = carried is not None, spans_of(background)
    rows = shape((chunks, own, cols), bf16)
    return pl.pallas_call(
        functools.partial(attn_forward_kernel, width, spread, hold, spans, carry),
        in_specs=[HBM_SPEC] * (2 * len(spans) + carry) + [HBM_SPEC] * 6,
        out_specs=[HBM_SPEC] * 5 + [VMEM_SPEC] + [HBM_SPEC] * (carry + len(spans)),
        out_shape=[
            shape(moved, bf16),
            shape((tokens, 2 * q_width), f32),
            shape((tokens, q_width // 2), bf16),
            shape((tokens, q_width), bf16),
            shape((chunks, own, cols), f32),
            rows,
        ]
        + [rows] * carry
        + gather_shapes(background),
        scratch_shapes=[
            pltpu.VMEM(hidden.shape, bf16),
            pltpu.VMEM(model_gains.shape, f32),
            pltpu.VMEM(gains.shape, f32),
            pltpu.VMEM(tables.shape, f32),
            pltpu.VMEM(masks.shape, f32),
            pltpu.VMEM((chunks, tokens, cols), bf16),
            pltpu.VMEM(moved, bf16),
            pltpu.VMEM((tokens, 2 * q_width), f32),
            pltpu.VMEM((tokens, q_width // 2), bf16),
            pltpu.VMEM((tokens, q_width), bf16),
            pltpu.VMEM((chunks, own, cols), f32),
            pltpu.VMEM(pack.shape, bf16),
        ]
        + exchange_scratch(chunks, own, cols),
        compiler_params=params(numbers.of("attn_forward", hold, carry, spans)),
        cost_estimate=cost(2 * tokens * pack.size, pack.size * 2),
        name="attn_forward",
    )(*sum([list(blocks) for blocks, *_ in background], []), *([carried] if carry else []), hidden, pack, model_gains, gains, tables, masks)


def ffn_forward(rows, mixed, pack, hop, held_rows, background, numbers):
    chunks, own, cols = rows.shape
    tokens, units = 4 * own, pack.shape[1] // 3
    depth = chunks * cols
    spans, spread = spans_of(background), held_rows is not None
    return pl.pallas_call(
        functools.partial(ffn_forward_kernel, hop, spread, spans),
        in_specs=[HBM_SPEC] * (spread + 2 * len(spans)) + [HBM_SPEC] * 3,
        out_specs=[HBM_SPEC] * 3 + [VMEM_SPEC] * (2 if hop else 1) + [HBM_SPEC] * (spread + len(spans)),
        out_shape=[
            shape((depth, tokens), bf16),
            shape((tokens, 2 * units), f32),
            shape((tokens, units), bf16),
        ]
        + [shape((chunks, own, cols), bf16)] * (2 if hop else 1)
        + [shape((chunks, tokens, cols), bf16)] * spread
        + gather_shapes(background),
        scratch_shapes=[
            pltpu.VMEM((chunks, tokens, cols), bf16),
            pltpu.VMEM((depth, tokens), bf16),
            pltpu.VMEM((chunks, own, cols), f32),
            pltpu.VMEM((tokens, units), bf16),
            pltpu.VMEM((tokens, 2 * units), f32),
            pltpu.VMEM(pack.shape, bf16),
        ]
        + exchange_scratch(chunks, own, cols),
        compiler_params=params(numbers.of("ffn_forward", hop, spread, spans)),
        cost_estimate=cost(2 * tokens * pack.size, pack.size * 2),
        name="ffn_forward",
    )(*([held_rows] if spread else []), *sum([list(blocks) for blocks, *_ in background], []), rows, mixed, pack)


def ffn_backward(rows, mixed, gate_up, pack, model_gains, spread, carried, handed, background, numbers):
    chunks, own, cols = rows.shape
    tokens, units = 4 * own, pack.shape[1] // 3
    moved = (chunks, tokens, cols) if spread else (chunks * cols, tokens)
    carry, spans = carried is not None, spans_of(background)
    return pl.pallas_call(
        functools.partial(ffn_backward_kernel, spread, spans, carry, handed),
        in_specs=[HBM_SPEC] * (2 * len(spans) + carry) + [HBM_SPEC] * 7,
        out_specs=[HBM_SPEC] * 2 + [VMEM_SPEC] * 3 + [HBM_SPEC] * (carry + len(spans)),
        out_shape=[
            shape(moved, bf16),
            shape((tokens, 2 * units), bf16),
            shape((chunks, own, cols), f32),
            shape((chunks, own, cols), bf16),
            shape((chunks, cols), f32),
        ]
        + [shape((chunks, own, cols), bf16)] * carry
        + gather_shapes(background),
        scratch_shapes=[
            pltpu.VMEM(model_gains.shape, f32),
            pltpu.VMEM((chunks, tokens, cols), bf16),
            pltpu.VMEM(moved, bf16),
            pltpu.VMEM((chunks, own, cols), f32),
            pltpu.VMEM((tokens, 2 * units), bf16),
            pltpu.VMEM((tokens, 2 * units), f32),
            pltpu.VMEM((tokens, units), f32),
            pltpu.VMEM(pack.shape, bf16),
        ]
        + exchange_scratch(chunks, own, cols),
        compiler_params=params(numbers.of("ffn_backward", carry, handed, spans)),
        cost_estimate=cost(2 * tokens * pack.size, pack.size * 2),
        name="ffn_backward",
    )(*sum([list(blocks) for blocks, *_ in background], []), *([carried] if carry else []), rows, *mixed, *gate_up, pack, model_gains)


def attn_backward(
    rows, grad_mixed, hidden, projected, values, pack, model_gains, gains, tables, masks, spread, hop,
    background, numbers
):
    chunks, own, cols = rows.shape
    tokens, q_width, width = 4 * own, pack.shape[1] // 3, gains.shape[1]
    moved = (chunks, tokens, cols) if spread else (chunks * cols, tokens)
    spans = spans_of(background)
    return pl.pallas_call(
        functools.partial(attn_backward_kernel, width, spread, spans, hop),
        in_specs=[HBM_SPEC] * (2 * len(spans)) + [HBM_SPEC] * 13,
        out_specs=[HBM_SPEC] * 2 + [VMEM_SPEC] * (4 if hop else 3) + [HBM_SPEC] * len(spans),
        out_shape=[
            shape(moved, bf16),
            shape((tokens, 2 * q_width), bf16),
            shape((chunks, own, cols), bf16),
            shape((chunks, cols), f32),
            shape((8, width), f32),
        ]
        + [shape((chunks, own, cols), bf16)] * (1 if hop else 0)
        + gather_shapes(background),
        scratch_shapes=[
            pltpu.VMEM(grad_mixed.shape, f32),
            pltpu.VMEM(model_gains.shape, f32),
            pltpu.VMEM(gains.shape, f32),
            pltpu.VMEM(tables.shape, f32),
            pltpu.VMEM(masks.shape, f32),
            pltpu.VMEM((chunks, tokens, cols), bf16),
            pltpu.VMEM(moved, bf16),
            pltpu.VMEM((tokens, 2 * q_width), bf16),
            pltpu.VMEM((chunks, own, cols), bf16),
            pltpu.VMEM((tokens, 2 * q_width), f32),
            pltpu.VMEM((tokens, q_width // 2), bf16),
            pltpu.VMEM((tokens, q_width), f32),
            pltpu.VMEM((chunks, own, cols), f32),
            pltpu.VMEM(pack.shape, bf16),
        ]
        + exchange_scratch(chunks, own, cols),
        compiler_params=params(numbers.of("attn_backward", hop, spans)),
        cost_estimate=cost(2 * tokens * pack.size, pack.size * 2),
        name="attn_backward",
    )(
        *sum([list(blocks) for blocks, *_ in background], []), rows, grad_mixed, *hidden, *projected, *values, pack, model_gains, gains, tables, masks
    )


def weight_grad(lefts, rights):
    depth, tokens = lefts[0][0].shape
    blk = 512
    widths = [right[0].shape[1] for right in rights]
    return pl.pallas_call(
        functools.partial(weight_grad_kernel, blk, len(lefts)),
        in_specs=[HBM_SPEC] * (6 * len(lefts)),
        out_specs=HBM_SPEC,
        out_shape=shape((depth, sum(widths)), bf16),
        scratch_shapes=[pltpu.VMEM((depth, 2 * tokens), bf16) for _ in lefts]
        + [pltpu.VMEM((2 * tokens, width), bf16) for width in widths]
        + [
            pltpu.VMEM((2, depth, blk), bf16),
            pltpu.SemaphoreType.DMA((4 * len(lefts) + sum(widths) // blk,)),
        ],
        compiler_params=params(),
        cost_estimate=cost(4 * depth * tokens * sum(widths), 2 * depth * sum(widths)),
        name="weight_grad",
    )(*sum(lefts, []), *sum(rights, []))


def rope_tables(position, head_width):
    exponent = jnp.arange(0, head_width, 2).astype(f32) / head_width
    inverse = rope_base ** (-exponent)
    angles = position.astype(f32)[:, None] * inverse[None, :]
    cosine, sine = jnp.cos(angles), jnp.sin(angles)
    return (
        jnp.concatenate([cosine, cosine], axis=-1),
        jnp.concatenate([-sine, sine], axis=-1),
    )


def per_device(
    block_input,
    segment_ids,
    out_cotangent,
    attn_norm,
    q_weight,
    k_weight,
    v_weight,
    o_weight,
    q_norm,
    k_norm,
    ffn_norm,
    gate_weight,
    up_weight,
    down_weight,
):
    section = lax.axis_index("section")
    place = lax.axis_index("dp")
    core = place % 2
    half = lax.axis_index("tensor")
    n_dp = lax.axis_size("dp")
    n_chip = n_dp // 2
    micro_count, own_rows, depth = block_input.shape
    length = 2 * own_rows
    head_width = q_norm.shape[1]
    first_core = core == 0
    swap_core = [(i, i ^ 1) for i in range(n_dp)]
    swap_half = [(0, 1), (1, 0)]
    chip_groups = [[2 * chip + one for chip in range(n_chip)] for one in (0, 1)]

    def to_core(values):
        return lax.ppermute(values, "dp", swap_core)

    def to_half(values):
        return lax.ppermute(values, "tensor", swap_half)

    def split_columns(weight):
        side = weight.shape[1] // 2
        left, right = weight[:, :side], weight[:, side:]
        return jnp.where(first_core, left, right), jnp.where(first_core, right, left)

    def split_rows(weight):
        side = weight.shape[0] // 2
        left, right = weight[:side].T, weight[side:].T
        return jnp.where(first_core, left, right), jnp.where(first_core, right, left)

    def chip_block(pairs):
        mine = jnp.concatenate([pair[0] for pair in pairs], axis=1)
        theirs = to_core(jnp.concatenate([pair[1] for pair in pairs], axis=1))
        return jnp.concatenate(
            [jnp.where(first_core, mine, theirs), jnp.where(first_core, theirs, mine)], axis=0
        )

    def gathered(block):
        return lax.all_gather(block, "dp", axis=0, tiled=True, axis_index_groups=chip_groups)

    square = n_chip == row_chunks
    numbers = Numbers()
    attn_block = chip_block(
        [
            split_columns(q_weight[0]),
            split_columns(k_weight[0]),
            split_columns(v_weight[0]),
            split_rows(o_weight[0]),
        ]
    )
    ffn_block = chip_block(
        [split_columns(gate_weight[0]), split_columns(up_weight[0]), split_rows(down_weight[0])]
    )
    if square:
        attn_block, ffn_block = lax.optimization_barrier((attn_block, ffn_block))
        attn_pack = chip_gather([attn_block], numbers.of("chip_gather", 0)).reshape(depth, -1)
    else:
        attn_pack = gathered(attn_block)
    ffn_pack = gathered(ffn_block)

    cols = depth // row_chunks
    model_gains = jnp.concatenate([attn_norm, ffn_norm], axis=0).reshape(2, row_chunks, cols)
    head_gains = jnp.concatenate([q_norm, k_norm, jnp.zeros((6, head_width), f32)], axis=0)

    def chunked(rows):
        return rows.reshape(rows.shape[0], row_chunks, cols).transpose(1, 0, 2)

    def joined(rows):
        return rows.transpose(1, 0, 2).reshape(rows.shape[1], depth)

    inputs = [chunked(block_input[micro]) for micro in range(2)]
    cotangents = [chunked(out_cotangent[micro]) for micro in range(2)]

    def arranged(values):
        sides = values[..., :own_rows], values[..., own_rows:]
        return jnp.concatenate(
            [jnp.where(half == 0, *sides), jnp.where(half == 0, *sides[::-1])], axis=-1
        )

    position = arranged(jnp.arange(length, dtype=jnp.int32))
    tables = jnp.stack(rope_tables(position, head_width))
    ids = arranged(jnp.stack([segment_ids, to_core(segment_ids)], axis=1))
    causal = position[:, None] >= position[None, :]
    masks = (causal & (ids[..., :, None] == ids[..., None, :])).astype(f32)

    at_first = section == 0

    def pick(first, second):
        return jax.tree.map(lambda a, b: jnp.where(at_first, a, b), first, second)

    zero_rows = jnp.zeros_like(inputs[0])
    forward_masks = [masks[0], pick(masks[1], masks[0]), masks[1]]
    backward_masks = [masks[0], pick(masks[0], masks[1]), masks[1]]
    results, backs, saves = [], [], []
    grads, ffn_saves, attn_saves, gains = [], [], [], []

    def forward_step(step, arrived, hop, carried=None, attn_work=(), ffn_work=()):
        hidden = inputs[step] if step < 2 else zero_rows
        if step > 0:
            hidden = pick(hidden, arrived)
        turned_in, projected, values, attended, mixed, rows, *more = attn_forward(
            hidden, attn_pack, model_gains, head_gains, tables, forward_masks[step],
            square and step > 0, square and step == 0, carried, attn_work, numbers,
        )
        turned_mid, gate_up, activated, result, *rest = ffn_forward(
            rows, mixed, ffn_pack, hop, turned_in if square and step == 0 else None, ffn_work, numbers
        )
        if square and step == 0:
            turned_in = rest.pop(1)
        results.append(result)
        backs.append((hidden, projected, values, mixed, gate_up))
        saves.append((turned_in, attended, turned_mid, activated))
        return more + rest

    def back_ffn(step, arrived, carried=None, work=()):
        rows = pick(arrived, cotangents[step]) if step < 2 else arrived
        *_, mixed, gate_up = zip(backs[0], backs[2]) if step == 1 else zip(backs[1], backs[1])
        turned_rows, ffn_grads, grad_mixed, proj_rows, gain_grad, *more = ffn_backward(
            rows, mixed, gate_up, ffn_pack, model_gains, square, carried, step == 2, work, numbers
        )
        ffn_saves.append((turned_rows, ffn_grads))
        return (proj_rows, grad_mixed, gain_grad), more

    def back_attn(step, proj_rows, grad_mixed, ffn_gain_grad, hop, work=()):
        hidden, projected, values, *_ = (
            zip(backs[0], backs[2]) if step == 1 else zip(backs[1], backs[1])
        )
        turned_rows, attn_grads, grad_hidden, attn_gain_grad, head_gain_grads, *rest = attn_backward(
            proj_rows, grad_mixed, hidden, projected, values, attn_pack, model_gains, head_gains,
            tables, backward_masks[step], square, hop, work, numbers,
        )
        attn_saves.append((turned_rows, attn_grads))
        grads.append(grad_hidden)
        step_gains = (attn_gain_grad, ffn_gain_grad, head_gain_grads)
        gains.append(pick(step_gains, jax.tree.map(jnp.zeros_like, step_gains)) if step == 2 else step_gains)
        return rest

    def column(table, item):
        return [row[item] for row in table]

    def work(*items):
        return items if square else ()

    def of_micro(micro, item):
        return saves[micro][item], saves[micro + 1][item]

    tokens = 2 * length
    (arrived,) = forward_step(0, zero_rows, True)
    forward_step(1, arrived, False)
    active, attended = of_micro(0, 3), of_micro(0, 1)
    part = tokens // 4
    others, (arrived, *pieces) = back_ffn(0, zero_rows, results[1], work((active, 0, part)))
    active_pieces = [(0, pieces)]
    pieces = back_attn(0, *others, False, work((active, part, part)))
    active_pieces.append((part, pieces))
    grad_arrived, *pieces = forward_step(
        2, arrived, False, grads[0], work((active, 2 * part, part)),
        work((active, 3 * part, part), (attended, 0, tokens)),
    )
    active_pieces += [(2 * part, pieces[:1]), (3 * part, pieces[1:2])]
    attended_all = [pieces[2:]]
    active, attended = of_micro(1, 3), of_micro(1, 1)
    side = tokens // 2
    grad_arrived, results[2] = lax.optimization_barrier((grad_arrived, results[2]))
    first_side = side + part // 3
    others, pieces = back_ffn(1, grad_arrived, None, work((active, 0, first_side)))
    late_pieces = [(0, pieces)]
    pieces = back_attn(
        1, *others, False, work((active, first_side, tokens - first_side))
    )
    late_pieces.append((first_side, pieces[:1]))
    early_block = attn_saves[1][1], attn_saves[0][1]
    (proj_rows, *others), pieces = back_ffn(
        2, grads[1], None, work((attended, 0, tokens), (early_block, 0, tokens))
    )
    attended_all.append(pieces[:1])
    early_grads = pieces[1:]
    if square:
        ffn_partial = weight_grad([column(saves, 2)], [column(ffn_saves, 1)])
    else:
        ffn_partial = weight_grad(
            [column(saves, 2), column(ffn_saves, 0)], [column(ffn_saves, 1), column(saves, 3)]
        )
    proj_rows, ffn_partial = lax.optimization_barrier((proj_rows, ffn_partial))
    back_attn(2, proj_rows, *others, False)
    if not square:
        attn_partial = weight_grad(
            [column(saves, 0), column(attn_saves, 0)], [column(attn_saves, 1), column(saves, 1)]
        )
    gain_total = functools.reduce(lambda a, b: jax.tree.map(jnp.add, a, b), gains)

    section_outputs = jnp.stack(
        [joined(pick(results[micro], results[micro + 1])) for micro in range(2)]
    )[None]
    section_input_grads = jnp.stack(
        [joined(pick(grads[micro + 1], grads[micro])) for micro in range(2)]
    )[None]

    def scattered(partial):
        return lax.psum_scatter(
            partial, "dp", scatter_dimension=0, tiled=True, axis_index_groups=chip_groups
        )

    def owned(rows):
        side = rows.shape[0] // 2
        own = jnp.where(first_core, rows[:side], rows[side:])
        other = to_core(jnp.where(first_core, rows[side:], rows[:side]))
        return (
            jnp.where(first_core, own, other).astype(f32),
            jnp.where(first_core, other, own).astype(f32),
        )

    units = gate_weight.shape[2] // 2
    if square:
        late_grads = chip_gather([attn_saves[2][1], attn_saves[1][1]], numbers.of("chip_gather", 1))

        def flat(rows):
            return rows.reshape(-1, rows.shape[-1])

        def summed(rows, pieces):
            return sum(
                dot_tn(flat(rows[:, first : first + piece.shape[1]]), flat(piece))
                for first, (piece,) in pieces
            )

        def forward_rows(micro):
            return pick(saves[micro][0], saves[micro + 1][0])

        def backward_rows(table, micro):
            return pick(table[micro + 1][0], table[micro][0])

        down_rows = summed(backward_rows(ffn_saves, 0), active_pieces) + summed(
            backward_rows(ffn_saves, 1), late_pieces
        )
        o_rows = sum(
            summed(backward_rows(attn_saves, micro), [(0, attended_all[micro])])
            for micro in range(2)
        )
        early_pieces = [(0, early_grads)]
        qkv_rows = summed(forward_rows(0), early_pieces) + summed(
            forward_rows(1), [(0, [late_grads])]
        )
        attn_rows = jnp.concatenate([qkv_rows, o_rows], axis=1)
        ffn_rows = scattered(ffn_partial)
    else:
        attn_partial, ffn_rows = lax.optimization_barrier((attn_partial, scattered(ffn_partial)))
        ffn_sides = owned(ffn_rows)
        attn_sides = owned(scattered(attn_partial))
    q_width = q_weight.shape[2] // 2
    kv_width = k_weight.shape[2] // 2

    def across(sides, first, width):
        return jnp.concatenate([side[:, first : first + width] for side in sides], axis=1)[None]

    def down(sides, first):
        return jnp.concatenate([side[:, first:].T for side in sides], axis=0)[None]

    packed = jnp.concatenate(
        [
            gain_total[0].reshape(-1),
            gain_total[1].reshape(-1),
            gain_total[2][0],
            gain_total[2][1],
        ]
    ).reshape(-1, head_width)
    packed = packed + to_core(packed)
    packed = packed + to_half(packed)
    reach = 2
    while reach < n_dp:
        packed = packed + lax.ppermute(packed, "dp", [(i, i ^ reach) for i in range(n_dp)])
        reach *= 2
    packed = packed.reshape(-1)
    gain_grads = (
        packed[None, :depth],
        packed[None, 2 * depth : 2 * depth + head_width],
        packed[None, 2 * depth + head_width :],
        packed[None, depth : 2 * depth],
    )
    if square:
        attn_wide = ((q_width, False), (kv_width, False), (kv_width, False), (q_width, True))
        attn_grads = place_parts(attn_rows, core_swap(attn_rows, numbers.of("core_swap", 0)), attn_wide)
        down_swapped = core_swap(down_rows, numbers.of("core_swap", 1))
        down_grads = place_parts(down_rows, down_swapped, ((units, True),))
        others = (section_outputs, section_input_grads, gain_grads, attn_grads, down_grads)
        others, ffn_rows = lax.optimization_barrier((others, ffn_rows))
        section_outputs, section_input_grads, gain_grads, attn_grads, down_grads = others
        ffn_swapped = core_swap(ffn_rows, numbers.of("core_swap", 2))
        wide_grads = place_parts(ffn_rows, ffn_swapped, ((units, False), (units, False)))
        weight_grads = [grad[None] for grad in (*attn_grads, *wide_grads, *down_grads)]
    else:
        weight_grads = [
            across(attn_sides, 0, q_width),
            across(attn_sides, q_width, kv_width),
            across(attn_sides, q_width + kv_width, kv_width),
            down(attn_sides, 2 * q_width),
            across(ffn_sides, 0, units),
            across(ffn_sides, units, units),
            down(ffn_sides, 2 * units),
        ]
    return (
        section_outputs,
        section_input_grads,
        gain_grads[0],
        *weight_grads[:4],
        *gain_grads[1:],
        *weight_grads[4:],
    )


def solution(mesh):
    rows = P(None, ("dp", "tensor"), None)
    out_rows = P("section", None, ("dp", "tensor"), None)
    gain = P("section", None)
    wide = P("section", "dp", "tensor")
    tall = P("section", "tensor", "dp")
    return jax.shard_map(
        per_device,
        mesh=mesh,
        in_specs=(
            rows, P(None, "dp"), rows, gain, wide, wide, wide, tall, gain, gain, gain, wide, wide, tall,
        ),
        out_specs=(
            out_rows, out_rows, gain, wide, wide, wide, tall, gain, gain, gain, wide, wide, tall,
        ),
        check_vma=False,
    )
```
